32 devices in a mesh: dp: 8 (over z, y), tensor: 4 (over x, core).
Axes of the slice: x: 2, y: 2, z: 4, core: 2. Of those that a mesh axis runs over, the one named last changes fastest.
Arguments:
- tokens: bfloat16 [10240, 960], P('dp'), may hold values from -6 to 6
- cotangent: bfloat16 [10240, 960], P('dp'), may hold values from -6 to 6
- lengths: int32 [8, 3], P('dp'), may hold values from 1 to 1024, 1280 in all within a row
- valid: int32 [10240], P('dp'), may hold values 0 or 1
- query_group: int32 [15], replicated, may hold values from 0 to 14, each once
- w_query: float32 [960, 960], P('dp'), may hold values from -0.1875 to 0.1875
- w_keyval: float32 [960, 640], P('dp'), may hold values from -0.1875 to 0.1875
- w_output: float32 [960, 960], P(None, 'dp'), may hold values from -3.5 to 3.5
- w_ffn_in: float32 [960, 2, 2560], P('dp', None, 'tensor'), may hold values from -0.1875 to 0.1875
- w_ffn_out: float32 [2560, 960], P('tensor', 'dp'), may hold values from -0.125 to 0.125
- norm_gains: float32 [2, 960], P(None, 'dp'), may hold values from 0.5 to 1.5
- first_query: float32 [960, 960], P('dp'), may hold values from -1792 to 1792
- first_keyval: float32 [960, 640], P('dp'), may hold values from -3072 to 3072
- first_output: float32 [960, 960], P(None, 'dp'), may hold values from -96 to 96
- first_ffn_in: float32 [960, 2, 2560], P('dp', None, 'tensor'), may hold values from -224 to 224
- first_ffn_out: float32 [2560, 960], P('tensor', 'dp'), may hold values from -384 to 384
- first_gains: float32 [2, 960], P(None, 'dp'), may hold values from -2974.4512 to 2974.4512
- second_query: float32 [960, 960], P('dp'), may hold values from 40960 to 163840
- second_keyval: float32 [960, 640], P('dp'), may hold values from 122880 to 491520
- second_output: float32 [960, 960], P(None, 'dp'), may hold values from 128 to 512
- second_ffn_in: float32 [960, 2, 2560], P('dp', None, 'tensor'), may hold values from 1228.8 to 4915.2
- second_ffn_out: float32 [2560, 960], P('tensor', 'dp'), may hold values from 3686.4 to 14745.6
- second_gains: float32 [2, 960], P(None, 'dp'), may hold values from 2048 to 491520
- average_query: float32 [960, 960], P('dp'), may hold values from -0.1875 to 0.1875
- average_keyval: float32 [960, 640], P('dp'), may hold values from -0.1875 to 0.1875
- average_output: float32 [960, 960], P(None, 'dp'), may hold values from -3.5 to 3.5
- average_ffn_in: float32 [960, 2, 2560], P('dp', None, 'tensor'), may hold values from -0.1875 to 0.1875
- average_ffn_out: float32 [2560, 960], P('tensor', 'dp'), may hold values from -0.125 to 0.125
- average_gains: float32 [2, 960], P(None, 'dp'), may hold values from 0.5 to 1.5
Outputs:
- layer_out: bfloat16 [10240, 960], P('dp')
- input_grad: bfloat16 [10240, 960], P('dp')
- grad_query: float32 [960, 960], P('dp')
- grad_keyval: float32 [960, 640], P('dp')
- grad_output: float32 [960, 960], P(None, 'dp')
- grad_ffn_in: float32 [960, 2, 2560], P('dp', None, 'tensor')
- grad_ffn_out: float32 [2560, 960], P('tensor', 'dp')
- grad_gains: float32 [2, 960], P(None, 'dp')
- new_first_query: float32 [960, 960], P('dp')
- new_first_keyval: float32 [960, 640], P('dp')
- new_first_output: float32 [960, 960], P(None, 'dp')
- new_first_ffn_in: float32 [960, 2, 2560], P('dp', None, 'tensor')
- new_first_ffn_out: float32 [2560, 960], P('tensor', 'dp')
- new_first_gains: float32 [2, 960], P(None, 'dp')
- new_second_query: float32 [960, 960], P('dp')
- new_second_keyval: float32 [960, 640], P('dp')
- new_second_output: float32 [960, 960], P(None, 'dp')
- new_second_ffn_in: float32 [960, 2, 2560], P('dp', None, 'tensor')
- new_second_ffn_out: float32 [2560, 960], P('tensor', 'dp')
- new_second_gains: float32 [2, 960], P(None, 'dp')
- updated_query: float32 [960, 960], P('dp')
- updated_keyval: float32 [960, 640], P('dp')
- updated_output: float32 [960, 960], P(None, 'dp')
- updated_ffn_in: float32 [960, 2, 2560], P('dp', None, 'tensor')
- updated_ffn_out: float32 [2560, 960], P('tensor', 'dp')
- updated_gains: float32 [2, 960], P(None, 'dp')
- new_average_query: float32 [960, 960], P('dp')
- new_average_keyval: float32 [960, 640], P('dp')
- new_average_output: float32 [960, 960], P(None, 'dp')
- new_average_ffn_in: float32 [960, 2, 2560], P('dp', None, 'tensor')
- new_average_ffn_out: float32 [2560, 960], P('tensor', 'dp')
- new_average_gains: float32 [2, 960], P(None, 'dp')
The draws below stay inside these ranges and needn't reach their ends.
Inputs may be any that keep to these rules, and one draw needn't show every extreme that they name: Row b holds the lengths of the 3 sequences of index b of dp in order; each row sums to 1280 and its largest entry is exactly 1024. A permutation; query head h uses key-value group query_group[h] // 3.
All inputs are finite; a program needn't handle non-finite values. No bound on the sum of `valid` on one device may be relied on, other than what follows from the above.
Results may differ from the reference program's by a relative error of at most 0.018.
Values may be sent and summed in bfloat16 or wider, within the bound.
No kernel may reach another device: no remote copies, remote signals or barrier semaphores. Data moves between devices by JAX's collectives and lax.ppermute only.
A program may use at most 192 MiB of HBM per device.

```python
import math
import jax
import jax.numpy as jnp
import numpy as np
from jax import lax

D = 960
FF = 2560
NQ = 15
KV = 5
HD = 64
TOK_DEV = 1280
NSEQ = 3
BLOCK = 640
STEP = 10
GROUP = 3
LONGEST = 1024
OUT_FAN = 3
TOKENS = 10240
N_DP = 8


def draw_first_gains(key, part):
    key = jax.random.fold_in(key, 11)
    scales = jnp.sqrt(jnp.array([24.0, 0.4], jnp.float32) * TOKENS)
    noise = jnp.clip(jax.random.normal(key, (2, D), jnp.float32), -6.0, 6.0)
    return noise * scales[:, None]


def draw_second_gains(key, part):
    key = jax.random.fold_in(key, 13)
    lowest = jnp.array([12.0, 0.2], jnp.float32) * TOKENS
    spread = jax.random.uniform(key, (2, D), jnp.float32, 0.0, 1.0)
    return lowest[:, None] * jnp.exp(spread * jnp.log(4.0))


def with_ends(values, stream_key, low, top_value):
    place = [jax.random.randint(jax.random.fold_in(stream_key, axis), (), 0, length) for axis, length in enumerate(values.shape)]
    widest = values.shape.index(max(values.shape))
    next_to = place[:widest] + [(place[widest] + 1) % values.shape[widest]] + place[widest + 1:]
    return values.at[tuple(place)].set(low).at[tuple(next_to)].set(top_value)


def block_scale(own_key, extent, shards, smallest, largest):
    gain, own = 1.0, jax.random.fold_in(own_key, 6)
    for dim, shards_of in shards:
        draws = jnp.exp(jax.random.uniform(jax.random.fold_in(own, dim), (shards_of,), jnp.float32, smallest / len(shards), largest / len(shards)))
        gain = gain * jnp.repeat(draws, extent[dim] // shards_of).reshape([-1 if axis == dim else 1 for axis in range(len(extent))])
    return gain


def split_up(count, total, bound, skew):
    portions = [(1 << 20) // math.isqrt(grade ** skew) + 1 for grade in range(2, count + 1)]
    surplus, given = total - bound - (count - 1), [1] * (count - 1)
    while surplus > 0:
        free = [i for i in range(count - 1) if given[i] < bound]
        whole, remaining = sum([portions[i] for i in free]), surplus
        for i in free:
            extra = min(bound - given[i], max(1, remaining * portions[i] // whole), surplus)
            given[i] = given[i] + extra
            surplus = surplus - extra
    return np.array([bound] + given)


def ragged(own_key, count, total, bound, skew):
    if count == 2:
        one = jax.random.randint(own_key, (), max(1, total - bound), min(bound, total - 1) + 1)
        return jnp.stack([one, total - one])
    sizes = jnp.asarray(split_up(count, total, bound, skew), jnp.int32)
    couples = (count - 1) // 2
    donor, taker = sizes[1:1 + 2 * couples:2], sizes[2:2 + 2 * couples:2]
    margin = jnp.minimum(donor - 1, bound - taker)
    passed = jax.random.randint(jax.random.fold_in(own_key, 1), (couples,), 0, 1 << 20) % (margin + 1)
    sizes = sizes.at[1:1 + 2 * couples:2].set(donor - passed).at[2:2 + 2 * couples:2].set(taker + passed)
    return sizes[jax.random.permutation(jax.random.fold_in(own_key, 2), count)]


def centred(key, dims, width, limit, cuts=(), kind=jnp.bfloat16):
    gain = block_scale(key, dims, cuts, -0.22, 0.18) if cuts else 1.0
    entries = jax.random.normal(key, dims, jnp.float32) * width * gain
    return jnp.minimum(jnp.maximum(entries, -limit), limit).astype(kind)


def setup_inputs(seed: int = 0) -> dict:
    arg_keys = jax.random.split(jax.random.key(seed), 30)
    tokens = centred(arg_keys[0], (TOKENS, D), 1.0, 6.0, ((0, 8),))
    cotangent = centred(arg_keys[1], (TOKENS, D), 1.0, 6.0, ((0, 8),))
    lengths = jax.vmap(lambda own: ragged(own, NSEQ, TOK_DEV, LONGEST, 2))(jax.random.split(arg_keys[2], N_DP)).reshape((N_DP, NSEQ)).astype(jnp.int32)
    valid = with_ends((jax.random.randint(arg_keys[3], (TOKENS,), 0, 8) < 7).astype(jnp.int32), jax.random.fold_in(arg_keys[3], 1), 0, 1)
    query_group = jax.random.permutation(arg_keys[4], NQ).astype(jnp.int32)
    w_query = centred(arg_keys[5], (D, NQ * HD), D ** -0.5, 0.1875, ((0, 8),), jnp.float32)
    w_keyval = centred(arg_keys[6], (D, 2 * KV * HD), D ** -0.5, 0.1875, ((0, 8),), jnp.float32)
    w_output = centred(arg_keys[7], (NQ * HD, D), OUT_FAN ** -0.5, 3.5, ((1, 8),), jnp.float32)
    w_ffn_in = centred(arg_keys[8], (D, 2, FF), D ** -0.5, 0.1875, ((0, 8), (2, 4)), jnp.float32)
    w_ffn_out = centred(arg_keys[9], (FF, D), FF ** -0.5, 0.125, ((0, 4), (1, 8)), jnp.float32)
    norm_gains = jnp.clip(1.0 + 0.1 * jax.random.normal(arg_keys[10], (2, D), jnp.float32), 0.5, 1.5)
    first_query = centred(arg_keys[11], (D, NQ * HD), ((8 * TOKENS) ** 0.5), 1792.0, ((0, 8),), jnp.float32)
    first_keyval = centred(arg_keys[12], (D, 2 * KV * HD), ((25 * TOKENS) ** 0.5), 3072.0, ((0, 8),), jnp.float32)
    first_output = centred(arg_keys[13], (NQ * HD, D), ((32 * N_DP) ** 0.5), 96.0, ((1, 8),), jnp.float32)
    first_ffn_in = centred(arg_keys[14], (D, 2, FF), ((0.12 * TOKENS) ** 0.5), 224.0, ((0, 8), (2, 4)), jnp.float32)
    first_ffn_out = centred(arg_keys[15], (FF, D), ((0.36 * TOKENS) ** 0.5), 384.0, ((0, 4), (1, 8)), jnp.float32)
    first_gains = draw_first_gains(jax.random.fold_in(arg_keys[29], 71), 0)
    second_query = jnp.clip(jnp.exp(math.log(163840.0) - 1.3862944 * jax.random.uniform(arg_keys[17], (D, NQ * HD), jnp.float32) ** block_scale(arg_keys[17], (D, NQ * HD), ((0, 8),), -0.2, 0.2)), 40960.0, 163840.0)
    second_keyval = jnp.clip(jnp.exp(math.log(491520.0) - 1.3862944 * jax.random.uniform(arg_keys[18], (D, 2 * KV * HD), jnp.float32) ** block_scale(arg_keys[18], (D, 2 * KV * HD), ((0, 8),), -0.2, 0.2)), 122880.0, 491520.0)
    second_output = jnp.clip(jnp.exp(math.log(512.0) - 1.3862944 * jax.random.uniform(arg_keys[19], (NQ * HD, D), jnp.float32) ** block_scale(arg_keys[19], (NQ * HD, D), ((1, 8),), -0.2, 0.2)), 128.0, 512.0)
    second_ffn_in = jnp.clip(jnp.exp(math.log(4915.2) - 1.3862944 * jax.random.uniform(arg_keys[20], (D, 2, FF), jnp.float32) ** block_scale(arg_keys[20], (D, 2, FF), ((0, 8), (2, 4)), -0.2, 0.2)), 1228.8, 4915.2)
    second_ffn_out = jnp.clip(jnp.exp(math.log(14745.6) - 1.3862944 * jax.random.uniform(arg_keys[21], (FF, D), jnp.float32) ** block_scale(arg_keys[21], (FF, D), ((0, 4), (1, 8)), -0.2, 0.2)), 3686.4, 14745.6)
    second_gains = draw_second_gains(jax.random.fold_in(arg_keys[29], 71), 0)
    average_query = centred(arg_keys[23], (D, NQ * HD), D ** -0.5, 0.1875, ((0, 8),), jnp.float32)
    average_keyval = centred(arg_keys[24], (D, 2 * KV * HD), D ** -0.5, 0.1875, ((0, 8),), jnp.float32)
    average_output = centred(arg_keys[25], (NQ * HD, D), OUT_FAN ** -0.5, 3.5, ((1, 8),), jnp.float32)
    average_ffn_in = centred(arg_keys[26], (D, 2, FF), D ** -0.5, 0.1875, ((0, 8), (2, 4)), jnp.float32)
    average_ffn_out = centred(arg_keys[27], (FF, D), FF ** -0.5, 0.125, ((0, 4), (1, 8)), jnp.float32)
    average_gains = jnp.clip(1.0 + 0.1 * jax.random.normal(arg_keys[28], (2, D), jnp.float32), 0.5, 1.5)
    return dict(tokens=tokens, cotangent=cotangent, lengths=lengths, valid=valid, query_group=query_group, w_query=w_query, w_keyval=w_keyval, w_output=w_output, w_ffn_in=w_ffn_in, w_ffn_out=w_ffn_out, norm_gains=norm_gains, first_query=first_query, first_keyval=first_keyval, first_output=first_output, first_ffn_in=first_ffn_in, first_ffn_out=first_ffn_out, first_gains=first_gains, second_query=second_query, second_keyval=second_keyval, second_output=second_output, second_ffn_in=second_ffn_in, second_ffn_out=second_ffn_out, second_gains=second_gains, average_query=average_query, average_keyval=average_keyval, average_output=average_output, average_ffn_in=average_ffn_in, average_ffn_out=average_ffn_out, average_gains=average_gains)


norm_eps = 1e-05
rope_base = 10000.0
beta_first = 0.5
beta_second = 0.5
adam_eps = 1e-08
average_keep = 0.5
highest = lax.Precision.HIGHEST

@jax.custom_vjp
def low(v):
    return lax.optimization_barrier(v.astype(jnp.bfloat16)).astype(jnp.float32)

@jax.custom_vjp
def low_back(v):
    return v

def low_keep(v):
    return (low(v), None)

def low_pass(kept, grad):
    return (grad,)

def back_keep(v):
    return (v, None)

def back_low(kept, grad):
    return (low(grad),)
low.defvjp(low_keep, low_pass)
low_back.defvjp(back_keep, back_low)

def rms_factor(values):
    return lax.rsqrt(lax.optimization_barrier(jnp.mean(values * values, axis=-1, keepdims=True)) + norm_eps)

def rotate_pairs(values, cosine, sine):
    half_width = values.shape[-1] // 2
    first = values[..., :half_width]
    second = values[..., half_width:]
    return jnp.concatenate([first * cosine - second * sine, second * cosine + first * sine], axis=-1)

def sequence_layout(length_row, row_count, valid_row):
    seq_count = length_row.shape[0]
    seq_ends = jnp.cumsum(length_row).astype(jnp.int32)
    seq_starts = (seq_ends - length_row).astype(jnp.int32)
    row_index = jnp.arange(row_count, dtype=jnp.int32)
    segment = lax.optimization_barrier(jnp.sum((row_index[:, None] >= seq_ends[None, :]).astype(jnp.int32), axis=1))
    matches = segment[:, None] == jnp.arange(seq_count, dtype=jnp.int32)[None, :]
    position = row_index - lax.optimization_barrier(jnp.sum(jnp.where(matches, seq_starts[None, :], 0), axis=1))
    frequency = rope_base ** (-jnp.arange(0, HD, 2, dtype=jnp.float32) / HD)
    angles = position.astype(jnp.float32)[:, None] * frequency[None, :]
    allowed = (segment[:, None] == segment[None, :]) & (row_index[None, :] <= row_index[:, None])
    allowed = allowed & ((valid_row[None, :] == 1) | (row_index[:, None] == row_index[None, :]))
    return (jnp.cos(angles), jnp.sin(angles), allowed)

def attend(block_queries, head_keys, head_values, block_mask):
    scores = jnp.einsum('bnh,tnh->nbt', block_queries, head_keys, precision=highest) * HD ** (-0.5)
    scores = low_back(scores)
    scores = jnp.where(block_mask[None], scores, -1e+30)
    probs = low(jax.nn.softmax(scores, axis=-1))
    return jnp.einsum('nbt,tnh->bnh', probs, head_values, precision=highest)

def residual_block(inputs, params, owners, cosine, sine, allowed):
    w_query, w_keyval, w_output, w_ffn_in, w_ffn_out, gains = params
    row_count = inputs.shape[0]
    normed_one = low(inputs * rms_factor(inputs) * gains[0])
    queries = jnp.dot(normed_one, low(w_query), precision=highest).reshape(row_count, NQ, HD)
    keyval = jnp.dot(normed_one, low(w_keyval), precision=highest).reshape(row_count, 2, KV, HD)
    queries = low(rotate_pairs(low_back(queries), cosine[:, None, :], sine[:, None, :]))
    keys = low(rotate_pairs(low_back(keyval[:, 0]), cosine[:, None, :], sine[:, None, :]))
    values = low(low_back(keyval[:, 1]))
    head_keys = jnp.take(keys, owners, axis=1)
    head_values = jnp.take(values, owners, axis=1)
    blocks = row_count // BLOCK
    kept_attend = jax.checkpoint(attend)
    attended = lax.map(lambda paired: kept_attend(paired[0], head_keys, head_values, paired[1]), (queries.reshape(blocks, BLOCK, NQ, HD), allowed.reshape(blocks, BLOCK, row_count)))
    attended = low(low_back(attended.reshape(row_count, NQ * HD)))
    branch = low_back(jnp.dot(attended, low(w_output), precision=highest))
    middle = inputs + branch
    normed_two = low(middle * rms_factor(middle) * gains[1])
    gate_up = jnp.einsum('td,dsf->tsf', normed_two, low(w_ffn_in), precision=highest)
    gate_act = low_back(gate_up[:, 0])
    up_act = low_back(gate_up[:, 1])
    hidden = low(jax.nn.silu(gate_act) * up_act)
    return middle + jnp.dot(hidden, low(w_ffn_out), precision=highest)

def adam_step(weight, first, second, average, gradient, step_rate, decay_rate):
    first_new = beta_first * first + (1.0 - beta_first) * gradient
    second_new = beta_second * second + (1.0 - beta_second) * gradient * gradient
    corrected_first = first_new / (1.0 - beta_first ** STEP)
    corrected_second = second_new / (1.0 - beta_second ** STEP)
    weight_new = weight - step_rate * (corrected_first / (jnp.sqrt(corrected_second) + adam_eps) + decay_rate * weight)
    average_new = average_keep * average + (1.0 - average_keep) * weight_new
    return (first_new, second_new, weight_new, average_new)

def reference(tokens, cotangent, lengths, valid, query_group, w_query, w_keyval, w_output, w_ffn_in, w_ffn_out, norm_gains, first_query, first_keyval, first_output, first_ffn_in, first_ffn_out, first_gains, second_query, second_keyval, second_output, second_ffn_in, second_ffn_out, second_gains, average_query, average_keyval, average_output, average_ffn_in, average_ffn_out, average_gains):
    weights = (w_query, w_keyval, w_output, w_ffn_in, w_ffn_out, norm_gains)
    owners = (query_group // GROUP).astype(jnp.int32)
    token_blocks = tokens.reshape(N_DP, TOK_DEV, D)
    cotangent_blocks = cotangent.reshape(N_DP, TOK_DEV, D)
    valid_blocks = valid.reshape(N_DP, TOK_DEV)

    def one_device(running, element):
        token_rows, cotangent_rows, length_row, valid_row = element
        cosine, sine, allowed = sequence_layout(length_row, TOK_DEV, valid_row)

        def forward(inputs, *params):
            return residual_block(inputs, params, owners, cosine, sine, allowed)
        result, pullback = jax.vjp(forward, token_rows.astype(jnp.float32), *weights)
        gradients = pullback(cotangent_rows.astype(jnp.float32))
        running = tuple((earlier + current for earlier, current in zip(running, gradients[1:])))
        return (running, (result.astype(jnp.bfloat16), gradients[0].astype(jnp.bfloat16)))
    initial = tuple((jnp.zeros_like(weight) for weight in weights))
    summed, (layer_rows, input_rows) = lax.scan(one_device, initial, (token_blocks, cotangent_blocks, lengths, valid_blocks))
    matrix_rate = 0.5 * D ** (-0.5)
    rates = (matrix_rate, matrix_rate, 0.5 * OUT_FAN ** (-0.5), matrix_rate, 0.5 * FF ** (-0.5), 0.3)
    decays = (0.1, 0.1, 0.1, 0.1, 0.1, 0.0)
    firsts = (first_query, first_keyval, first_output, first_ffn_in, first_ffn_out, first_gains)
    seconds = (second_query, second_keyval, second_output, second_ffn_in, second_ffn_out, second_gains)
    averages = (average_query, average_keyval, average_output, average_ffn_in, average_ffn_out, average_gains)
    updates = [adam_step(weights[member], firsts[member], seconds[member], averages[member], summed[member], rates[member], decays[member]) for member in range(6)]
    return (layer_rows.reshape(TOKENS, D), input_rows.reshape(TOKENS, D), summed[0], summed[1], summed[2], summed[3], summed[4], summed[5], updates[0][0], updates[1][0], updates[2][0], updates[3][0], updates[4][0], updates[5][0], updates[0][1], updates[1][1], updates[2][1], updates[3][1], updates[4][1], updates[5][1], updates[0][2], updates[1][2], updates[2][2], updates[3][2], updates[4][2], updates[5][2], updates[0][3], updates[1][3], updates[2][3], updates[3][3], updates[4][3], updates[5][3])
```

```python
import functools

import jax
import jax.numpy as jnp
import numpy as np
from jax import lax
from jax.experimental import pallas as pl
from jax.experimental.pallas import tpu as pltpu
from jax.sharding import PartitionSpec as P

D = 960
FF = 2560
NQ = 15
KV = 5
HD = 64
STEP = 10
GROUP = 3
OUT_FAN = 3
SLAB = 320
QUART = 80
HEADW = GROUP * HD
KEY_BLOCK = 256

norm_eps = 1e-05
rope_base = 10000.0
beta_first = 0.5
beta_second = 0.5
adam_eps = 1e-08
average_keep = 0.5
bf16 = jnp.bfloat16
f32 = jnp.float32
VMEM_LIMIT = 48 * 1024 * 1024


def params(*semantics):
    return pltpu.CompilerParams(dimension_semantics=semantics, vmem_limit_bytes=VMEM_LIMIT)


def swap(x, axis, offset):
    count = lax.axis_size(axis)
    return lax.ppermute(x, axis, [(i, i ^ offset) for i in range(count)])


def dot_nn(a, b):
    return lax.dot_general(a, b, (((1,), (0,)), ((), ())), preferred_element_type=f32)


def dot_nt(a, b):
    return lax.dot_general(a, b, (((1,), (1,)), ((), ())), preferred_element_type=f32)


def dot_tn(a, b):
    return lax.dot_general(a, b, (((0,), (0,)), ((), ())), preferred_element_type=f32)


def place_body(index_ref, *refs):
    out_ref = refs[-1]
    slot = 0
    for piece in refs[:-1]:
        for part in range(piece.shape[0]):
            out_ref[index_ref[slot]] = piece[part]
            slot += 1


def place(pieces, index):
    total = sum(piece.shape[0] for piece in pieces)
    _, rows, columns = pieces[0].shape
    whole = pl.BlockSpec(memory_space=pltpu.VMEM)
    return pl.pallas_call(
        place_body,
        out_shape=jax.ShapeDtypeStruct((total, rows, columns), pieces[0].dtype),
        in_specs=[pl.BlockSpec(memory_space=pltpu.SMEM)] + [whole] * len(pieces),
        out_specs=whole,
        compiler_params=pltpu.CompilerParams(vmem_limit_bytes=VMEM_LIMIT),
        cost_estimate=pl.CostEstimate(flops=0, bytes_accessed=4 * total * rows * columns, transcendentals=0),
        name="place",
    )(index, *pieces)


def gather_dp(x):
    count = lax.axis_size("dp")
    if count != 8:
        return lax.all_gather(x, "dp", axis=0, tiled=True)
    me = lax.axis_index("dp")
    along_z = [x] + [swap(x, "dp", k) for k in (2, 4, 6)]
    along_y = [swap(piece, "dp", 1) for piece in along_z]
    offsets = [0, 2, 4, 6, 1, 3, 5, 7]
    index = jnp.stack([me ^ k for k in offsets]).astype(jnp.int32)
    out = place([piece[None] for piece in along_z + along_y], index)
    return out.reshape(count * x.shape[0], x.shape[1])


def scatter_dp(g, direct):
    count = lax.axis_size("dp")
    if count != 8:
        return lax.psum_scatter(g.astype(f32), "dp", scatter_dimension=0, tiled=True)
    me = lax.axis_index("dp")
    rows, columns = g.shape[0] // count, g.shape[1]
    if direct:
        shaped = g.reshape(count, rows, columns)
        total = lax.dynamic_index_in_dim(shaped, me, 0, False).astype(f32)
        for k in (6, 4, 2, 7, 5, 3, 1):
            piece = lax.dynamic_index_in_dim(shaped, me ^ k, 0, False)
            total = total + swap(piece, "dp", k).astype(f32)
        return total
    shaped = g.reshape(count // 2, 2, rows, columns)
    at_y, at_z = me & 1, me >> 1
    sent = lax.dynamic_index_in_dim(shaped, 1 - at_y, 1, False)
    kept = lax.dynamic_index_in_dim(shaped, at_y, 1, False)
    half = kept.astype(f32) + swap(sent, "dp", 1).astype(f32)
    half_low = half.astype(bf16)
    total = lax.dynamic_index_in_dim(half, at_z, 0, False)
    for k in (3, 2, 1):
        piece = lax.dynamic_index_in_dim(half_low, at_z ^ k, 0, False)
        total = total + swap(piece, "dp", 2 * k).astype(f32)
    return total


def gather_tensor(x):
    across = swap(x, "tensor", 2)
    beside = swap(x, "tensor", 1)
    return [x, beside, across, swap(across, "tensor", 1)]


def scatter_tensor(pieces):
    low = [piece.astype(bf16) for piece in pieces]
    near = pieces[0].astype(f32) + swap(low[1], "tensor", 1).astype(f32)
    far = pieces[2].astype(f32) + swap(low[3], "tensor", 1).astype(f32)
    return near + swap(far.astype(bf16), "tensor", 2).astype(f32)


def exchange_tensor(pieces):
    return [pieces[0]] + [swap(pieces[k], "tensor", k) for k in (1, 2, 3)]


def proj_body(normalise, x_ref, gain_ref, w_ref, cos_ref, sin_ref, *outs):
    rows = x_ref.shape[0]
    if normalise:
        normed_ref, q_ref, k_ref, v_ref = outs
        x = x_ref[...].astype(f32)
        factor = lax.rsqrt(jnp.mean(x * x, axis=-1, keepdims=True) + norm_eps)
        normed = (x * factor * gain_ref[...]).astype(bf16)
        normed_ref[...] = normed
    else:
        q_ref, k_ref, v_ref = outs
        normed = x_ref[...]
    y = dot_nn(normed, w_ref[...])
    first, second = y[:, :128], y[:, 128:256]
    cosine, sine = cos_ref[...], sin_ref[...]
    turned_first = first * cosine - second * sine
    turned_second = second * cosine + first * sine
    for head in range(GROUP + 1):
        columns = slice(32 * head, 32 * head + 32)
        both = jnp.concatenate([turned_first[:, columns], turned_second[:, columns]], axis=1)
        if head < GROUP:
            both = (both.astype(bf16).astype(f32) * HD ** (-0.5)).astype(bf16)
            q_ref[0, head * rows : (head + 1) * rows, :] = both
        else:
            k_ref[...] = both.astype(bf16)
    if q_ref.shape[1] > GROUP * rows:
        q_ref[0, GROUP * rows :, :] = jnp.zeros((q_ref.shape[1] - GROUP * rows, HD), bf16)
    v_ref[...] = y[:, 256:].astype(bf16)


def project(x, gain, weight, cosine, sine, rows, lanes, normalise):
    count = x.shape[0] // rows
    outs = [
        (jax.ShapeDtypeStruct((count, lanes, HD), bf16), pl.BlockSpec((1, lanes, HD), lambda i: (i, 0, 0))),
        (jax.ShapeDtypeStruct((x.shape[0], HD), bf16), pl.BlockSpec((rows, HD), lambda i: (i, 0))),
        (jax.ShapeDtypeStruct((x.shape[0], HD), bf16), pl.BlockSpec((rows, HD), lambda i: (i, 0))),
    ]
    if normalise:
        outs = [
            (jax.ShapeDtypeStruct(x.shape, bf16), pl.BlockSpec((rows, D), lambda i: (i, 0)))
        ] + outs
    return pl.pallas_call(
        functools.partial(proj_body, normalise),
        grid=(count,),
        out_shape=[shape for shape, _ in outs],
        in_specs=[
            pl.BlockSpec((rows, D), lambda i: (i, 0)),
            pl.BlockSpec((1, D), lambda i: (0, 0)),
            pl.BlockSpec((D, SLAB), lambda i: (0, 0)),
            pl.BlockSpec((rows, 128), lambda i: (i, 0)),
            pl.BlockSpec((rows, 128), lambda i: (i, 0)),
        ],
        out_specs=[spec for _, spec in outs],
        compiler_params=params("arbitrary"),
        cost_estimate=pl.CostEstimate(
            flops=2 * x.shape[0] * D * SLAB, bytes_accessed=x.size * 4 + D * SLAB * 2, transcendentals=0
        ),
        name="project",
    )(x, gain, weight, cosine, sine)


def key_mask(key_ref, at, size, row, start):
    key = key_ref[pl.ds(at, size), :1]
    index = at + lax.broadcasted_iota(jnp.int32, (size, row.shape[1]), 0)
    return ((key >= start) & (key <= row)) | (index == row)


def forward_body(block_ref, low_ref, high_ref, q_ref, k_ref, vt_ref, key_ref, row_ref, start_ref, out_ref, log_ref, acc):
    step = pl.program_id(0)
    q = q_ref[0]
    row, start = row_ref[0], start_ref[0]
    lanes = q.shape[0]
    rows = out_ref.shape[0]
    acc[...] = jnp.zeros_like(acc)

    def visit(j, carry):
        peak, total = carry
        at = pl.multiple_of(j * KEY_BLOCK, KEY_BLOCK)
        scores = dot_nt(k_ref[pl.ds(at, KEY_BLOCK), :], q)
        scores = jnp.where(key_mask(key_ref, at, KEY_BLOCK, row, start), scores, -1e30)
        new_peak = jnp.maximum(peak, jnp.max(scores, axis=0, keepdims=True))
        exponent = jnp.exp(scores - new_peak)
        shrink = jnp.exp(peak - new_peak)
        total = total * shrink + jnp.sum(exponent, axis=0, keepdims=True)
        acc[...] = acc[...] * shrink + dot_nn(vt_ref[:, pl.ds(at, KEY_BLOCK)], exponent.astype(bf16))
        return new_peak, total

    peak, total = lax.fori_loop(
        low_ref[step],
        high_ref[step],
        visit,
        (jnp.full((1, lanes), -1e30, f32), jnp.zeros((1, lanes), f32)),
    )
    log_ref[0] = peak + jnp.log(total)
    attended = jnp.transpose(acc[...] / total)
    out_ref[...] = jnp.concatenate(
        [attended[head * rows : (head + 1) * rows] for head in range(GROUP)], axis=1
    ).astype(bf16)


def attend_forward(blocks, low, high, q, k, v, key, row, start, rows):
    count = blocks.shape[0]
    length, lanes = k.shape[0], q.shape[1]
    picked = lambda i, b, lo, hi: (b[i], 0, 0)
    whole = lambda i, b, lo, hi: (0, 0)
    return pl.pallas_call(
        forward_body,
        out_shape=[
            jax.ShapeDtypeStruct((count * rows, HEADW), bf16),
            jax.ShapeDtypeStruct((count, 1, lanes), f32),
        ],
        grid_spec=pltpu.PrefetchScalarGridSpec(
            num_scalar_prefetch=3,
            grid=(count,),
            in_specs=[
                pl.BlockSpec((1, lanes, HD), picked),
                pl.BlockSpec((length, HD), whole),
                pl.BlockSpec((HD, length), whole),
                pl.BlockSpec((length, 128), whole),
                pl.BlockSpec((1, 1, lanes), picked),
                pl.BlockSpec((1, 1, lanes), picked),
            ],
            out_specs=[
                pl.BlockSpec((rows, HEADW), lambda i, b, lo, hi: (i, 0)),
                pl.BlockSpec((1, 1, lanes), lambda i, b, lo, hi: (i, 0, 0)),
            ],
            scratch_shapes=[pltpu.VMEM((HD, lanes), f32)],
        ),
        compiler_params=params("arbitrary"),
        cost_estimate=pl.CostEstimate(
            flops=8 * count * lanes * length * HD, bytes_accessed=count * lanes * 512, transcendentals=count * lanes * length
        ),
        name="attend_forward",
    )(blocks, low, high, q, k, jnp.transpose(v), key, row, start)


def backward_body(
    block_ref, low_ref, high_ref, q_ref, k_ref, kt_ref, v_ref, key_ref, row_ref, start_ref, log_ref,
    out_ref, up_ref, cos_ref, sin_ref, dq_ref, dk_ref, dv_ref, acc,
):
    step = pl.program_id(0)
    rows = up_ref.shape[0]
    q = q_ref[0]
    lanes = q.shape[0]
    row, start, logs = row_ref[0], start_ref[0], log_ref[0]

    @pl.when(step == 0)
    def _():
        dk_ref[...] = jnp.zeros_like(dk_ref)
        dv_ref[...] = jnp.zeros_like(dv_ref)

    def stack(wide):
        parts = [wide[:, head * HD : (head + 1) * HD] for head in range(GROUP)]
        if lanes > GROUP * rows:
            parts.append(jnp.zeros((lanes - GROUP * rows, HD), wide.dtype))
        return jnp.concatenate(parts, axis=0)

    up = stack(up_ref[...])
    both = up.astype(f32) * stack(out_ref[...]).astype(f32)
    both_high = both.astype(bf16)
    both_low = (both - both_high.astype(f32)).astype(bf16)
    ones = jnp.ones((8, HD), bf16)
    inner = (dot_nt(ones, both_high) + dot_nt(ones, both_low))[:1]
    acc[...] = jnp.zeros_like(acc)

    def visit(j, carry):
        at = pl.multiple_of(j * KEY_BLOCK, KEY_BLOCK)
        here = pl.ds(at, KEY_BLOCK)
        scores = dot_nt(k_ref[here, :], q)
        scores = jnp.where(key_mask(key_ref, at, KEY_BLOCK, row, start), scores, -1e30)
        probs = jnp.exp(scores - logs)
        d_probs = dot_nt(v_ref[here, :], up)
        d_scores = (probs * (d_probs - inner)).astype(bf16)
        dv_ref[here, :] += dot_nn(probs.astype(bf16), up)
        dk_ref[here, :] += dot_nn(d_scores, q)
        acc[...] += dot_nn(kt_ref[:, here], d_scores)
        return carry

    lax.fori_loop(low_ref[step], high_ref[step], visit, 0)
    first, second = acc[:32], acc[32:]
    cosine, sine = cos_ref[0], sin_ref[0]
    scale = HD ** (-0.5)
    d_first = jnp.transpose((first * cosine + second * sine) * scale)
    d_second = jnp.transpose((second * cosine - first * sine) * scale)
    parts = [d_first[head * rows : (head + 1) * rows] for head in range(GROUP)]
    parts += [d_second[head * rows : (head + 1) * rows] for head in range(GROUP)]
    dq_ref[...] = jnp.concatenate(parts, axis=1).astype(bf16)


def attend_backward(blocks, low, high, q, k, v, key, row, start, logs, attended, upstream, cosine, sine, rows):
    count = blocks.shape[0]
    length, lanes = k.shape[0], q.shape[1]
    picked = lambda i, b, lo, hi: (b[i], 0, 0)
    whole = lambda i, b, lo, hi: (0, 0)
    mine = lambda i, b, lo, hi: (i, 0)
    return pl.pallas_call(
        backward_body,
        out_shape=[
            jax.ShapeDtypeStruct((count * rows, HEADW), bf16),
            jax.ShapeDtypeStruct((length, HD), f32),
            jax.ShapeDtypeStruct((length, HD), f32),
        ],
        grid_spec=pltpu.PrefetchScalarGridSpec(
            num_scalar_prefetch=3,
            grid=(count,),
            in_specs=[
                pl.BlockSpec((1, lanes, HD), picked),
                pl.BlockSpec((length, HD), whole),
                pl.BlockSpec((HD, length), whole),
                pl.BlockSpec((length, HD), whole),
                pl.BlockSpec((length, 128), whole),
                pl.BlockSpec((1, 1, lanes), picked),
                pl.BlockSpec((1, 1, lanes), picked),
                pl.BlockSpec((1, 1, lanes), lambda i, b, lo, hi: (i, 0, 0)),
                pl.BlockSpec((rows, HEADW), mine),
                pl.BlockSpec((rows, HEADW), mine),
                pl.BlockSpec((1, 32, lanes), picked),
                pl.BlockSpec((1, 32, lanes), picked),
            ],
            out_specs=[
                pl.BlockSpec((rows, HEADW), mine),
                pl.BlockSpec((length, HD), whole),
                pl.BlockSpec((length, HD), whole),
            ],
            scratch_shapes=[pltpu.VMEM((HD, lanes), f32)],
        ),
        compiler_params=params("arbitrary"),
        cost_estimate=pl.CostEstimate(
            flops=20 * count * lanes * length * HD, bytes_accessed=count * lanes * 1024, transcendentals=count * lanes * length
        ),
        name="attend_backward",
    )(blocks, low, high, q, k, jnp.transpose(k), v, key, row, start, logs, attended, upstream, cosine, sine)


def out_body(x_ref, gain_ref, *refs):
    pieces, weights = refs[: KV], refs[KV : 2 * KV]
    middle_ref, normed_ref = refs[2 * KV :]
    middle = x_ref[...].astype(f32)
    for piece, weight in zip(pieces, weights):
        middle = middle + dot_nt(piece[...], weight[...])
    middle_ref[...] = middle
    factor = lax.rsqrt(jnp.mean(middle * middle, axis=-1, keepdims=True) + norm_eps)
    normed_ref[...] = (middle * factor * gain_ref[...]).astype(bf16)


def out_project(x, gain, pieces, weights):
    rows = 256
    count = x.shape[0] // rows
    by_row = lambda width: pl.BlockSpec((rows, width), lambda i: (i, 0))
    return pl.pallas_call(
        out_body,
        grid=(count,),
        out_shape=[jax.ShapeDtypeStruct(x.shape, f32), jax.ShapeDtypeStruct(x.shape, bf16)],
        in_specs=[by_row(D), pl.BlockSpec((1, D), lambda i: (0, 0))]
        + [by_row(HEADW)] * KV
        + [pl.BlockSpec((D, HEADW), lambda i: (0, 0))] * KV,
        out_specs=[by_row(D), by_row(D)],
        compiler_params=params("arbitrary"),
        cost_estimate=pl.CostEstimate(
            flops=2 * x.shape[0] * D * D, bytes_accessed=x.size * 10 + D * D * 2, transcendentals=0
        ),
        name="out_project",
    )(x, gain, *pieces, *weights)


def rms_factor(values):
    return lax.rsqrt(jnp.mean(values * values, axis=-1, keepdims=True) + norm_eps)


def one_hot(index, size):
    return (jnp.arange(size, dtype=jnp.int32)[:, None] == index[None, :]).astype(bf16)


def adam_step(weight, first, second, average, gradient, step_rate, decay_rate):
    first_new = beta_first * first + (1.0 - beta_first) * gradient
    second_new = beta_second * second + (1.0 - beta_second) * gradient * gradient
    corrected_first = first_new / (1.0 - beta_first**STEP)
    corrected_second = second_new / (1.0 - beta_second**STEP)
    weight_new = weight - step_rate * (
        corrected_first / (jnp.sqrt(corrected_second) + adam_eps) + decay_rate * weight
    )
    average_new = average_keep * average + (1.0 - average_keep) * weight_new
    return (first_new, second_new, weight_new, average_new)


def own_columns(slot_head, group):
    heads = lax.dynamic_slice(slot_head, (group * GROUP,), (GROUP,))
    bases = jnp.concatenate([heads * HD, (NQ * HD + group * HD)[None]])
    half = (bases[:, None] + jnp.arange(32, dtype=jnp.int32)[None, :]).reshape(-1)
    value = NQ * HD + KV * HD + group * HD + jnp.arange(HD, dtype=jnp.int32)
    return jnp.concatenate([half, half + 32, value])


def shared_columns(slot_head, part):
    group = KV - 1
    heads = slot_head[group * GROUP :]
    bases = jnp.concatenate([heads * HD, jnp.full((1,), NQ * HD + group * HD, jnp.int32)])
    half = (bases[:, None] + 8 * part + jnp.arange(8, dtype=jnp.int32)[None, :]).reshape(-1)
    value = NQ * HD + KV * HD + group * HD + 16 * part + jnp.arange(16, dtype=jnp.int32)
    return jnp.concatenate([half, half + 32, value])


def own_out(slot_head, group):
    heads = lax.dynamic_slice(slot_head, (group * GROUP,), (GROUP,))
    return (heads[:, None] * HD + jnp.arange(HD, dtype=jnp.int32)[None, :]).reshape(-1)


def shared_out(slot_head, part):
    heads = slot_head[(KV - 1) * GROUP :]
    return (heads[:, None] * HD + 16 * part + jnp.arange(16, dtype=jnp.int32)[None, :]).reshape(-1)


def slab_order(t):
    part, rest = [], []
    for half in range(2):
        for head in range(GROUP + 1):
            for quarter in range(4):
                part += [quarter] * 8
                rest += [half * 32 + head * 8 + r for r in range(8)]
    for quarter in range(4):
        part += [quarter] * 16
        rest += [64 + r for r in range(16)]
    return (np.array(part, np.int32) ^ t) * QUART + np.array(rest, np.int32)


def out_order(t):
    part, rest = [], []
    for head in range(GROUP):
        for quarter in range(4):
            part += [quarter] * 16
            rest += [head * 16 + r for r in range(16)]
    return (np.array(part, np.int32) ^ t) * 48 + np.array(rest, np.int32)


def local(
    tokens, cotangent, lengths, valid, query_group,
    w_query, w_keyval, w_output, w_ffn_in, w_ffn_out, norm_gains,
    first_query, first_keyval, first_output, first_ffn_in, first_ffn_out, first_gains,
    second_query, second_keyval, second_output, second_ffn_in, second_ffn_out, second_gains,
    average_query, average_keyval, average_output, average_ffn_in, average_ffn_out, average_gains,
):
    t = lax.axis_index("tensor").astype(jnp.int32)
    row_count = tokens.shape[0]
    owned_rows = w_query.shape[0]
    hidden_count = w_ffn_out.shape[0]
    part_rows = row_count // 8
    slots = jnp.arange(NQ, dtype=jnp.int32)
    slot_head = jnp.sum(
        jnp.where(query_group[None, :] == slots[:, None], slots[None, :], 0), axis=1
    ).astype(jnp.int32)

    projection = jnp.concatenate([w_query, w_keyval], axis=1).astype(bf16)
    mine = jnp.concatenate([own_columns(slot_head, t), shared_columns(slot_head, t)])
    gain_high = norm_gains.astype(bf16)
    gain_rest = norm_gains - gain_high.astype(f32)
    gain_middle = gain_rest.astype(bf16)
    gain_low = (gain_rest - gain_middle.astype(f32)).astype(bf16)
    gain_parts = jnp.concatenate([gain_high, gain_middle, gain_low], axis=0)
    attn_part = jnp.concatenate(
        [dot_nn(projection, one_hot(mine, NQ * HD + 2 * KV * HD)).astype(bf16), jnp.transpose(gain_parts)], axis=1
    )
    out_mine = jnp.concatenate([own_out(slot_head, t), shared_out(slot_head, t)])
    out_part = dot_tn(w_output.astype(bf16), one_hot(out_mine, NQ * HD)).astype(bf16)
    in_part = w_ffn_in.astype(bf16).reshape(owned_rows, 2 * hidden_count)
    ffn_out_part = jnp.transpose(w_ffn_out.astype(bf16))

    attn_all = gather_dp(attn_part)
    out_part, in_part, ffn_out_part, attn_all = lax.optimization_barrier(
        (out_part, in_part, ffn_out_part, attn_all)
    )
    shared_all = gather_tensor(attn_all[:, SLAB : SLAB + QUART])
    shared_slab = dot_nn(jnp.concatenate(shared_all, axis=1), one_hot(slab_order(t), SLAB)).astype(bf16)
    own_slab = attn_all[:, :SLAB]
    slabs = gather_tensor(own_slab)
    out_all = gather_dp(out_part)
    gate_rows = gather_dp(in_part)
    ffn_rows = gather_dp(ffn_out_part)
    out_pieces = gather_tensor(out_all)
    out_weights = [piece[:, :HEADW] for piece in out_pieces]
    out_shared = dot_nn(
        jnp.concatenate([piece[:, HEADW:] for piece in out_pieces], axis=1), one_hot(out_order(t), HEADW)
    ).astype(bf16)
    out_weights.append(out_shared)
    pick_gain = (jnp.arange(SLAB + QUART + 6)[None, :] == SLAB + QUART + jnp.arange(8)[:, None]).astype(bf16)
    gains_six = dot_nt(pick_gain, attn_all)
    gains = gains_six[0:2] + gains_six[2:4] + gains_six[4:6]

    seq_ends = jnp.cumsum(lengths[0])
    seq_starts = seq_ends - lengths[0]
    row_index = jnp.arange(row_count, dtype=jnp.int32)
    segment = jnp.sum((row_index[:, None] >= seq_ends[None, :]).astype(jnp.int32), axis=1)
    matches = segment[:, None] == jnp.arange(lengths.shape[1], dtype=jnp.int32)[None, :]
    row_start = jnp.sum(jnp.where(matches, seq_starts[None, :], 0), axis=1).astype(jnp.int32)
    position = (row_index - row_start).astype(f32)
    key_index = jnp.where(valid == 1, row_index, -1)
    key_index = jnp.broadcast_to(key_index[:, None], (row_count, 128))
    frequency = rope_base ** (-jnp.arange(0, HD, 2, dtype=f32) / HD)
    angles = position[:, None] * frequency[None, :]
    cosine, sine = jnp.cos(angles), jnp.sin(angles)

    def by_block(values, rows, lanes, fill):
        count = row_count // rows
        if values.ndim == 1:
            shaped = jnp.tile(values.reshape(count, 1, rows), (1, 1, GROUP))
        else:
            shaped = jnp.tile(jnp.swapaxes(values.reshape(count, rows, 32), 1, 2), (1, 1, GROUP))
        return jnp.pad(shaped, ((0, 0), (0, 0), (0, lanes - GROUP * rows)), constant_values=fill)

    own_block, own_lanes = 256, 768
    part_lanes = 512
    far = 1 << 20
    own_row, own_start = (by_block(v, own_block, own_lanes, far) for v in (row_index, row_start))
    part_row, part_start = (by_block(v, part_rows, part_lanes, far) for v in (row_index, row_start))
    own_turn = [by_block(v, own_block, own_lanes, 0.0) for v in (cosine, sine)]
    part_turn = [by_block(v, part_rows, part_lanes, 0.0) for v in (cosine, sine)]
    own_blocks = jnp.arange(row_count // own_block, dtype=jnp.int32)
    own_low = row_start[own_blocks * own_block] // KEY_BLOCK
    own_high = own_blocks + 1
    part_blocks = jnp.stack([t, 7 - t])
    part_low = row_start[part_blocks * part_rows] // KEY_BLOCK
    part_high = (part_blocks * part_rows + part_rows + KEY_BLOCK - 1) // KEY_BLOCK

    def take_rows(values, owner):
        return jnp.concatenate(
            [
                lax.dynamic_slice_in_dim(values, part_rows * block, part_rows, 0)
                for block in (owner, 7 - owner)
            ],
            axis=0,
        )

    owners = jnp.stack([b for k in range(4) for b in ((t ^ k), 7 - (t ^ k))]).astype(jnp.int32)

    def place_rows(pieces):
        width = pieces[0].shape[1]
        out = place([piece.reshape(2, part_rows, width) for piece in pieces], owners)
        return out.reshape(row_count, width)

    gain_one, gain_two = gains[0:1], gains[1:2]
    tile_four = lambda v: jnp.tile(v, (1, 4))
    normed_one, q_own, k_own, v_own = project(
        tokens, gain_one, own_slab, tile_four(cosine), tile_four(sine), own_block, own_lanes, True
    )
    att_own, log_own = attend_forward(
        own_blocks, own_low, own_high, q_own, k_own, v_own, key_index, own_row, own_start, own_block
    )
    q_part, k_part, v_part = project(
        normed_one, gain_one, shared_slab, tile_four(cosine), tile_four(sine), part_rows, part_lanes, False
    )
    att_part, log_part = attend_forward(
        part_blocks, part_low, part_high, q_part, k_part, v_part, key_index, part_row, part_start, part_rows
    )
    att_pieces = gather_tensor(att_own)
    att_shared = place_rows(gather_tensor(att_part))
    middle, normed_two = out_project(tokens, gain_two, att_pieces + [att_shared], out_weights)

    gate_up = dot_nn(normed_two, gate_rows)
    gate_act, up_act = gate_up[:, :hidden_count], gate_up[:, hidden_count:]
    sigmoid_gate = jax.nn.sigmoid(gate_act)
    silu_gate = gate_act * sigmoid_gate
    hidden = (silu_gate * up_act).astype(bf16)
    d_hidden = dot_nn(cotangent, ffn_rows)
    d_gate = (d_hidden * up_act * sigmoid_gate * (1.0 + gate_act * (1.0 - sigmoid_gate))).astype(bf16)
    d_up = (d_hidden * silu_gate).astype(bf16)
    d_gate_up = jnp.concatenate([d_gate, d_up], axis=1)
    d_normed_two = dot_nt(d_gate_up, gate_rows).astype(bf16)
    d_two = scatter_tensor([take_rows(d_normed_two, t ^ k) for k in range(4)])

    ffn_terms = dot_nt(hidden, ffn_rows).astype(bf16)
    ffn_mine = scatter_tensor([take_rows(ffn_terms, t ^ k) for k in range(4)])
    middle_mine = take_rows(middle, t)
    layer_mine = (middle_mine + ffn_mine).astype(bf16)
    layer_out = place_rows(gather_tensor(layer_mine))

    grad_ffn_out = dot_tn(cotangent, hidden).astype(bf16)
    grad_ffn_in = dot_tn(normed_two, d_gate_up).astype(bf16)

    factor_two = rms_factor(middle_mine)
    weighted = d_two * gain_two
    inner = jnp.mean(weighted * middle_mine, axis=-1, keepdims=True)
    d_middle = take_rows(cotangent, t).astype(f32) + (
        factor_two * weighted - middle_mine * factor_two**3 * inner
    )
    d_branch = d_middle.astype(bf16)
    d_att = [dot_nn(d_branch, weight).astype(bf16) for weight in out_weights]
    att_rows = [take_rows(piece, t) for piece in att_pieces] + [att_part]
    grad_out_terms = [dot_tn(d_branch, piece) for piece in att_rows]
    d_att_own = place_rows(exchange_tensor(d_att[:4]))

    dq_part, dk_part, dv_part = attend_backward(
        part_blocks, part_low, part_high, q_part, k_part, v_part, key_index, part_row, part_start,
        log_part, att_part, d_att[4], part_turn[0], part_turn[1], part_rows,
    )
    dq_own, dk_own, dv_own = attend_backward(
        own_blocks, own_low, own_high, q_own, k_own, v_own, key_index, own_row, own_start,
        log_own, att_own, d_att_own, own_turn[0], own_turn[1], own_block,
    )

    def slab_of(dq, dk, dv, cos, sin):
        first, second = dk[:, :32], dk[:, 32:]
        back_first = (first * cos + second * sin).astype(bf16)
        back_second = (second * cos - first * sin).astype(bf16)
        return jnp.concatenate(
            [dq[:, :96], back_first, dq[:, 96:], back_second, dv.astype(bf16)], axis=1
        )

    d_own = slab_of(dq_own, dk_own, dv_own, cosine, sine)
    dkv_part = jnp.concatenate([dk_part, dv_part], axis=1).astype(bf16)
    dkv_mine = sum(
        piece.astype(f32)
        for piece in exchange_tensor([take_rows(dkv_part, t ^ k) for k in range(4)])
    )
    d_shared = slab_of(
        dq_part, dkv_mine[:, :HD], dkv_mine[:, HD:], take_rows(cosine, t), take_rows(sine, t)
    )
    d_rows = exchange_tensor([take_rows(d_own, t ^ k) for k in range(4)]) + [d_shared]
    d_one = sum(dot_nt(piece, slab) for piece, slab in zip(d_rows, slabs + [shared_slab]))
    inputs = take_rows(tokens, t).astype(f32)
    factor_one = rms_factor(inputs)
    weighted = d_one * gain_one
    inner = jnp.mean(weighted * inputs, axis=-1, keepdims=True)
    grad_mine = (d_middle + factor_one * weighted - inputs * factor_one**3 * inner).astype(bf16)
    input_grad = place_rows(gather_tensor(grad_mine))

    shared_grad = dot_tn(take_rows(normed_one, t), d_shared).astype(bf16)
    shared_grad = dot_nt(shared_grad, one_hot(slab_order(t), SLAB))
    shared_grad = scatter_tensor([shared_grad[:, QUART * k : QUART * (k + 1)] for k in range(4)])
    own_grad = dot_tn(normed_one, d_own)
    attn_grad = jnp.concatenate([own_grad, shared_grad], axis=1).astype(bf16)
    out_shared_grad = dot_nt(grad_out_terms[4].astype(bf16), one_hot(out_order(t), HEADW))
    out_grad = scatter_tensor(
        [
            jnp.concatenate([grad_out_terms[k], out_shared_grad[:, 48 * k : 48 * (k + 1)]], axis=1)
            for k in range(4)
        ]
    ).astype(bf16)
    owned_ffn_out = jnp.transpose(scatter_dp(grad_ffn_out, False))
    owned_gate = scatter_dp(grad_ffn_in[:, :hidden_count], False)
    owned_up = scatter_dp(grad_ffn_in[:, hidden_count:], False)
    owned_out = scatter_dp(out_grad, True).astype(bf16)
    owned_attn = scatter_dp(attn_grad, True).astype(bf16)
    owned_ffn_in = jnp.stack([owned_gate, owned_up], axis=1)
    gain_term = jnp.sum(in_part.reshape(owned_rows, 2, hidden_count).astype(f32) * owned_ffn_in, axis=(1, 2))
    owned_all = gather_tensor(jnp.concatenate([owned_attn, owned_out], axis=1))
    attn_cols = jnp.concatenate(
        [own_columns(slot_head, t ^ k) for k in range(4)] + [shared_columns(slot_head, t ^ k) for k in range(4)]
    )
    attn_grads = jnp.concatenate(
        [piece[:, :SLAB] for piece in owned_all] + [piece[:, SLAB : SLAB + QUART] for piece in owned_all], axis=1
    )
    projection_grad = dot_nt(attn_grads, one_hot(attn_cols, NQ * HD + 2 * KV * HD))
    out_cols = jnp.concatenate(
        [own_out(slot_head, t ^ k) for k in range(4)] + [shared_out(slot_head, t ^ k) for k in range(4)]
    )
    out_grads = jnp.concatenate(
        [piece[:, SLAB + QUART : SLAB + QUART + HEADW] for piece in owned_all]
        + [piece[:, SLAB + QUART + HEADW :] for piece in owned_all],
        axis=1,
    )
    output_grad = dot_nt(one_hot(out_cols, NQ * HD), out_grads)
    gain_one_grad = jnp.sum(projection.astype(f32) * projection_grad, axis=1) / norm_gains[0]
    gain_two_grad = sum(gather_tensor(gain_term)) / norm_gains[1]
    gains_grad = jnp.stack([gain_one_grad, gain_two_grad], axis=0)

    matrix_rate = 0.5 * D ** (-0.5)
    rates = (matrix_rate, matrix_rate, 0.5 * OUT_FAN ** (-0.5), matrix_rate, 0.5 * FF ** (-0.5), 0.3)
    decays = (0.1, 0.1, 0.1, 0.1, 0.1, 0.0)
    reduced = (
        projection_grad[:, : NQ * HD], projection_grad[:, NQ * HD :], output_grad, owned_ffn_in, owned_ffn_out, gains_grad,
    )
    weights = (w_query, w_keyval, w_output, w_ffn_in, w_ffn_out, norm_gains)
    firsts = (first_query, first_keyval, first_output, first_ffn_in, first_ffn_out, first_gains)
    seconds = (second_query, second_keyval, second_output, second_ffn_in, second_ffn_out, second_gains)
    averages = (average_query, average_keyval, average_output, average_ffn_in, average_ffn_out, average_gains)
    updates = [
        adam_step(weights[m], firsts[m], seconds[m], averages[m], reduced[m], rates[m], decays[m])
        for m in range(6)
    ]
    return (layer_out, input_grad) + reduced + tuple(updates[m][part] for part in range(4) for m in range(6))


def solution(mesh):
    token, rows, columns = P("dp", None), P("dp", None), P(None, "dp")
    weight_specs = (rows, rows, columns, P("dp", None, "tensor"), P("tensor", "dp"), columns)
    in_specs = (token, token, P("dp", None), P("dp"), P()) + weight_specs * 4
    out_specs = (token, token) + weight_specs * 5
    return jax.shard_map(local, mesh=mesh, in_specs=in_specs, out_specs=out_specs, check_vma=False)
```

```python
import functools

import jax
import jax.numpy as jnp
import numpy as np
from jax import lax
from jax.experimental import pallas as pl
from jax.experimental.layout import Layout, with_layout_constraint
from jax.experimental.pallas import tpu as pltpu
from jax.sharding import PartitionSpec as P

D = 960
FF = 2560
NQ = 15
KV = 5
HD = 64
STEP = 10
GROUP = 3
OUT_FAN = 3
SLAB = 320
HEADW = GROUP * HD
WIDE = SLAB + HEADW
PIECE = 160
KEYS = 256

norm_eps = 1e-05
rope_base = 10000.0
beta_first = 0.5
beta_second = 0.5
adam_eps = 1e-08
average_keep = 0.5
bf16 = jnp.bfloat16
f32 = jnp.float32
VMEM_LIMIT = 48 * 1024 * 1024


def params(*semantics):
    return pltpu.CompilerParams(dimension_semantics=semantics, vmem_limit_bytes=VMEM_LIMIT)


def by_rows(x):
    return with_layout_constraint(x, Layout(major_to_minor=tuple(range(x.ndim))))


def swap(x, axis, offset):
    count = lax.axis_size(axis)
    return by_rows(lax.ppermute(by_rows(x), axis, [(i, i ^ offset) for i in range(count)]))


def dot_nn(a, b):
    return lax.dot_general(a, b, (((1,), (0,)), ((), ())), preferred_element_type=f32)


def dot_nt(a, b):
    return lax.dot_general(a, b, (((1,), (1,)), ((), ())), preferred_element_type=f32)


def dot_tn(a, b):
    return lax.dot_general(a, b, (((0,), (0,)), ((), ())), preferred_element_type=f32)


def kernel_call(body, scalars, arrays, *, out_shape, grid, in_specs, out_specs, scratch_shapes=(), name, far=False):
    single = not isinstance(out_shape, (list, tuple))
    shapes = [out_shape] if single else out_shape
    call = pl.pallas_call(
        body,
        out_shape=shapes,
        grid_spec=pltpu.PrefetchScalarGridSpec(
            num_scalar_prefetch=len(scalars),
        grid=grid,
        in_specs=in_specs,
        out_specs=[out_specs] if single else out_specs,
        scratch_shapes=scratch_shapes,
        ),
        compiler_params=params("arbitrary"),
        cost_estimate=pl.CostEstimate(flops=1000, bytes_accessed=1000, transcendentals=0),
        name=name,
    )
    if far:
        arrays = [pltpu.with_memory_space_constraint(x, pltpu.HBM) for x in arrays]
    outs = call(*scalars, *arrays)
    return outs[0] if single else outs


def after(values, *earlier):
    return lax.optimization_barrier((values, earlier))[0]


def turn(k):
    return (k & 1) * 2 + k // 2


def place_of(block, t):
    owner = jnp.minimum(block, 7 - block)
    return 2 * turn(owner ^ t) + (block > 3).astype(jnp.int32)


def place_body(index_ref, *refs):
    pieces, (slab_ref, out_ref, quarter_ref, rest_ref) = refs[:-4], refs[-4:]
    rows = slab_ref.shape[1]
    half = len(pieces) // 2
    for slot, piece in enumerate(pieces):
        at = index_ref[slot]
        slab_ref[at] = piece[:rows, : slab_ref.shape[2]]
        quarter_ref[at] = piece[:rows, WIDE:]
        rest_ref[at] = piece[rows:, :128]
        out = piece[:rows, SLAB:WIDE]

        @pl.when(at < half)
        def _():
            out_ref[at, :, :HEADW] = out

        @pl.when(at >= half)
        def _():
            out_ref[at - half, :, HEADW:] = out


def place(pieces, index, rows):
    height = pieces[0].shape[0]
    count = len(pieces)
    shapes = [(count, rows, 384), (count // 2, rows, 2 * HEADW), (count, rows, 128), (count, height - rows, 128)]
    return kernel_call(
        place_body,
        [index],
        pieces,
        out_shape=[jax.ShapeDtypeStruct(shape, pieces[0].dtype) for shape in shapes],
        grid=(1,),
        in_specs=[whole_spec(pieces[0].shape)] * count,
        out_specs=[whole_spec(shape) for shape in shapes],
        name="place",
        far=True,
    )


def assemble_body(t_ref, *refs):
    for k in range(4):
        at = pl.multiple_of((t_ref[0] ^ k) * 128, 128)
        refs[4][:, pl.ds(at, 128)] = refs[k][...]


def assemble(t, pieces):
    rows = pieces[0].shape[0]
    return kernel_call(
        assemble_body,
        [t],
        pieces,
        out_shape=jax.ShapeDtypeStruct((rows, WIDE), bf16),
        grid=(1,),
        in_specs=[whole_spec((rows, 128))] * 4,
        out_specs=whole_spec((rows, WIDE)),
        name="assemble",
    )


def reorder_body(t_ref, x_ref, out_ref):
    out_ref[...] = x_ref[...]


def own_order(x, t):
    width = x.shape[1]
    owner = lambda p, t_ref: t_ref[0] ^ turn(p // 2)
    return kernel_call(
        reorder_body,
        [t],
        [x],
        out_shape=jax.ShapeDtypeStruct(x.shape, x.dtype),
        grid=(8,),
        in_specs=[
                pl.BlockSpec(
                    (PIECE, width),
                    lambda p, t_ref: (jnp.where(p % 2 == 0, owner(p, t_ref), 7 - owner(p, t_ref)), 0),
                )
            ],
        out_specs=pl.BlockSpec((PIECE, width), lambda p, t_ref: (p, 0)),
        name="own_order",
    )


def natural_body(t_ref, *refs):
    block = pl.program_id(0)
    k = jnp.minimum(block, 7 - block) ^ t_ref[0]
    for which, piece in enumerate(refs[:-1]):

        @pl.when(k == which)
        def _():
            refs[-1][...] = piece[...]


def natural_order(pieces, t):
    width = pieces[0].shape[1]
    return kernel_call(
        natural_body,
        [t],
        [*pieces],
        out_shape=jax.ShapeDtypeStruct((8 * PIECE, width), pieces[0].dtype),
        grid=(8,),
        in_specs=[pl.BlockSpec((PIECE, width), lambda b, t_ref: (b // 4, 0))] * 4,
        out_specs=pl.BlockSpec((PIECE, width), lambda b, t_ref: (b, 0)),
        name="natural_order",
    )


def gather_one(x):
    if lax.axis_size("dp") != 8:
        return [x]
    return [x] + [swap(x, "dp", k) for k in (2, 4, 6)]


def gather_two(pieces):
    if len(pieces) == 1:
        return pieces
    return pieces + [swap(piece, "dp", 1) for piece in pieces]


def gather_end(pieces, rows):
    if len(pieces) == 1:
        both = lax.all_gather(pieces[0], "dp", axis=0)
        whole = both[:, :rows].reshape(D, WIDE + 128)
        out = whole[:, SLAB:WIDE]
        return whole[:, :384], jnp.concatenate([out[: D // 2], out[D // 2 :]], axis=1), whole[:, WIDE:], both[:, rows:, :128]
    me = lax.axis_index("dp")
    index = jnp.stack([me ^ k for k in (0, 2, 4, 6, 1, 3, 5, 7)]).astype(jnp.int32)
    slab, out, quarter, rest = place(pieces, index, rows)
    return slab.reshape(D, 384), out.reshape(D // 2, 2 * HEADW), quarter.reshape(D, 128), rest


def scatter_one(kept, sent):
    if sent is None:
        return (kept,)
    return kept, swap(sent, "dp", 1)


def scatter_two(halves):
    if len(halves) == 1:
        return halves
    mine, *sent = half_sums(lax.axis_index("dp").astype(jnp.int32).reshape(1), *halves)
    return [mine] + [swap(piece, "dp", 2 * (k + 1)) for k, piece in enumerate(sent)]


def scatter_end(quarters):
    if len(quarters) == 1:
        return lax.psum_scatter(quarters[0].astype(f32), "dp", scatter_dimension=0, tiled=True)
    return sum(quarter.astype(f32) for quarter in quarters)


def half_body(me_ref, kept_ref, came_ref, mine_ref, *sent_refs):
    at_z = me_ref[0] >> 1
    mine_ref[...] = kept_ref[at_z].astype(f32) + came_ref[at_z].astype(f32)
    for k, sent_ref in enumerate(sent_refs):
        at = at_z ^ (k + 1)
        sent_ref[...] = (kept_ref[at].astype(f32) + came_ref[at].astype(f32)).astype(bf16)


def half_sums(me, kept, came):
    count, rows, columns = kept.shape
    return kernel_call(
        half_body,
        [me],
        [kept, came],
        out_shape=[jax.ShapeDtypeStruct((rows, columns), f32)]
        + [jax.ShapeDtypeStruct((rows, columns), bf16)] * (count - 1),
        grid=(1,),
        in_specs=[whole_spec(kept.shape)] * 2,
        out_specs=[whole_spec((rows, columns))] * count,
        name="half_sums",
    )


def split_chunks(me_ref, chunks, kept_ref, sent_ref):
    at_y = (me_ref[0] & 1) == 0
    for z in range(len(chunks) // 2):
        even, odd = chunks[2 * z].astype(bf16), chunks[2 * z + 1].astype(bf16)
        kept_ref[z] = jnp.where(at_y, even, odd)
        sent_ref[z] = jnp.where(at_y, odd, even)


def gather_tensor(x):
    across = swap(x, "tensor", 2)
    beside = swap(x, "tensor", 1)
    return [x, beside, across, swap(across, "tensor", 1)]


def exchange_tensor(pieces):
    return [swap(piece, "tensor", k + 1) for k, piece in enumerate(pieces)]


def slab_target(group, group_ref):
    lane = lax.broadcasted_iota(jnp.int32, (1, SLAB), 1)
    second = lane >= 128
    value = lane >= 256
    within = jnp.where(second, lane - 128, lane)
    inside = (within & 31) + jnp.where(second, 32, 0)
    member = within >> 5
    query_at = jnp.full_like(lane, -1)
    for which in range(GROUP):
        query_at = jnp.where(member == which, head_of(group, which, group_ref) * HD + inside, query_at)
    query_at = jnp.where(value, -1, query_at)
    key_at = jnp.where(member == GROUP, group * HD + inside, -1)
    key_at = jnp.where(value, KV * HD + group * HD + lane - 256, key_at)
    return query_at, key_at


def head_of(group, which, group_ref):
    slot = group * GROUP + which
    head = jnp.int32(0)
    for h in range(NQ):
        head = jnp.where(group_ref[h] == slot, h, head)
    return head


def pick(width, index):
    rows = lax.broadcasted_iota(jnp.int32, (width, index.shape[1]), 0)
    return jnp.where(rows == index, 1.0, 0.0).astype(bf16)


def unit(count):
    rows = lax.broadcasted_iota(jnp.int32, (count, count), 0)
    return jnp.where(rows == lax.broadcasted_iota(jnp.int32, (count, count), 1), 1.0, 0.0).astype(bf16)


def prep_body(t_ref, index_ref, query_ref, keyval_ref, output_ref, gains_ref, out_ref):
    count = query_ref.shape[0]
    query, keyval = query_ref[...].astype(bf16), keyval_ref[...].astype(bf16)

    def block(group):
        query_at, key_at = slab_target(group, index_ref)
        picked = dot_nn(query, pick(NQ * HD, query_at)) + dot_nn(keyval, pick(2 * KV * HD, key_at))
        heads = [
            output_ref[pl.ds(pl.multiple_of(head_of(group, which, index_ref) * HD, HD), HD), :] for which in range(GROUP)
        ]
        turned = dot_nt(unit(count), jnp.concatenate(heads, axis=0).astype(bf16))
        return jnp.concatenate([picked, turned], axis=1)

    t = t_ref[0]
    shared = block(KV - 1)
    quarter = shared[:, :128]
    for k in (1, 2, 3):
        quarter = jnp.where(t == k, shared[:, 128 * k : 128 * (k + 1)], quarter)
    out_ref[:count, :] = jnp.concatenate([block(t), quarter], axis=1).astype(bf16)
    missing = out_ref.shape[0] - count
    gains = gains_ref[...]
    high = gains.astype(bf16).astype(f32)
    middle = (gains - high).astype(bf16).astype(f32)
    low = gains - high - middle
    rest = jnp.concatenate([high, middle, low, jnp.zeros((missing - 6, count), f32)], axis=0)
    rest = jnp.concatenate([rest, jnp.zeros((missing, WIDE + 128 - count), f32)], axis=1)
    out_ref[count:, :] = rest.astype(bf16)


def prepare(t, query_group, w_query, w_keyval, w_output, norm_gains, rows):
    return kernel_call(
        prep_body,
        [t, query_group],
        [w_query, w_keyval, w_output, norm_gains],
        out_shape=jax.ShapeDtypeStruct((rows, WIDE + 128), bf16),
        grid=(1,),
        in_specs=[whole_spec(x.shape) for x in (w_query, w_keyval, w_output, norm_gains)],
        out_specs=whole_spec((rows, WIDE + 128)),
        name="prepare",
        far=True,
    )


def pair_specs(width):
    owner = lambda p, t_ref: t_ref[0] ^ turn(p)
    return [
        pl.BlockSpec((PIECE, width), lambda p, t_ref: (owner(p, t_ref), 0)),
        pl.BlockSpec((PIECE, width), lambda p, t_ref: (7 - owner(p, t_ref), 0)),
    ]


def packed_specs():
    owner = lambda p, t_ref: t_ref[0] ^ turn(p)
    return [
        pl.BlockSpec((PIECE, 2 * HEADW), lambda p, t_ref: (owner(p, t_ref), 0)),
        pl.BlockSpec((PIECE, 2 * HEADW), lambda p, t_ref: (3 - owner(p, t_ref), 0)),
    ]


def unpack(low, high):
    return jnp.concatenate([low[:, :HEADW], high[:, HEADW:]], axis=0)


def pack(pair):
    rows = pair.shape[0] // 2
    return jnp.concatenate([pair[:rows], pair[rows:]], axis=1)


def split_heads(normed, w_ref, cosine, sine, q_ref, k_ref, v_ref):
    y = dot_nn(normed, w_ref[:, :SLAB])
    first, second = y[:, :128], y[:, 128:256]
    turned_first = first * cosine - second * sine
    turned_second = second * cosine + first * sine
    for head in range(GROUP + 1):
        columns = slice(32 * head, 32 * head + 32)
        both = jnp.concatenate([turned_first[:, columns], turned_second[:, columns]], axis=1)
        if head < GROUP:
            q_ref[head] = (both.astype(bf16).astype(f32) * HD ** (-0.5)).astype(bf16)
        else:
            k_ref[...] = both.astype(bf16)
    v_ref[...] = y[:, 256:].astype(bf16)


def proj_own_body(x_ref, gain_ref, w_ref, cos_ref, sin_ref, normed_ref, q_ref, k_ref, v_ref):
    x = x_ref[...].astype(f32)
    factor = lax.rsqrt(jnp.mean(x * x, axis=-1, keepdims=True) + norm_eps)
    normed = (x * factor * gain_ref[...]).astype(bf16)
    normed_ref[...] = normed
    split_heads(normed, w_ref, cos_ref[...], sin_ref[...], q_ref, k_ref, v_ref)


def proj_shared_body(normed_ref, w_ref, cos_ref, sin_ref, q_ref, k_ref, v_ref):
    split_heads(normed_ref[...], w_ref, cos_ref[...], sin_ref[...], q_ref, k_ref, v_ref)


def project(x, gain, weight, cosine, sine):
    rows = x.shape[0]
    step = 2 * PIECE
    by_step = lambda width: pl.BlockSpec((step, width), lambda i: (i, 0))
    narrow = (jax.ShapeDtypeStruct((rows, HD), bf16), by_step(HD))
    stack = (jax.ShapeDtypeStruct((GROUP, rows, HD), bf16), pl.BlockSpec((GROUP, step, HD), lambda i: (0, i, 0)))
    outs = [stack, narrow, narrow]
    if gain is not None:
        outs = [(jax.ShapeDtypeStruct(x.shape, bf16), by_step(D))] + outs
    gains = [] if gain is None else [gain]
    return kernel_call(
        proj_shared_body if gain is None else proj_own_body,
        [],
        [x, *gains, weight, cosine, sine],
        grid=(rows // step,),
        out_shape=[shape for shape, _ in outs],
        in_specs=[by_step(D)]
        + [whole_spec((1, D))] * len(gains)
        + [whole_spec(weight.shape), by_step(128), by_step(128)],
        out_specs=[spec for _, spec in outs],
        name="project",
    )


def lanes_of(rows):
    return -(-GROUP * rows // 128) * 128


def start_of(row, length_ref):
    end_one = length_ref[0]
    end_two = end_one + length_ref[1]
    return jnp.where(row >= end_two, end_two, jnp.where(row >= end_one, end_one, 0))


def lane_rows(block, rows, length_ref):
    lane = lax.broadcasted_iota(jnp.int32, (1, lanes_of(rows)), 1)
    head = sum((lane >= h * rows).astype(jnp.int32) for h in range(1, GROUP + 1))
    row = jnp.where(head < GROUP, block * rows + lane - head * rows, 1 << 20)
    return row, jnp.where(head < GROUP, start_of(row, length_ref), 1 << 20)


def key_range(block, rows, length_ref):
    first = start_of(block * rows, length_ref) // KEYS
    return first, (block * rows + rows + KEYS - 1) // KEYS


def key_mask(valid, at, row, start):
    index = at + lax.broadcasted_iota(jnp.int32, (KEYS, row.shape[1]), 0)
    return ((index >= start) & (index <= row) & (valid == 1)) | (index == row)


def fill(stacked, lanes):
    parts = [stacked[head] for head in range(GROUP)]
    missing = lanes - GROUP * stacked[0].shape[0]
    if missing:
        parts.append(jnp.zeros((missing, HD), bf16))
    return jnp.concatenate(parts, axis=0)


def forward_body(length_ref, block_ref, q_ref, k_ref, v_ref, valid_ref, out_ref, log_ref, acc):
    rows = q_ref.shape[1]
    lanes = acc.shape[1]
    block = block_ref[pl.program_id(0)]
    q = fill(q_ref[...], lanes)
    row, start = lane_rows(block, rows, length_ref)
    acc[...] = jnp.zeros_like(acc)

    def visit(j, carry):
        peak, total = carry
        at = pl.multiple_of(j * KEYS, KEYS)
        here = pl.ds(at, KEYS)
        scores = dot_nt(k_ref[here, :], q)
        scores = jnp.where(key_mask(valid_ref[here, :1], at, row, start), scores, -1e30)
        new_peak = jnp.maximum(peak, jnp.max(scores, axis=0, keepdims=True))
        exponent = jnp.exp(scores - new_peak)
        shrink = jnp.exp(peak - new_peak)
        total = total * shrink + jnp.sum(exponent, axis=0, keepdims=True)
        acc[...] = acc[...] * shrink + dot_tn(v_ref[here, :], exponent.astype(bf16))
        return new_peak, total

    low, high = key_range(block, rows, length_ref)
    peak, total = lax.fori_loop(
        low, high, visit, (jnp.full((1, lanes), -1e30, f32), jnp.zeros((1, lanes), f32))
    )
    log_ref[0] = peak + jnp.log(total)
    attended = jnp.transpose(acc[...] / total)
    attended = jnp.concatenate(
        [attended[head * rows : (head + 1) * rows] for head in range(GROUP)], axis=1
    ).astype(bf16)
    half = out_ref.shape[0]
    chunk = min(rows, 128) if half > rows else rows
    for part in range(rows // chunk):
        at = pl.program_id(0) * rows + part * chunk
        piece = attended[part * chunk : (part + 1) * chunk]

        @pl.when(at < half)
        def _():
            out_ref[pl.ds(pl.multiple_of(at, chunk), chunk), :HEADW] = piece

        @pl.when(at >= half)
        def _():
            out_ref[pl.ds(pl.multiple_of(at - half, chunk), chunk), HEADW:] = piece


def attend_forward(lengths, blocks, size, q, k, v, valid):
    count, rows = blocks.shape[0], k.shape[0]
    lanes = lanes_of(size)
    return kernel_call(
        forward_body,
        [lengths, blocks],
        [q, k, v, valid],
        out_shape=[
            jax.ShapeDtypeStruct((count * size // 2, 2 * HEADW), bf16),
            jax.ShapeDtypeStruct((count, 1, lanes), f32),
        ],
        grid=(count,),
        in_specs=[
                pl.BlockSpec((GROUP, size, HD), lambda i, lengths, blocks: (0, blocks[i], 0)),
                whole_spec((rows, HD)), whole_spec((rows, HD)), whole_spec((rows, 128)),
            ],
        out_specs=[
                whole_spec((count * size // 2, 2 * HEADW)),
                pl.BlockSpec((1, 1, lanes), lambda i, *scalars: (i, 0, 0)),
            ],
        scratch_shapes=[pltpu.VMEM((HD, lanes), f32)],
        name="attend_forward",
    )


def backward_block(block, rows, length_ref, q, k_ref, v_ref, valid_ref, logs, attended, upstream, cosine, sine, dk, dv, acc):
    lanes = q.shape[0]
    row, start = lane_rows(block, rows, length_ref)
    heads = lambda wide: fill([wide[:, h * HD : (h + 1) * HD] for h in range(GROUP)], lanes)
    up = heads(upstream)
    both = up.astype(f32) * heads(attended).astype(f32)
    both_high = both.astype(bf16)
    both_low = (both - both_high.astype(f32)).astype(bf16)
    ones = jnp.ones((8, HD), bf16)
    inner = (dot_nt(ones, both_high) + dot_nt(ones, both_low))[:1]
    acc[...] = jnp.zeros_like(acc)

    def visit(j, carry):
        at = pl.multiple_of(j * KEYS, KEYS)
        here = pl.ds(at, KEYS)
        scores = dot_nt(k_ref[here, :], q)
        scores = jnp.where(key_mask(valid_ref[here, :1], at, row, start), scores, -1e30)
        probs = jnp.exp(scores - logs)
        d_probs = dot_nt(v_ref[here, :], up)
        d_scores = (probs * (d_probs - inner)).astype(bf16)
        dv[here, :] += dot_nn(probs.astype(bf16), up)
        dk[here, :] += dot_nn(d_scores, q)
        acc[...] += dot_tn(k_ref[here, :], d_scores)
        return carry

    low, high = key_range(block, rows, length_ref)
    lax.fori_loop(low, high, visit, 0)
    turned = jnp.transpose(acc[...] * HD ** (-0.5))
    first = jnp.concatenate([turned[h * rows : (h + 1) * rows, :32] for h in range(GROUP)], axis=1)
    second = jnp.concatenate([turned[h * rows : (h + 1) * rows, 32:] for h in range(GROUP)], axis=1)
    cosine, sine = cosine[:, :96], sine[:, :96]
    return first * cosine + second * sine, second * cosine - first * sine


def turn_back(dk, cosine, sine):
    first, second = dk[:, :32], dk[:, 32:]
    cosine, sine = cosine[:, :32], sine[:, :32]
    return first * cosine + second * sine, second * cosine - first * sine


def rows_at(block):
    return pl.ds(pl.multiple_of(block * PIECE, PIECE), PIECE)


def attended_rows(out_ref, at, rows):
    half = out_ref.shape[0]
    parts = []
    for part in range(rows // 128):
        here = at + part * 128
        low = pl.multiple_of(jnp.where(here < half, here, here - half), 128)
        both = out_ref[pl.ds(low, 128), :]
        parts.append(jnp.where(here < half, both[:, :HEADW], both[:, HEADW:]))
    return jnp.concatenate(parts, axis=0)


def backward_own_body(
    t_ref, length_ref, q_ref, k_ref, v_ref, valid_ref, log_ref, out_ref, up_0, up_1, up_2, up_3, cos_ref, sin_ref, shared_ref,
    slab_ref, *rest
):
    send_refs, mine_ref, (dk, dv, acc, upstream) = rest[:3], rest[3], rest[4:]
    rows = q_ref.shape[1]
    step = pl.program_id(0)
    t = t_ref[0]
    block = pl.num_programs(0) - 1 - step

    @pl.when(step == 0)
    def _():
        dk[...] = jnp.zeros_like(dk)
        dv[...] = jnp.zeros_like(dv)
        for k, piece in enumerate((up_0, up_1, up_2, up_3)):
            upstream[rows_at(t ^ k), :] = piece[:, :HEADW]
            upstream[rows_at(7 - (t ^ k)), :] = piece[:, HEADW:]

    cosine, sine = cos_ref[...], sin_ref[...]
    here = pl.ds(pl.multiple_of(block * rows, rows), rows)
    q = fill(q_ref[...], acc.shape[1])
    first, second = backward_block(
        block, rows, length_ref, q, k_ref, v_ref, valid_ref, log_ref[0], attended_rows(out_ref, block * rows, rows),
        upstream[here, :], cosine, sine, dk, dv, acc,
    )
    key_first, key_second = turn_back(dk[here, :], cosine, sine)
    slab_ref[here, :] = jnp.concatenate([first, key_first, second, key_second, dv[here, :]], axis=1).astype(bf16)

    @pl.when(step == pl.num_programs(0) - 1)
    def _():
        for half, owner in enumerate((t, 7 - t)):
            mine_ref[half * PIECE : (half + 1) * PIECE, :] = slab_ref[rows_at(owner), :]
        for k, target in enumerate(send_refs):
            for half, owner in enumerate((t ^ (k + 1), 7 - (t ^ (k + 1)))):
                own, shared = slab_ref[rows_at(owner), :], shared_ref[rows_at(owner), :]
                target[half * PIECE : (half + 1) * PIECE, :] = jnp.concatenate(
                    [own, shared[:, 96:128], shared[:, 224:256], shared[:, 256:], jnp.zeros((PIECE, 64), bf16)], axis=1
                )


def attend_backward_own(t, lengths, q, k, v, valid, logs, attended, pieces, cosine, sine, shared):
    rows = k.shape[0]
    size = KEYS
    count, lanes = rows // size, lanes_of(size)
    at = lambda i: count - 1 - i
    by_step = lambda width: pl.BlockSpec((size, width), lambda i, *scalars: (at(i), 0))
    return kernel_call(
        backward_own_body,
        [t, lengths],
        [q, k, v, valid, logs, attended, *pieces, cosine, sine, shared],
        out_shape=[jax.ShapeDtypeStruct((rows, SLAB), bf16)]
        + [jax.ShapeDtypeStruct((2 * PIECE, WIDE), bf16)] * 3
        + [jax.ShapeDtypeStruct((2 * PIECE, SLAB), bf16)],
        grid=(count,),
        in_specs=[
                pl.BlockSpec((GROUP, size, HD), lambda i, *scalars: (0, at(i), 0)),
                whole_spec((rows, HD)), whole_spec((rows, HD)), whole_spec((rows, 128)),
                pl.BlockSpec((1, 1, lanes), lambda i, *scalars: (at(i), 0, 0)), whole_spec((rows // 2, 2 * HEADW)),
            ]
            + [whole_spec((PIECE, 2 * HEADW))] * 4
            + [by_step(128)] * 2
            + [whole_spec((rows, SLAB))],
        out_specs=[whole_spec((rows, SLAB))] + [whole_spec((2 * PIECE, WIDE))] * 3 + [whole_spec((2 * PIECE, SLAB))],
        scratch_shapes=[
                pltpu.VMEM((rows, HD), f32), pltpu.VMEM((rows, HD), f32), pltpu.VMEM((HD, lanes), f32),
                pltpu.VMEM((rows, HEADW), bf16),
            ],
        name="attend_backward_own",
    )


def backward_shared_body(
    t_ref, length_ref, block_ref, q_ref, k_ref, v_ref, valid_ref, log_ref, out_ref, up_ref, cos_ref, sin_ref, cos_all, sin_all,
    slab_ref, mine_ref, dk, dv, acc
):
    step = pl.program_id(0)
    t = t_ref[0]
    block = block_ref[step]

    @pl.when(step == 0)
    def _():
        dk[...] = jnp.zeros_like(dk)
        dv[...] = jnp.zeros_like(dv)
        slab_ref[...] = jnp.zeros_like(slab_ref)

    half = lambda ref: jnp.where(step == 0, ref[:, :HEADW], ref[:, HEADW:])
    first, second = backward_block(
        block, PIECE, length_ref, fill(q_ref[...], acc.shape[1]), k_ref, v_ref, valid_ref, log_ref[0], half(out_ref), half(up_ref),
        cos_ref[...], sin_ref[...], dk, dv, acc,
    )
    slab_ref[rows_at(block), :96] = first.astype(bf16)
    slab_ref[rows_at(block), 128:224] = second.astype(bf16)

    @pl.when(step == pl.num_programs(0) - 1)
    def _():
        key_first, key_second = turn_back(dk[...], cos_all[...], sin_all[...])
        slab_ref[:, 96:128] = key_first.astype(bf16)
        slab_ref[:, 224:256] = key_second.astype(bf16)
        slab_ref[:, 256:] = dv[...].astype(bf16)
        mine_ref[:PIECE, :] = slab_ref[rows_at(t), :]
        mine_ref[PIECE:, :] = slab_ref[rows_at(7 - t), :]


def attend_backward_shared(t, lengths, blocks, q, k, v, valid, logs, attended, upstream, cosine, sine):
    rows = k.shape[0]
    lanes = lanes_of(PIECE)
    mine = whole_spec((PIECE, 2 * HEADW))
    natural = pl.BlockSpec((PIECE, 128), lambda i, t_ref, length_ref, block_ref: (block_ref[i], 0))
    return kernel_call(
        backward_shared_body,
        [t, lengths, blocks],
        [q, k, v, valid, logs, attended, upstream, cosine, sine, cosine, sine],
        out_shape=[jax.ShapeDtypeStruct((rows, SLAB), bf16), jax.ShapeDtypeStruct((2 * PIECE, SLAB), bf16)],
        grid=(2,),
        in_specs=[
                pl.BlockSpec((GROUP, PIECE, HD), lambda i, t_ref, length_ref, block_ref: (0, block_ref[i], 0)),
                whole_spec((rows, HD)), whole_spec((rows, HD)), whole_spec((rows, 128)),
                pl.BlockSpec((1, 1, lanes), lambda i, *scalars: (i, 0, 0)), mine, mine,
            ]
            + [natural] * 2
            + [whole_spec((rows, 128))] * 2,
        out_specs=[whole_spec((rows, SLAB)), whole_spec((2 * PIECE, SLAB))],
        scratch_shapes=[pltpu.VMEM((rows, HD), f32), pltpu.VMEM((rows, HD), f32), pltpu.VMEM((HD, lanes), f32)],
        name="attend_backward_shared",
    )


def whole_spec(shape):
    return pl.BlockSpec(shape, lambda i, *scalars: (0,) * len(shape))


def out_weight(weight):
    if weight.shape[0] == D:
        return weight[:, SLAB:]
    return jnp.concatenate([weight[:, :HEADW], weight[:, HEADW:]], axis=0)


def out_body(t_ref, x_a, x_b, gain_ref, *refs):
    owns, shares, weights = refs[:8], refs[8:12], refs[12:17]
    low_ref, high_ref, mine_ref, normed_ref, w_out = refs[17:]
    step = pl.program_id(0)

    @pl.when(step == 0)
    def _():
        for k, weight in enumerate(weights):
            w_out[k] = out_weight(weight)

    middle = jnp.concatenate([x_a[...], x_b[...]], axis=0).astype(f32)
    for k in range(4):
        middle = middle + dot_nt(unpack(owns[2 * k][...], owns[2 * k + 1][...]), w_out[k])
    share = jnp.where(
        step == 0, shares[0][...],
        jnp.where(step == 1, shares[2][...], jnp.where(step == 2, shares[1][...], shares[3][...])),
    )
    middle = middle + dot_nt(unpack(share, share), w_out[4])
    low_ref[...] = middle[:PIECE]
    high_ref[...] = middle[PIECE:]
    factor = lax.rsqrt(jnp.mean(middle * middle, axis=-1, keepdims=True) + norm_eps)
    normed_ref[...] = (middle * factor * gain_ref[...]).astype(bf16)

    @pl.when(step == 0)
    def _():
        mine_ref[...] = middle


def out_project(t, x, gain, owns, shares, weights):
    rows = x.shape[0]
    owner = lambda p, t_ref: t_ref[0] ^ turn(p)
    half = jax.ShapeDtypeStruct((rows // 2, D), f32)
    return kernel_call(
        out_body,
        [t],
        [x, x, gain, *[piece for piece in owns for _ in range(2)], *shares, *weights],
        out_shape=[half, half, jax.ShapeDtypeStruct((2 * PIECE, D), f32), jax.ShapeDtypeStruct(x.shape, bf16)],
        grid=(4,),
        in_specs=pair_specs(D)
            + [whole_spec((1, D))]
            + packed_specs() * 4
            + [whole_spec((PIECE, 2 * HEADW))] * 4
            + [whole_spec(weight.shape) for weight in weights],
        out_specs=[
                pl.BlockSpec((PIECE, D), lambda p, t_ref: (owner(p, t_ref), 0)),
                pl.BlockSpec((PIECE, D), lambda p, t_ref: (3 - owner(p, t_ref), 0)),
                whole_spec((2 * PIECE, D)),
                pl.BlockSpec((2 * PIECE, D), lambda p, t_ref: (p, 0)),
            ],
        scratch_shapes=[pltpu.VMEM((5, D, HEADW), bf16)],
        name="out_project",
    )


def feed_body(t_ref, normed_ref, cot_ref, w_ref, hidden_ref, d_ref, kept_ref, sent_ref, low_ref, high_ref):
    step = pl.program_id(0)
    width = hidden_ref.shape[1]
    w_gate, w_up, w_out = (w_ref[:, width * part : width * (part + 1)] for part in range(3))
    normed = normed_ref[...]
    gate = dot_nn(normed, w_gate)
    up = dot_nn(normed, w_up)
    d_hidden = dot_nn(cot_ref[...], w_out)
    sigmoid = 1.0 / (1.0 + jnp.exp(-gate))
    silu = gate * sigmoid
    hidden = (silu * up).astype(bf16)
    d_gate = (d_hidden * up * sigmoid * (1.0 + gate * (1.0 - sigmoid))).astype(bf16)
    d_up = (d_hidden * silu).astype(bf16)
    hidden_ref[...] = hidden
    d_ref[:, :width] = d_gate
    d_ref[:, width:] = d_up
    back = (dot_nt(d_gate, w_gate) + dot_nt(d_up, w_up)).astype(bf16)

    @pl.when(step < 2)
    def _():
        sent_ref[0] = back

    @pl.when(step >= 2)
    def _():
        kept_ref[0] = back

    terms = dot_nt(hidden, w_out).astype(bf16)
    low_ref[...] = terms[:PIECE]
    high_ref[...] = terms[PIECE:]


def feed_forward(t, normed, cotangent, weights):
    rows, width = normed.shape[0], weights.shape[1] // 3
    at = lambda i: (i + 2) % 4
    owner = lambda i, t_ref: t_ref[0] ^ turn(at(i))
    by_step = lambda columns: pl.BlockSpec((2 * PIECE, columns), lambda i, t_ref: (at(i), 0))
    pair = jax.ShapeDtypeStruct((2, 2 * PIECE, D), bf16)
    half = jax.ShapeDtypeStruct((rows // 2, D), bf16)
    return kernel_call(
        feed_body,
        [t],
        [normed, cotangent, weights],
        out_shape=[
            jax.ShapeDtypeStruct((rows, width), bf16), jax.ShapeDtypeStruct((rows, 2 * width), bf16), pair, pair, half, half,
        ],
        grid=(4,),
        in_specs=[by_step(D), by_step(D), whole_spec(weights.shape)],
        out_specs=[
                by_step(width), by_step(2 * width),
                pl.BlockSpec((1, 2 * PIECE, D), lambda i, t_ref: (jnp.maximum(i - 2, 0), 0, 0)),
                pl.BlockSpec((1, 2 * PIECE, D), lambda i, t_ref: (jnp.minimum(i, 1), 0, 0)),
                pl.BlockSpec((PIECE, D), lambda i, t_ref: (owner(i, t_ref), 0)),
                pl.BlockSpec((PIECE, D), lambda i, t_ref: (3 - owner(i, t_ref), 0)),
            ],
        name="feed_forward",
    )


def near_far_body(kept_ref, came_ref, near_ref, far_ref):
    near_ref[...] = kept_ref[0].astype(f32) + came_ref[0].astype(f32)
    far_ref[...] = (kept_ref[1].astype(f32) + came_ref[1].astype(f32)).astype(bf16)


def near_far(kept, came):
    shape = kept.shape[1:]
    return kernel_call(
        near_far_body,
        [],
        [kept, came],
        grid=(1,),
        out_shape=[jax.ShapeDtypeStruct(shape, f32), jax.ShapeDtypeStruct(shape, bf16)],
        in_specs=[whole_spec(kept.shape)] * 2,
        out_specs=[whole_spec(shape)] * 2,
        name="near_far",
    )


def norm_back(values, gain, upstream):
    factor = lax.rsqrt(jnp.mean(values * values, axis=-1, keepdims=True) + norm_eps)
    weighted = upstream * gain
    inner = jnp.mean(weighted * values, axis=-1, keepdims=True)
    return factor * weighted - values * factor**3 * inner


def middle_body(near_ref, far_ref, middle_ref, up_ref, gain_ref, *refs):
    weights, d_middle_ref, d_branch_ref, d_refs = refs[:5], refs[5], refs[6], refs[7:]
    upstream = near_ref[...] + far_ref[...].astype(f32)
    d_middle = up_ref[...].astype(f32) + norm_back(middle_ref[...], gain_ref[...], upstream)
    d_middle_ref[...] = d_middle
    d_branch = d_middle.astype(bf16)
    d_branch_ref[...] = d_branch
    for weight, d_ref in zip(weights, d_refs):
        d_ref[...] = pack(dot_nn(d_branch, out_weight(weight)).astype(bf16))


def middle_backward(near, far, middle, upstream, gain, weights):
    rows = near.shape[0]
    top = whole_spec((rows, D))
    return kernel_call(
        middle_body,
        [],
        [near, far, middle, upstream, gain, *weights],
        grid=(1,),
        out_shape=[jax.ShapeDtypeStruct((rows, D), f32), jax.ShapeDtypeStruct((rows, D), bf16)]
        + [jax.ShapeDtypeStruct((rows // 2, 2 * HEADW), bf16)] * 5,
        in_specs=[top] * 4 + [whole_spec((1, D))] + [whole_spec(weight.shape) for weight in weights],
        out_specs=[top, top] + [whole_spec((rows // 2, 2 * HEADW))] * 5,
        name="middle_backward",
    )


def early_body(t_ref, d_branch_ref, *refs):
    owns, share_ref, normed_ref, slab_ref, kept_ref, sent_ref, block = refs[:8], *refs[8:]
    t = t_ref[0]
    d_branch = d_branch_ref[...]
    share = share_ref[...]
    block[...] = jnp.concatenate(
        [dot_tn(normed_ref[...], slab_ref[...]), dot_tn(d_branch, unpack(share, share))], axis=1
    ).astype(bf16)
    for k in range(4):
        target = (kept_ref, sent_ref)[k & 1]
        piece = unpack(owns[2 * k][...], owns[2 * k + 1][...])
        at = pl.multiple_of((t ^ k) * 128, 128)
        target[k // 2, :, :128] = block[:, pl.ds(at, 128)]
        target[k // 2, :, 128:SLAB] = dot_tn(d_branch, piece).astype(bf16)
        target[k // 2, :, SLAB:] = jnp.zeros((D, 64), bf16)


def early_grads(t, d_branch, owns, share, normed, slab):
    rows = d_branch.shape[0]
    pair = jax.ShapeDtypeStruct((2, D, 384), bf16)
    return kernel_call(
        early_body,
        [t],
        [d_branch, *[piece for piece in owns for _ in range(2)], share, normed, slab],
        out_shape=[pair, pair],
        grid=(1,),
        in_specs=[whole_spec((rows, D))]
        + packed_specs() * 4
        + [whole_spec((PIECE, 2 * HEADW)), whole_spec(normed.shape), whole_spec(slab.shape)],
        out_specs=[whole_spec((2, D, 384))] * 2,
        scratch_shapes=[pltpu.VMEM((D, WIDE), bf16)],
        name="early_grads",
    )


def attn_grad_body(me_ref, normed_ref, slab_ref, near_ref, far_ref, kept_ref, sent_ref):
    early = near_ref[...] + far_ref[...].astype(f32)
    grad = dot_tn(normed_ref[...], slab_ref[...])
    whole = jnp.concatenate([early, grad, jnp.zeros((D, 64), f32)], axis=1)
    rows = kept_ref.shape[1]
    split_chunks(me_ref, [whole[rows * j : rows * (j + 1)] for j in range(D // rows)], kept_ref, sent_ref)


def attn_grads(me, normed, slab, near, far):
    half = jax.ShapeDtypeStruct((4, D // 8, 768), bf16)
    arrays = [normed, slab, near, far]
    return kernel_call(
        attn_grad_body,
        [me],
        arrays,
        out_shape=[half, half],
        grid=(1,),
        in_specs=[whole_spec(x.shape) for x in arrays],
        out_specs=[whole_spec(half.shape)] * 2,
        name="attn_grads",
    )


def input_body(t_ref, x_a, x_b, d_middle_ref, gain_ref, own_ref, shared_ref, *refs):
    came_refs, slabs, shared_slab, out_ref = refs[:3], refs[3:7], refs[7], refs[8]
    upstream = dot_nt(own_ref[...], slabs[0][0, :, :SLAB])
    for piece, slab in zip(came_refs, slabs[1:4]):
        upstream = upstream + dot_nt(piece[:, :SLAB], slab[0, :, :SLAB])
    shared = shared_ref[...]
    key_value = jnp.concatenate([shared[:, 96:128], shared[:, 224:256], shared[:, 256:]], axis=1).astype(f32)
    for piece in came_refs:
        key_value = key_value + piece[:, SLAB : SLAB + 2 * HD].astype(f32)
    key_value = key_value.astype(bf16)
    shared = jnp.concatenate(
        [shared[:, :96], key_value[:, :32], shared[:, 128:224], key_value[:, 32:64], key_value[:, 64:]], axis=1
    )
    upstream = upstream + dot_nt(shared, shared_slab[:, :SLAB])
    x = jnp.concatenate([x_a[...], x_b[...]], axis=0).astype(f32)
    out_ref[...] = (d_middle_ref[...] + norm_back(x, gain_ref[...], upstream)).astype(bf16)


def input_backward(t, x, d_middle, gain, own, shared, came, slabs, shared_block):
    rows = 2 * PIECE
    of_owner = [
        pl.BlockSpec((1, D, 384), functools.partial(lambda k, i, t_ref: (t_ref[0] ^ k, 0, 0), k)) for k in range(4)
    ]
    return kernel_call(
        input_body,
        [t],
        [x, x, d_middle, gain, own, shared, *came, *[slabs] * 4, shared_block],
        out_shape=jax.ShapeDtypeStruct((rows, D), bf16),
        grid=(1,),
        in_specs=pair_specs(D)
        + [whole_spec((rows, D)), whole_spec((1, D))]
        + [whole_spec((rows, SLAB))] * 2
        + [whole_spec((rows, WIDE))] * 3
        + of_owner
        + [pl.BlockSpec((D, 384), lambda i, *scalars: (0, 0))],
        out_specs=whole_spec((rows, D)),
        name="input_backward",
    )


def one_hot(index, size):
    return (jnp.arange(size, dtype=jnp.int32)[:, None] == index[None, :]).astype(bf16)


def adam_step(weight, first, second, average, gradient, step_rate, decay_rate):
    first_new = beta_first * first + (1.0 - beta_first) * gradient
    second_new = beta_second * second + (1.0 - beta_second) * gradient * gradient
    corrected_first = first_new / (1.0 - beta_first**STEP)
    corrected_second = second_new / (1.0 - beta_second**STEP)
    weight_new = weight - step_rate * (
        corrected_first / (jnp.sqrt(corrected_second) + adam_eps) + decay_rate * weight
    )
    average_new = average_keep * average + (1.0 - average_keep) * weight_new
    return (first_new, second_new, weight_new, average_new)


def slab_columns(slot_head, group):
    heads = lax.dynamic_slice(slot_head, (group * GROUP,), (GROUP,))
    bases = jnp.concatenate([heads * HD, (NQ * HD + group * HD)[None]])
    half = (bases[:, None] + jnp.arange(32, dtype=jnp.int32)[None, :]).reshape(-1)
    value = NQ * HD + KV * HD + group * HD + jnp.arange(HD, dtype=jnp.int32)
    return jnp.concatenate([half, half + 32, value])


def out_rows(slot_head, group):
    heads = lax.dynamic_slice(slot_head, (group * GROUP,), (GROUP,))
    return (heads[:, None] * HD + jnp.arange(HD, dtype=jnp.int32)[None, :]).reshape(-1)


def local(
    tokens, cotangent, lengths, valid, query_group,
    w_query, w_keyval, w_output, w_ffn_in, w_ffn_out, norm_gains,
    first_query, first_keyval, first_output, first_ffn_in, first_ffn_out, first_gains,
    second_query, second_keyval, second_output, second_ffn_in, second_ffn_out, second_gains,
    average_query, average_keyval, average_output, average_ffn_in, average_ffn_out, average_gains,
):
    t = lax.axis_index("tensor").astype(jnp.int32)
    t_array = t.reshape(1)
    row_count = tokens.shape[0]
    owned_rows = w_query.shape[0]
    hidden_count = w_ffn_out.shape[0]
    last = jnp.int32(KV - 1)
    slots = jnp.arange(NQ, dtype=jnp.int32)
    slot_head = jnp.sum(
        jnp.where(query_group[None, :] == slots[:, None], slots[None, :], 0), axis=1
    ).astype(jnp.int32)

    me = lax.axis_index("dp").astype(jnp.int32).reshape(1)
    small = lax.axis_size("dp") == 8
    rest_rows = 8 if owned_rows % 8 == 0 else 17
    own_part = prepare(t_array, query_group, w_query, w_keyval, w_output, norm_gains, owned_rows + rest_rows)
    own_one = gather_one(own_part)
    w_in_now, w_out_now = after((w_ffn_in, w_ffn_out), own_part)
    feed_part = jnp.concatenate(
        [w_in_now[:, 0].astype(bf16), w_in_now[:, 1].astype(bf16), jnp.transpose(w_out_now).astype(bf16)], axis=1
    )
    feed_all = lax.all_gather(feed_part, "dp", axis=0, tiled=True)

    length_row = lengths[0]
    seq_ends = jnp.cumsum(length_row)
    valid, cotangent, seq_ends = after((valid, cotangent, seq_ends), feed_part)
    row_index = jnp.arange(row_count, dtype=jnp.int32)
    row_start = jnp.where(
        row_index >= seq_ends[1], seq_ends[1], jnp.where(row_index >= seq_ends[0], seq_ends[0], 0)
    )
    position = (row_index - row_start).astype(f32)
    frequency = rope_base ** (-jnp.arange(0, HD, 2, dtype=f32) / HD)
    angles = position[:, None] * jnp.tile(frequency, 4)[None, :]
    cosine, sine = jnp.cos(angles), jnp.sin(angles)
    valid_wide = jnp.broadcast_to(valid[:, None], (row_count, 128))
    own_cotangent = own_order(cotangent, t_array)
    tables = (cosine, sine, valid_wide, own_cotangent)

    own_two = gather_two(after(own_one, tables))
    slab_own, out_own, quarter, rest = gather_end(own_two, owned_rows)
    quarters = gather_tensor(quarter)
    parts = jnp.swapaxes(rest[:, :6, :owned_rows].astype(f32), 0, 1).reshape(6, D)
    gains = parts[0:2] + parts[2:4] + parts[4:6]
    gain_one, gain_two = gains[0:1], gains[1:2]

    normed_one, q_own, k_own, v_own = project(tokens, gain_one, slab_own, cosine, sine)
    out_owns = gather_tensor(after(out_own, normed_one))
    slabs = lax.all_gather(slab_own, "tensor", axis=0)
    blocks = jnp.arange(row_count // KEYS, dtype=jnp.int32)
    part_blocks = jnp.stack([t, 7 - t])
    q_own = after(q_own, out_owns[1])
    att_own, log_own = attend_forward(length_row, blocks, KEYS, q_own, k_own, v_own, valid_wide)
    att_owns = gather_tensor(att_own)
    shared_block = assemble(t_array, after(quarters, att_owns[1]))
    q_part, k_part, v_part = project(normed_one, None, shared_block, cosine, sine)
    att_part, log_part = attend_forward(length_row, part_blocks, PIECE, q_part, k_part, v_part, valid_wide)
    att_shares = gather_tensor(att_part)
    weights = out_owns + [shared_block]
    middle_low, middle_high, middle_mine, normed_two = out_project(
        t_array, tokens, gain_two, att_owns, att_shares, weights
    )
    hidden, d_gate_up, two_kept, two_sent, terms_low, terms_high = feed_forward(
        t_array, normed_two, own_cotangent, after(feed_all, normed_two)
    )

    two_came = swap(two_sent, "tensor", 1)
    d_gate_up = after(d_gate_up, two_kept)
    in_grad = dot_tn(normed_two, d_gate_up).astype(bf16)
    two_near, two_far = near_far(two_kept, after(two_came, in_grad))
    two_far = swap(two_far, "tensor", 2)
    ffn_grad = dot_tn(own_cotangent, after(hidden, two_near)).astype(bf16)

    def halves(g):
        if not small:
            return g, None
        shaped = g.reshape(4, 2, owned_rows, g.shape[1])
        at_y = lax.axis_index("dp") & 1
        return tuple(lax.dynamic_index_in_dim(shaped, at, 1, False) for at in (at_y, 1 - at_y))

    in_half = scatter_one(*halves(after(in_grad, two_near)))

    own_rows = 2 * PIECE
    d_middle, d_branch, *d_att = middle_backward(
        two_near, after(two_far, ffn_grad), middle_mine, own_cotangent[:own_rows], gain_two, weights
    )
    d_att_pieces = exchange_tensor(d_att[1:4])
    terms_low, terms_high = lax.psum(after((terms_low, terms_high), d_middle), "tensor")
    d_shared, shared_mine = attend_backward_shared(
        t_array, length_row, part_blocks, q_part, k_part, v_part, valid_wide, log_part, att_part,
        after(d_att[4], d_att_pieces[0]), cosine, sine,
    )
    early_kept, early_sent = early_grads(t_array, d_branch, att_owns, att_part, normed_one, d_shared)
    early_came = swap(early_sent, "tensor", 1)
    in_quarter = scatter_two(after(in_half, early_sent))
    early_near, early_far = near_far(early_kept, after(early_came, in_quarter[0]))
    early_far = swap(early_far, "tensor", 2)
    ffn_half = scatter_one(*halves(after(ffn_grad, in_quarter[0])))
    d_att_pieces = after(d_att_pieces, (early_near, ffn_half[0]))
    d_own, *own_sent, own_mine = attend_backward_own(
        t_array, length_row, q_own, k_own, v_own, valid_wide, log_own, att_own, [d_att[0]] + d_att_pieces, cosine, sine, d_shared
    )
    own_came = exchange_tensor(own_sent)
    if small:
        attn_half = scatter_one(*attn_grads(me, normed_one, after(d_own, own_came[0]), early_near, early_far))
    else:
        early = early_near + early_far.astype(f32)
        attn_half = (jnp.concatenate([early, dot_tn(normed_one, d_own), jnp.zeros((D, 64), f32)], axis=1),)
    ffn_quarter = scatter_two(after(ffn_half, attn_half[0]))
    grad_mine = input_backward(
        t_array, tokens, d_middle, gain_one, own_mine, shared_mine, after(own_came, ffn_quarter[0]), slabs, shared_block
    )
    grad_pieces = gather_tensor(grad_mine)
    attn_quarter = scatter_two(after(attn_half, grad_pieces[1]))
    layer_out = jnp.concatenate(
        [middle_low + terms_low.astype(f32), middle_high + terms_high.astype(f32)], axis=0
    ).astype(bf16)
    input_grad = natural_order(after(grad_pieces, attn_quarter[0]), t_array)

    owned_ffn_out = jnp.transpose(scatter_end(ffn_quarter))
    owned_in = scatter_end(in_quarter)
    owned_ffn_in = jnp.stack([owned_in[:, :hidden_count], owned_in[:, hidden_count:]], axis=1)
    gain_term = jnp.sum(w_ffn_in.astype(bf16).astype(f32) * owned_ffn_in, axis=(1, 2))
    gain_high = lax.reduce_precision(gain_term, 8, 7)
    owned_attn = scatter_end(attn_quarter)
    owned_attn = jnp.concatenate(
        [owned_attn[:, :SLAB], gain_high[:, None], (gain_term - gain_high)[:, None], owned_attn[:, SLAB + 2 :]], axis=1
    ).astype(bf16)
    all_pieces = gather_tensor(owned_attn)
    groups = [t ^ k for k in range(4)] + [last]
    in_order = jnp.zeros((owned_rows, WIDE), bf16)
    for k, piece in enumerate(all_pieces):
        in_order = lax.dynamic_update_slice_in_dim(in_order, piece[:, :128], 128 * (t ^ k), 1)
    attn_columns = jnp.concatenate([slab_columns(slot_head, group) for group in groups])
    projection_grad = dot_nt(
        jnp.concatenate([piece[:, 384 : 384 + SLAB] for piece in all_pieces] + [in_order[:, :SLAB]], axis=1),
        one_hot(attn_columns, NQ * HD + 2 * KV * HD),
    )
    out_columns = jnp.concatenate([out_rows(slot_head, group) for group in groups])
    output_grad = dot_nt(
        one_hot(out_columns, NQ * HD),
        jnp.concatenate([piece[:, 128:SLAB] for piece in all_pieces] + [in_order[:, SLAB:]], axis=1),
    )
    projection = jnp.concatenate([w_query, w_keyval], axis=1).astype(bf16).astype(f32)
    gain_one_grad = jnp.sum(projection * projection_grad, axis=1) / norm_gains[0]
    gain_two_grad = sum(jnp.sum(piece[:, SLAB : SLAB + 2].astype(f32), axis=1) for piece in all_pieces) / norm_gains[1]
    gains_grad = jnp.stack([gain_one_grad, gain_two_grad], axis=0)

    matrix_rate = 0.5 * D ** (-0.5)
    rates = (matrix_rate, matrix_rate, 0.5 * OUT_FAN ** (-0.5), matrix_rate, 0.5 * FF ** (-0.5), 0.3)
    decays = (0.1, 0.1, 0.1, 0.1, 0.1, 0.0)
    reduced = (
        projection_grad[:, : NQ * HD], projection_grad[:, NQ * HD :], output_grad, owned_ffn_in, owned_ffn_out, gains_grad,
    )
    weights = (w_query, w_keyval, w_output, w_ffn_in, w_ffn_out, norm_gains)
    firsts = (first_query, first_keyval, first_output, first_ffn_in, first_ffn_out, first_gains)
    seconds = (second_query, second_keyval, second_output, second_ffn_in, second_ffn_out, second_gains)
    averages = (average_query, average_keyval, average_output, average_ffn_in, average_ffn_out, average_gains)
    updates = [
        adam_step(weights[m], firsts[m], seconds[m], averages[m], reduced[m], rates[m], decays[m])
        for m in range(6)
    ]
    return (layer_out, input_grad) + reduced + tuple(updates[m][part] for part in range(4) for m in range(6))


def solution(mesh):
    token, rows, columns = P("dp", None), P("dp", None), P(None, "dp")
    weight_specs = (rows, rows, columns, P("dp", None, "tensor"), P("tensor", "dp"), columns)
    in_specs = (token, token, P("dp", None), P("dp"), P()) + weight_specs * 4
    out_specs = (token, token) + weight_specs * 5
    return jax.shard_map(local, mesh=mesh, in_specs=in_specs, out_specs=out_specs, check_vma=False)
```

```python
import functools

import jax
import jax.numpy as jnp
import numpy as np
from jax import lax
from jax.experimental import pallas as pl
from jax.experimental.layout import Layout, with_layout_constraint
from jax.experimental.pallas import tpu as pltpu
from jax.sharding import PartitionSpec as P

D = 960
FF = 2560
NQ = 15
KV = 5
HD = 64
STEP = 10
GROUP = 3
OUT_FAN = 3
SLAB = 320
HEADW = GROUP * HD
WIDE = SLAB + HEADW
PIECE = 160
KEYS = 256

norm_eps = 1e-05
rope_base = 10000.0
beta_first = 0.5
beta_second = 0.5
adam_eps = 1e-08
average_keep = 0.5
bf16 = jnp.bfloat16
f32 = jnp.float32
VMEM_LIMIT = 48 * 1024 * 1024


def params(*semantics):
    return pltpu.CompilerParams(dimension_semantics=semantics, vmem_limit_bytes=VMEM_LIMIT)


def by_rows(x):
    return with_layout_constraint(x, Layout(major_to_minor=tuple(range(x.ndim))))


def swap(x, axis, offset):
    count = lax.axis_size(axis)
    return by_rows(lax.ppermute(by_rows(x), axis, [(i, i ^ offset) for i in range(count)]))


def dot_nn(a, b):
    return lax.dot_general(a, b, (((1,), (0,)), ((), ())), preferred_element_type=f32)


def dot_nt(a, b):
    return lax.dot_general(a, b, (((1,), (1,)), ((), ())), preferred_element_type=f32)


def dot_tn(a, b):
    return lax.dot_general(a, b, (((0,), (0,)), ((), ())), preferred_element_type=f32)


TIMES = {
    "prepare": 2.5, "place": 3.5, "assemble": 1.0, "own_order": 1.0, "natural_order": 2.5, "project": 4.5,
    "attend_forward": 8.0, "out_project": 10.0, "feed_forward": 20.0, "feed_grads": 0.0, "near_far": 2.0, "half_sums": 2.0,
    "middle_backward": 4.5, "attend_backward_shared": 5.5, "early_grads": 6.5, "attend_backward_own": 18.0,
    "attn_grads": 5.0, "layer_rows": 1.5, "feed_adam": 5.0, "attn_adam": 6.0, "input_backward": 0.0,
}


def kernel_call(body, scalars, arrays, *, out_shape, grid, in_specs, out_specs, scratch_shapes=(), name, far=False, far_out=False):
    single = not isinstance(out_shape, (list, tuple))
    shapes = [out_shape] if single else out_shape
    call = pl.pallas_call(
        body,
        out_shape=[pltpu.HBM(shape.shape, shape.dtype) for shape in shapes] if far_out else shapes,
        grid_spec=pltpu.PrefetchScalarGridSpec(
            num_scalar_prefetch=len(scalars),
        grid=grid,
        in_specs=in_specs,
        out_specs=[out_specs] if single else out_specs,
        scratch_shapes=scratch_shapes,
        ),
        compiler_params=params("arbitrary"),
        cost_estimate=pl.CostEstimate(flops=0, bytes_accessed=int(TIMES[name] * 3.2e6), transcendentals=0),
        name=name,
    )
    if far:
        arrays = [pltpu.with_memory_space_constraint(x, pltpu.HBM) for x in arrays]
    outs = call(*scalars, *arrays)
    return outs[0] if single else outs


def after(values, *earlier):
    return lax.optimization_barrier((values, earlier))[0]


def turn(k):
    return (k & 1) * 2 + k // 2


def place_of(block, t):
    owner = jnp.minimum(block, 7 - block)
    return 2 * turn(owner ^ t) + (block > 3).astype(jnp.int32)


def place_body(index_ref, *refs):
    pieces, (slab_ref, out_ref, quarter_ref, rest_ref) = refs[:-4], refs[-4:]
    rows = slab_ref.shape[1]
    half = len(pieces) // 2
    for slot, piece in enumerate(pieces):
        at = index_ref[slot]
        slab_ref[at] = piece[:rows, : slab_ref.shape[2]]
        quarter_ref[at] = piece[:rows, WIDE:]
        rest_ref[at] = piece[rows:, :128]
        out = piece[:rows, SLAB:WIDE]

        @pl.when(at < half)
        def _():
            out_ref[at, :, :HEADW] = out

        @pl.when(at >= half)
        def _():
            out_ref[at - half, :, HEADW:] = out


def place(pieces, index, rows):
    height = pieces[0].shape[0]
    count = len(pieces)
    shapes = [(count, rows, 384), (count // 2, rows, 2 * HEADW), (count, rows, 128), (count, height - rows, 128)]
    return kernel_call(
        place_body,
        [index],
        pieces,
        out_shape=[jax.ShapeDtypeStruct(shape, pieces[0].dtype) for shape in shapes],
        grid=(1,),
        in_specs=[whole_spec(pieces[0].shape)] * count,
        out_specs=[whole_spec(shape) for shape in shapes],
        name="place",
        far=True,
        far_out=True,
    )


def assemble_body(t_ref, *refs):
    for k in range(4):
        at = pl.multiple_of((t_ref[0] ^ k) * 128, 128)
        refs[4][:, pl.ds(at, 128)] = refs[k][...]


def assemble(t, pieces):
    rows = pieces[0].shape[0]
    return kernel_call(
        assemble_body,
        [t],
        pieces,
        out_shape=jax.ShapeDtypeStruct((rows, WIDE), bf16),
        grid=(1,),
        in_specs=[whole_spec((rows, 128))] * 4,
        out_specs=whole_spec((rows, WIDE)),
        name="assemble",
    )


def reorder_body(t_ref, x_ref, out_ref):
    out_ref[...] = x_ref[...]


def own_order(x, t):
    width = x.shape[1]
    owner = lambda p, t_ref: t_ref[0] ^ turn(p // 2)
    return kernel_call(
        reorder_body,
        [t],
        [x],
        out_shape=jax.ShapeDtypeStruct(x.shape, x.dtype),
        grid=(8,),
        in_specs=[
                pl.BlockSpec(
                    (PIECE, width),
                    lambda p, t_ref: (jnp.where(p % 2 == 0, owner(p, t_ref), 7 - owner(p, t_ref)), 0),
                )
            ],
        out_specs=pl.BlockSpec((PIECE, width), lambda p, t_ref: (p, 0)),
        name="own_order",
    )


def natural_body(t_ref, *refs):
    half, t = pl.program_id(0), t_ref[0]
    pieces, out_ref = refs[:4], refs[4]
    parts = []
    for block in range(4):
        owner = jnp.where(half == 0, block, 3 - block)
        part = pieces[0][...]
        for k in (1, 2, 3):
            part = jnp.where((owner ^ t) == k, pieces[k][...], part)
        parts.append(part)
    out_ref[...] = jnp.transpose(jnp.concatenate(parts, axis=0))


def natural_order(pieces, t):
    width = pieces[0].shape[1]
    turned = kernel_call(
        natural_body,
        [t],
        pieces,
        out_shape=jax.ShapeDtypeStruct((width, 8 * PIECE), pieces[0].dtype),
        grid=(2,),
        in_specs=[pl.BlockSpec((PIECE, width), lambda b, t_ref: (b, 0))] * 4,
        out_specs=pl.BlockSpec((width, 4 * PIECE), lambda b, t_ref: (0, b)),
        name="natural_order",
        far=True,
    )
    return jnp.transpose(turned)


def gather_one(x):
    if lax.axis_size("dp") != 8:
        return [x]
    return [x] + [swap(x, "dp", k) for k in (2, 4, 6)]


def gather_two(pieces):
    if len(pieces) == 1:
        return pieces
    return pieces + [swap(piece, "dp", 1) for piece in pieces]


def gather_end(pieces, rows):
    if len(pieces) == 1:
        both = lax.all_gather(pieces[0], "dp", axis=0)
        whole = both[:, :rows].reshape(D, WIDE + 128)
        out = whole[:, SLAB:WIDE]
        return whole[:, :384], jnp.concatenate([out[: D // 2], out[D // 2 :]], axis=1), whole[:, WIDE:], both[:, rows:, :128]
    me = lax.axis_index("dp")
    index = jnp.stack([me ^ k for k in (0, 2, 4, 6, 1, 3, 5, 7)]).astype(jnp.int32)
    slab, out, quarter, rest = place(pieces, index, rows)
    return slab.reshape(D, 384), out.reshape(D // 2, 2 * HEADW), quarter.reshape(D, 128), rest


def scatter_one(kept, sent):
    if sent is None:
        return (kept,)
    return kept, swap(sent, "dp", 1)


def scatter_two(halves):
    if len(halves) == 1:
        return halves
    mine, *sent = half_sums(lax.axis_index("dp").astype(jnp.int32).reshape(1), *halves)
    return [mine] + [swap(piece, "dp", 2 * (k + 1)) for k, piece in enumerate(sent)]


def scatter_end(quarters):
    if len(quarters) == 1:
        return lax.psum_scatter(quarters[0].astype(f32), "dp", scatter_dimension=0, tiled=True)
    return sum(quarter.astype(f32) for quarter in quarters)


def half_body(me_ref, kept_ref, came_ref, mine_ref, *sent_refs):
    at_z = me_ref[0] >> 1
    mine_ref[...] = kept_ref[at_z].astype(f32) + came_ref[at_z].astype(f32)
    for k, sent_ref in enumerate(sent_refs):
        at = at_z ^ (k + 1)
        sent_ref[...] = (kept_ref[at].astype(f32) + came_ref[at].astype(f32)).astype(bf16)


def half_sums(me, kept, came):
    count, rows, columns = kept.shape
    return kernel_call(
        half_body,
        [me],
        [kept, came],
        out_shape=[jax.ShapeDtypeStruct((rows, columns), f32)]
        + [jax.ShapeDtypeStruct((rows, columns), bf16)] * (count - 1),
        grid=(1,),
        in_specs=[whole_spec(kept.shape)] * 2,
        out_specs=[whole_spec((rows, columns))] * count,
        name="half_sums",
    )


def split_chunks(me_ref, chunks, kept_ref, sent_ref):
    at_y = (me_ref[0] & 1) == 0
    for z in range(len(chunks) // 2):
        even, odd = chunks[2 * z].astype(bf16), chunks[2 * z + 1].astype(bf16)
        kept_ref[z] = jnp.where(at_y, even, odd)
        sent_ref[z] = jnp.where(at_y, odd, even)


def gather_first(x):
    across = swap(x, "tensor", 2)
    return [x, swap(x, "tensor", 1), across]


def gather_second(pieces):
    return pieces + [swap(pieces[2], "tensor", 1)]


def gather_tensor(x):
    return gather_second(gather_first(x))


def exchange_tensor(pieces):
    return [swap(piece, "tensor", k + 1) for k, piece in enumerate(pieces)]


def slab_target(group, group_ref):
    lane = lax.broadcasted_iota(jnp.int32, (1, SLAB), 1)
    second = lane >= 128
    value = lane >= 256
    within = jnp.where(second, lane - 128, lane)
    inside = (within & 31) + jnp.where(second, 32, 0)
    member = within >> 5
    query_at = jnp.full_like(lane, -1)
    for which in range(GROUP):
        query_at = jnp.where(member == which, head_of(group, which, group_ref) * HD + inside, query_at)
    query_at = jnp.where(value, -1, query_at)
    key_at = jnp.where(member == GROUP, group * HD + inside, -1)
    key_at = jnp.where(value, KV * HD + group * HD + lane - 256, key_at)
    return query_at, key_at


def head_of(group, which, group_ref):
    slot = group * GROUP + which
    head = jnp.int32(0)
    for h in range(NQ):
        head = jnp.where(group_ref[h] == slot, h, head)
    return head


def pick(width, index):
    rows = lax.broadcasted_iota(jnp.int32, (width, index.shape[1]), 0)
    return jnp.where(rows == index, 1.0, 0.0).astype(bf16)


def unit(count):
    rows = lax.broadcasted_iota(jnp.int32, (count, count), 0)
    return jnp.where(rows == lax.broadcasted_iota(jnp.int32, (count, count), 1), 1.0, 0.0).astype(bf16)


def prep_body(t_ref, index_ref, query_ref, keyval_ref, output_ref, gains_ref, out_ref):
    count = query_ref.shape[0]
    query, keyval = query_ref[...].astype(bf16), keyval_ref[...].astype(bf16)

    def block(group):
        query_at, key_at = slab_target(group, index_ref)
        picked = dot_nn(query, pick(NQ * HD, query_at)) + dot_nn(keyval, pick(2 * KV * HD, key_at))
        heads = [
            output_ref[pl.ds(pl.multiple_of(head_of(group, which, index_ref) * HD, HD), HD), :] for which in range(GROUP)
        ]
        turned = dot_nt(unit(count), jnp.concatenate(heads, axis=0).astype(bf16))
        return jnp.concatenate([picked, turned], axis=1)

    t = t_ref[0]
    shared = block(KV - 1)
    quarter = shared[:, :128]
    for k in (1, 2, 3):
        quarter = jnp.where(t == k, shared[:, 128 * k : 128 * (k + 1)], quarter)
    out_ref[:count, :] = jnp.concatenate([block(t), quarter], axis=1).astype(bf16)
    missing = out_ref.shape[0] - count
    gains = gains_ref[...]
    high = gains.astype(bf16).astype(f32)
    middle = (gains - high).astype(bf16).astype(f32)
    low = gains - high - middle
    rest = jnp.concatenate([high, middle, low, jnp.zeros((missing - 6, count), f32)], axis=0)
    rest = jnp.concatenate([rest, jnp.zeros((missing, WIDE + 128 - count), f32)], axis=1)
    out_ref[count:, :] = rest.astype(bf16)


def prepare(t, query_group, w_query, w_keyval, w_output, norm_gains, rows):
    return kernel_call(
        prep_body,
        [t, query_group],
        [w_query, w_keyval, w_output, norm_gains],
        out_shape=jax.ShapeDtypeStruct((rows, WIDE + 128), bf16),
        grid=(1,),
        in_specs=[whole_spec(x.shape) for x in (w_query, w_keyval, w_output, norm_gains)],
        out_specs=whole_spec((rows, WIDE + 128)),
        name="prepare",
        far=True,
    )


def pair_specs(width):
    owner = lambda p, t_ref: t_ref[0] ^ turn(p)
    return [
        pl.BlockSpec((PIECE, width), lambda p, t_ref: (owner(p, t_ref), 0)),
        pl.BlockSpec((PIECE, width), lambda p, t_ref: (7 - owner(p, t_ref), 0)),
    ]


def packed_specs():
    owner = lambda p, t_ref: t_ref[0] ^ turn(p)
    return [
        pl.BlockSpec((PIECE, 2 * HEADW), lambda p, t_ref: (owner(p, t_ref), 0)),
        pl.BlockSpec((PIECE, 2 * HEADW), lambda p, t_ref: (3 - owner(p, t_ref), 0)),
    ]


def unpack(low, high):
    return jnp.concatenate([low[:, :HEADW], high[:, HEADW:]], axis=0)


def pack(pair):
    rows = pair.shape[0] // 2
    return jnp.concatenate([pair[:rows], pair[rows:]], axis=1)


def split_heads(normed, w_ref, cosine, sine, guard, q_ref, k_ref, v_ref):
    y = dot_nn(normed, w_ref[:, :SLAB])
    first, second = y[:, :128], y[:, 128:256]
    turned_first = first * cosine - second * sine
    turned_second = second * cosine + first * sine
    for head in range(GROUP + 1):
        columns = slice(32 * head, 32 * head + 32)
        both = jnp.concatenate([turned_first[:, columns], turned_second[:, columns]], axis=1)
        if head < GROUP:
            both = both.astype(bf16).astype(f32) * HD ** (-0.5)
            q_ref[head] = jnp.concatenate([both, guard[:, :HD]], axis=1).astype(bf16)
        else:
            k_ref[...] = jnp.concatenate([both, guard[:, HD:]], axis=1).astype(bf16)
    v_ref[...] = y[:, 256:].astype(bf16)


def guards(length_ref, valid_ref, rows):
    row = pl.program_id(0) * rows + lax.broadcasted_iota(jnp.int32, (rows, 128), 0)
    lane = lax.broadcasted_iota(jnp.int32, (rows, 128), 1)
    end_one = length_ref[0]
    end_two = end_one + length_ref[1]
    sequence = (row >= end_one).astype(jnp.int32) + (row >= end_two).astype(jnp.int32)
    query = jnp.where((lane == sequence) | (lane == 3), 1.0, 0.0)
    shut = ((lane >= HD) & (lane < HD + 3) & (lane - HD != sequence)) | ((lane == HD + 3) & (valid_ref[...] != 1))
    return jnp.where(lane < HD, query, jnp.where(shut, -(2.0**100), 0.0))


def proj_own_body(length_ref, x_ref, gain_ref, w_ref, cos_ref, sin_ref, valid_ref, normed_ref, q_ref, k_ref, v_ref):
    x = x_ref[...].astype(f32)
    factor = lax.rsqrt(jnp.mean(x * x, axis=-1, keepdims=True) + norm_eps)
    normed = (x * factor * gain_ref[...]).astype(bf16)
    normed_ref[...] = normed
    guard = guards(length_ref, valid_ref, x.shape[0])
    split_heads(normed, w_ref, cos_ref[...], sin_ref[...], guard, q_ref, k_ref, v_ref)


def proj_shared_body(length_ref, normed_ref, w_ref, cos_ref, sin_ref, valid_ref, q_ref, k_ref, v_ref):
    guard = guards(length_ref, valid_ref, normed_ref.shape[0])
    split_heads(normed_ref[...], w_ref, cos_ref[...], sin_ref[...], guard, q_ref, k_ref, v_ref)


def project(lengths, x, gain, weight, cosine, sine, valid):
    rows = x.shape[0]
    step = 2 * PIECE
    by_step = lambda width: pl.BlockSpec((step, width), lambda i, *scalars: (i, 0))
    outs = [
        (jax.ShapeDtypeStruct((GROUP, rows, 128), bf16), pl.BlockSpec((GROUP, step, 128), lambda i, *scalars: (0, i, 0))),
        (jax.ShapeDtypeStruct((rows, 128), bf16), by_step(128)),
        (jax.ShapeDtypeStruct((rows, HD), bf16), by_step(HD)),
    ]
    if gain is not None:
        outs = [(jax.ShapeDtypeStruct(x.shape, bf16), by_step(D))] + outs
    gains = [] if gain is None else [gain]
    return kernel_call(
        proj_shared_body if gain is None else proj_own_body,
        [lengths],
        [x, *gains, weight, cosine, sine, valid],
        out_shape=[shape for shape, _ in outs],
        grid=(rows // step,),
        in_specs=[by_step(D)]
        + [whole_spec((1, D))] * len(gains)
        + [whole_spec(weight.shape), by_step(128), by_step(128), by_step(128)],
        out_specs=[spec for _, spec in outs],
        name="project",
        far=True,
        far_out=True,
    )


def lanes_of(rows):
    return -(-GROUP * rows // 128) * 128


def start_of(row, length_ref):
    end_one = length_ref[0]
    end_two = end_one + length_ref[1]
    return jnp.where(row >= end_two, end_two, jnp.where(row >= end_one, end_one, 0))


def lane_rows(block, rows, length_ref):
    lane = lax.broadcasted_iota(jnp.int32, (1, lanes_of(rows)), 1)
    head = sum((lane >= h * rows).astype(jnp.int32) for h in range(1, GROUP + 1))
    row = jnp.where(head < GROUP, block * rows + lane - head * rows, 1 << 20)
    return row, jnp.where(head < GROUP, start_of(row, length_ref), 1 << 20)


def key_range(block, rows, length_ref):
    first = start_of(block * rows, length_ref) // KEYS
    return first, (block * rows + rows + KEYS - 1) // KEYS


def key_mask(shut, at, row, start):
    index = at + lax.broadcasted_iota(jnp.int32, (KEYS, row.shape[1]), 0)
    return ((index >= start) & (index <= row) & (shut == 0.0)) | (index == row)


def fill(stacked, lanes):
    parts = [stacked[head] for head in range(GROUP)]
    missing = lanes - GROUP * stacked[0].shape[0]
    if missing:
        parts.append(jnp.zeros((missing, parts[0].shape[1]), bf16))
    return jnp.concatenate(parts, axis=0)


def forward_body(length_ref, block_ref, q_ref, k_ref, v_ref, out_ref, log_ref, acc):
    rows = q_ref.shape[1]
    lanes = acc.shape[1]
    block = block_ref[pl.program_id(0)]
    q = fill(q_ref[...], lanes)
    row, start = lane_rows(block, rows, length_ref)
    acc[...] = jnp.zeros_like(acc)

    def step(carry, here, scores):
        peak, total = carry
        new_peak = jnp.maximum(peak, jnp.max(scores, axis=0, keepdims=True))
        exponent = jnp.exp(scores - new_peak)
        shrink = jnp.exp(peak - new_peak)
        total = total * shrink + jnp.sum(exponent, axis=0, keepdims=True)
        acc[...] = acc[...] * shrink + dot_tn(v_ref[here, :], exponent.astype(bf16))
        return new_peak, total

    def before(j, carry):
        here = pl.ds(pl.multiple_of(j * KEYS, KEYS), KEYS)
        return step(carry, here, dot_nt(k_ref[here, :], q))

    def across(j, carry):
        at = pl.multiple_of(j * KEYS, KEYS)
        here = pl.ds(at, KEYS)
        scores = dot_nt(k_ref[here, :HD], q[:, :HD])
        return step(carry, here, jnp.where(key_mask(k_ref[here, HD + 3 : HD + 4].astype(f32), at, row, start), scores, -1e30))

    low, high = key_range(block, rows, length_ref)
    middle = jnp.maximum(low, block * rows // KEYS)
    carry = (jnp.full((1, lanes), -1e30, f32), jnp.zeros((1, lanes), f32))
    peak, total = lax.fori_loop(middle, high, across, lax.fori_loop(low, middle, before, carry))
    log_ref[0] = peak + jnp.log(total)
    attended = jnp.transpose(acc[...] / total)
    attended = jnp.concatenate(
        [attended[head * rows : (head + 1) * rows] for head in range(GROUP)], axis=1
    ).astype(bf16)
    half = out_ref.shape[0]
    chunk = min(rows, 128) if half > rows else rows
    for part in range(rows // chunk):
        at = pl.program_id(0) * rows + part * chunk
        piece = attended[part * chunk : (part + 1) * chunk]

        @pl.when(at < half)
        def _():
            out_ref[pl.ds(pl.multiple_of(at, chunk), chunk), :HEADW] = piece

        @pl.when(at >= half)
        def _():
            out_ref[pl.ds(pl.multiple_of(at - half, chunk), chunk), HEADW:] = piece


def attend_forward(lengths, blocks, size, q, k, v):
    count, rows = blocks.shape[0], k.shape[0]
    lanes = lanes_of(size)
    return kernel_call(
        forward_body,
        [lengths, blocks],
        [q, k, v],
        out_shape=[
            jax.ShapeDtypeStruct((count * size // 2, 2 * HEADW), bf16),
            jax.ShapeDtypeStruct((count, 1, lanes), f32),
        ],
        grid=(count,),
        in_specs=[
                pl.BlockSpec((GROUP, size, 128), lambda i, lengths, blocks: (0, blocks[i], 0)),
                whole_spec((rows, 128)), whole_spec((rows, HD)),
            ],
        out_specs=[
                whole_spec((count * size // 2, 2 * HEADW)),
                pl.BlockSpec((1, 1, lanes), lambda i, *scalars: (i, 0, 0)),
            ],
        scratch_shapes=[pltpu.VMEM((HD, lanes), f32)],
        name="attend_forward",
        far=True,
        far_out=True,
    )


def backward_block(block, rows, length_ref, q, k_ref, v_ref, logs, attended, upstream, cosine, sine, dk, dv, acc):
    lanes = q.shape[0]
    row, start = lane_rows(block, rows, length_ref)
    heads = lambda wide: fill([wide[:, h * HD : (h + 1) * HD] for h in range(GROUP)], lanes)
    up = heads(upstream)
    both = up.astype(f32) * heads(attended).astype(f32)
    both_high = both.astype(bf16)
    both_low = (both - both_high.astype(f32)).astype(bf16)
    ones = jnp.ones((8, HD), bf16)
    inner = (dot_nt(ones, both_high) + dot_nt(ones, both_low))[:1]
    acc[...] = jnp.zeros_like(acc)

    heads_only = q[:, :HD]

    def step(here, scores):
        probs = jnp.exp(scores - logs)
        d_probs = dot_nt(v_ref[here, :], up)
        d_scores = (probs * (d_probs - inner)).astype(bf16)
        dv[here, :] += dot_nn(probs.astype(bf16), up)
        dk[here, :] += dot_nn(d_scores, heads_only)
        acc[...] += dot_tn(k_ref[here, :HD], d_scores)

    def before(j, carry):
        here = pl.ds(pl.multiple_of(j * KEYS, KEYS), KEYS)
        step(here, dot_nt(k_ref[here, :], q))
        return carry

    def across(j, carry):
        at = pl.multiple_of(j * KEYS, KEYS)
        here = pl.ds(at, KEYS)
        scores = dot_nt(k_ref[here, :HD], heads_only)
        step(here, jnp.where(key_mask(k_ref[here, HD + 3 : HD + 4].astype(f32), at, row, start), scores, -1e30))
        return carry

    low, high = key_range(block, rows, length_ref)
    middle = jnp.maximum(low, block * rows // KEYS)
    lax.fori_loop(low, middle, before, 0)
    lax.fori_loop(middle, high, across, 0)
    turned = jnp.transpose(acc[...] * HD ** (-0.5))
    first = jnp.concatenate([turned[h * rows : (h + 1) * rows, :32] for h in range(GROUP)], axis=1)
    second = jnp.concatenate([turned[h * rows : (h + 1) * rows, 32:] for h in range(GROUP)], axis=1)
    cosine, sine = cosine[:, :96], sine[:, :96]
    return first * cosine + second * sine, second * cosine - first * sine


def turn_back(dk, cosine, sine):
    first, second = dk[:, :32], dk[:, 32:]
    cosine, sine = cosine[:, :32], sine[:, :32]
    return first * cosine + second * sine, second * cosine - first * sine


def rows_at(block):
    return pl.ds(pl.multiple_of(block * PIECE, PIECE), PIECE)


def attended_rows(out_ref, at, rows):
    half = out_ref.shape[0]
    parts = []
    for part in range(rows // 128):
        here = at + part * 128
        low = pl.multiple_of(jnp.where(here < half, here, here - half), 128)
        both = out_ref[pl.ds(low, 128), :]
        parts.append(jnp.where(here < half, both[:, :HEADW], both[:, HEADW:]))
    return jnp.concatenate(parts, axis=0)


def backward_own_body(
    t_ref, length_ref, q_ref, k_ref, v_ref, log_ref, out_ref, up_0, up_1, up_2, up_3, weight_ref, cos_ref, sin_ref, shared_ref,
    slab_ref, *rest
):
    send_refs, mine_ref, (dk, dv, acc, upstream) = rest[:3], rest[3], rest[4:]
    rows = q_ref.shape[1]
    step = pl.program_id(0)
    t = t_ref[0]
    block = pl.num_programs(0) - 1 - step

    @pl.when(step == 0)
    def _():
        dk[...] = jnp.zeros_like(dk)
        dv[...] = jnp.zeros_like(dv)
        weight = out_weight(weight_ref)
        for k, piece in enumerate((up_0, up_1, up_2, up_3)):
            d_attended = dot_nn(piece[...], weight).astype(bf16)
            upstream[rows_at(t ^ k), :] = d_attended[:PIECE]
            upstream[rows_at(7 - (t ^ k)), :] = d_attended[PIECE:]

    cosine, sine = cos_ref[...], sin_ref[...]
    here = pl.ds(pl.multiple_of(block * rows, rows), rows)
    q = fill(q_ref[...], acc.shape[1])
    first, second = backward_block(
        block, rows, length_ref, q, k_ref, v_ref, log_ref[0], attended_rows(out_ref, block * rows, rows),
        upstream[here, :], cosine, sine, dk, dv, acc,
    )
    key_first, key_second = turn_back(dk[here, :], cosine, sine)
    slab_ref[here, :] = jnp.concatenate([first, key_first, second, key_second, dv[here, :]], axis=1).astype(bf16)

    @pl.when(step == pl.num_programs(0) - 1)
    def _():
        for half, owner in enumerate((t, 7 - t)):
            mine_ref[half * PIECE : (half + 1) * PIECE, :] = slab_ref[rows_at(owner), :]
        for k, target in enumerate(send_refs):
            for half, owner in enumerate((t ^ (k + 1), 7 - (t ^ (k + 1)))):
                own, shared = slab_ref[rows_at(owner), :], shared_ref[rows_at(owner), :]
                target[half * PIECE : (half + 1) * PIECE, :] = jnp.concatenate(
                    [own, shared[:, 96:128], shared[:, 224:256], shared[:, 256:], jnp.zeros((PIECE, 64), bf16)], axis=1
                )


def attend_backward_own(t, lengths, q, k, v, logs, attended, pieces, weight, cosine, sine, shared):
    rows = k.shape[0]
    size = KEYS
    count, lanes = rows // size, lanes_of(size)
    at = lambda i: count - 1 - i
    by_step = lambda width: pl.BlockSpec((size, width), lambda i, *scalars: (at(i), 0))
    return kernel_call(
        backward_own_body,
        [t, lengths],
        [q, k, v, logs, attended, *pieces, weight, cosine, sine, shared],
        out_shape=[jax.ShapeDtypeStruct((rows, SLAB), bf16)]
        + [jax.ShapeDtypeStruct((2 * PIECE, WIDE), bf16)] * 3
        + [jax.ShapeDtypeStruct((2 * PIECE, SLAB), bf16)],
        grid=(count,),
        in_specs=[
                pl.BlockSpec((GROUP, size, 128), lambda i, *scalars: (0, at(i), 0)),
                whole_spec((rows, 128)), whole_spec((rows, HD)),
                pl.BlockSpec((1, 1, lanes), lambda i, *scalars: (at(i), 0, 0)), whole_spec((rows // 2, 2 * HEADW)),
            ]
            + [whole_spec((2 * PIECE, D))] * 4
            + [whole_spec(weight.shape)]
            + [by_step(128)] * 2
            + [whole_spec((rows, SLAB))],
        out_specs=[whole_spec((rows, SLAB))] + [whole_spec((2 * PIECE, WIDE))] * 3 + [whole_spec((2 * PIECE, SLAB))],
        scratch_shapes=[
                pltpu.VMEM((rows, HD), f32), pltpu.VMEM((rows, HD), f32), pltpu.VMEM((HD, lanes), f32),
                pltpu.VMEM((rows, HEADW), bf16),
            ],
        name="attend_backward_own",
        far_out=True,
    )


def backward_shared_body(
    t_ref, length_ref, block_ref, q_ref, k_ref, v_ref, log_ref, out_ref, up_ref, cos_ref, sin_ref, cos_all, sin_all,
    slab_ref, mine_ref, dk, dv, acc
):
    step = pl.program_id(0)
    t = t_ref[0]
    block = block_ref[step]

    @pl.when(step == 0)
    def _():
        dk[...] = jnp.zeros_like(dk)
        dv[...] = jnp.zeros_like(dv)
        slab_ref[...] = jnp.zeros_like(slab_ref)

    half = lambda ref: jnp.where(step == 0, ref[:, :HEADW], ref[:, HEADW:])
    first, second = backward_block(
        block, PIECE, length_ref, fill(q_ref[...], acc.shape[1]), k_ref, v_ref, log_ref[0], half(out_ref), half(up_ref),
        cos_ref[...], sin_ref[...], dk, dv, acc,
    )
    slab_ref[rows_at(block), :96] = first.astype(bf16)
    slab_ref[rows_at(block), 128:224] = second.astype(bf16)

    @pl.when(step == pl.num_programs(0) - 1)
    def _():
        key_first, key_second = turn_back(dk[...], cos_all[...], sin_all[...])
        slab_ref[:, 96:128] = key_first.astype(bf16)
        slab_ref[:, 224:256] = key_second.astype(bf16)
        slab_ref[:, 256:] = dv[...].astype(bf16)
        mine_ref[:PIECE, :] = slab_ref[rows_at(t), :]
        mine_ref[PIECE:, :] = slab_ref[rows_at(7 - t), :]


def attend_backward_shared(t, lengths, blocks, q, k, v, logs, attended, upstream, cosine, sine):
    rows = k.shape[0]
    lanes = lanes_of(PIECE)
    mine = whole_spec((PIECE, 2 * HEADW))
    natural = pl.BlockSpec((PIECE, 128), lambda i, t_ref, length_ref, block_ref: (block_ref[i], 0))
    return kernel_call(
        backward_shared_body,
        [t, lengths, blocks],
        [q, k, v, logs, attended, upstream, cosine, sine, cosine, sine],
        out_shape=[jax.ShapeDtypeStruct((rows, SLAB), bf16), jax.ShapeDtypeStruct((2 * PIECE, SLAB), bf16)],
        grid=(2,),
        in_specs=[
                pl.BlockSpec((GROUP, PIECE, 128), lambda i, t_ref, length_ref, block_ref: (0, block_ref[i], 0)),
                whole_spec((rows, 128)), whole_spec((rows, HD)),
                pl.BlockSpec((1, 1, lanes), lambda i, *scalars: (i, 0, 0)), mine, mine,
            ]
            + [natural] * 2
            + [whole_spec((rows, 128))] * 2,
        out_specs=[whole_spec((rows, SLAB)), whole_spec((2 * PIECE, SLAB))],
        scratch_shapes=[pltpu.VMEM((rows, HD), f32), pltpu.VMEM((rows, HD), f32), pltpu.VMEM((HD, lanes), f32)],
        name="attend_backward_shared",
        far=True,
    )


def whole_spec(shape):
    return pl.BlockSpec(shape, lambda i, *scalars: (0,) * len(shape))


def out_weight(weight):
    if weight.shape[0] == D:
        return weight[:, SLAB:]
    return jnp.concatenate([weight[:, :HEADW], weight[:, HEADW:]], axis=0)


def out_body(t_ref, x_a, x_b, gain_ref, *refs):
    owns, shares, weights = refs[:8], refs[8:12], refs[12:17]
    mine_ref, normed_ref, w_out = refs[17:]
    step = pl.program_id(0)

    @pl.when(step == 0)
    def _():
        w_out[...] = jnp.concatenate([out_weight(weight) for weight in weights], axis=1)

    middle = jnp.concatenate([x_a[...], x_b[...]], axis=0).astype(f32)
    heads = [unpack(owns[2 * k][...], owns[2 * k + 1][...]) for k in range(4)]
    share = jnp.where(
        step == 0, shares[0][...],
        jnp.where(step == 1, shares[2][...], jnp.where(step == 2, shares[1][...], shares[3][...])),
    )
    middle = middle + dot_nt(jnp.concatenate(heads + [unpack(share, share)], axis=1), w_out[...])
    factor = lax.rsqrt(jnp.mean(middle * middle, axis=-1, keepdims=True) + norm_eps)
    normed_ref[...] = (middle * factor * gain_ref[...]).astype(bf16)

    @pl.when(step == 0)
    def _():
        mine_ref[...] = middle


def out_project(t, x, gain, owns, shares, weights):
    rows = x.shape[0]
    return kernel_call(
        out_body,
        [t],
        [x, x, gain, *[piece for piece in owns for _ in range(2)], *shares, *weights],
        out_shape=[jax.ShapeDtypeStruct((2 * PIECE, D), f32), jax.ShapeDtypeStruct(x.shape, bf16)],
        grid=(4,),
        in_specs=pair_specs(D)
        + [whole_spec((1, D))]
        + packed_specs() * 4
        + [whole_spec((PIECE, 2 * HEADW))] * 4
        + [whole_spec(weight.shape) for weight in weights],
        out_specs=[whole_spec((2 * PIECE, D)), pl.BlockSpec((2 * PIECE, D), lambda p, t_ref: (p, 0))],
        scratch_shapes=[pltpu.VMEM((D, D), bf16)],
        name="out_project",
        far=True,
    )


def feed_body(
    normed_ref, cot_ref, w_ref, hidden_ref, d_ref, kept_ref, sent_ref, terms_kept_ref, terms_sent_ref
):
    step = pl.program_id(0)
    width = hidden_ref.shape[1]
    w_gate, w_up, w_out = (w_ref[:, width * part : width * (part + 1)] for part in range(3))
    normed = normed_ref[...]
    gate = dot_nn(normed, w_gate)
    up = dot_nn(normed, w_up)
    d_hidden = dot_nn(cot_ref[...], w_out)
    sigmoid = 1.0 / (1.0 + jnp.exp(-gate))
    silu = gate * sigmoid
    hidden = (silu * up).astype(bf16)
    d_gate = (d_hidden * up * sigmoid * (1.0 + gate * (1.0 - sigmoid))).astype(bf16)
    d_up = (d_hidden * silu).astype(bf16)
    hidden_ref[...] = hidden
    d_ref[:, :width] = d_gate
    d_ref[:, width:] = d_up
    back = (dot_nt(d_gate, w_gate) + dot_nt(d_up, w_up)).astype(bf16)
    terms = dot_nt(hidden, w_out).astype(bf16)

    @pl.when(step < 2)
    def _():
        sent_ref[0] = back
        terms_sent_ref[0] = terms

    @pl.when(step >= 2)
    def _():
        kept_ref[0] = back
        terms_kept_ref[0] = terms


def feed_forward(normed, cotangent, weights):
    rows, width = normed.shape[0], weights.shape[1] // 3
    at = lambda i: (i + 2) % 4
    by_step = lambda columns: pl.BlockSpec((2 * PIECE, columns), lambda i: (at(i), 0))
    pair = jax.ShapeDtypeStruct((2, 2 * PIECE, D), bf16)
    kept = pl.BlockSpec((1, 2 * PIECE, D), lambda i: (jnp.maximum(i - 2, 0), 0, 0))
    sent = pl.BlockSpec((1, 2 * PIECE, D), lambda i: (jnp.minimum(i, 1), 0, 0))
    return kernel_call(
        feed_body,
        [],
        [normed, cotangent, weights],
        out_shape=[jax.ShapeDtypeStruct((rows, width), bf16), jax.ShapeDtypeStruct((rows, 2 * width), bf16)] + [pair] * 4,
        grid=(4,),
        in_specs=[by_step(D), by_step(D), whole_spec(weights.shape)],
        out_specs=[by_step(width), by_step(2 * width), kept, sent, kept, sent],
        name="feed_forward",
        far_out=True,
    )


def feed_grad_body(normed_ref, cot_ref, d_ref, hidden_ref, grad_ref):
    step = pl.program_id(0)

    @pl.when(step < 2)
    def _():
        grad_ref[...] = dot_tn(normed_ref[...], d_ref[...]).astype(bf16)

    @pl.when(step == 2)
    def _():
        grad_ref[...] = dot_tn(cot_ref[...], hidden_ref[...]).astype(bf16)


def feed_grads(normed, cotangent, d_gate_up, hidden):
    rows, width = hidden.shape
    return kernel_call(
        feed_grad_body,
        [],
        [normed, cotangent, d_gate_up, hidden],
        out_shape=jax.ShapeDtypeStruct((D, 3 * width), bf16),
        grid=(3,),
        in_specs=[
            whole_spec((rows, D)), whole_spec((rows, D)),
            pl.BlockSpec((rows, width), lambda i: (0, jnp.minimum(i, 1))), whole_spec((rows, width)),
        ],
        out_specs=pl.BlockSpec((D, width), lambda i: (0, i)),
        name="feed_grads",
        far_out=True,
    )


def near_far_body(kept_ref, came_ref, near_ref, far_ref):
    near_ref[...] = kept_ref[0].astype(f32) + came_ref[0].astype(f32)
    far_ref[...] = (kept_ref[1].astype(f32) + came_ref[1].astype(f32)).astype(bf16)


def near_far(kept, came):
    shape = kept.shape[1:]
    return kernel_call(
        near_far_body,
        [],
        [kept, came],
        grid=(1,),
        out_shape=[jax.ShapeDtypeStruct(shape, f32), jax.ShapeDtypeStruct(shape, bf16)],
        in_specs=[whole_spec(kept.shape)] * 2,
        out_specs=[whole_spec(shape)] * 2,
        name="near_far",
        far=True,
    )


def norm_back(values, gain, upstream):
    factor = lax.rsqrt(jnp.mean(values * values, axis=-1, keepdims=True) + norm_eps)
    weighted = upstream * gain
    inner = jnp.mean(weighted * values, axis=-1, keepdims=True)
    return factor * weighted - values * factor**3 * inner


def layer_body(middle_ref, near_ref, far_ref, out_ref):
    out_ref[...] = (middle_ref[...] + near_ref[...] + far_ref[...].astype(f32)).astype(bf16)


def layer_rows(middle, near, far):
    top = whole_spec(middle.shape)
    return kernel_call(
        layer_body,
        [],
        [middle, near, far],
        out_shape=jax.ShapeDtypeStruct(middle.shape, bf16),
        grid=(1,),
        in_specs=[top] * 3,
        out_specs=top,
        name="layer_rows",
    )


def middle_body(near_ref, far_ref, middle_ref, up_ref, gain_ref, weight_ref, d_middle_ref, d_branch_ref, d_ref):
    upstream = near_ref[...] + far_ref[...].astype(f32)
    d_middle = up_ref[...].astype(f32) + norm_back(middle_ref[...], gain_ref[...], upstream)
    d_middle_ref[...] = d_middle
    d_branch = d_middle.astype(bf16)
    d_branch_ref[...] = d_branch
    d_ref[...] = pack(dot_nn(d_branch, weight_ref[:, SLAB:]).astype(bf16))


def middle_backward(near, far, middle, upstream, gain, shared_block):
    rows = near.shape[0]
    top = whole_spec((rows, D))
    packed = (rows // 2, 2 * HEADW)
    return kernel_call(
        middle_body,
        [],
        [near, far, middle, upstream, gain, shared_block],
        out_shape=[
            jax.ShapeDtypeStruct((rows, D), f32), jax.ShapeDtypeStruct((rows, D), bf16), jax.ShapeDtypeStruct(packed, bf16),
        ],
        grid=(1,),
        in_specs=[top] * 4 + [whole_spec((1, D)), whole_spec(shared_block.shape)],
        out_specs=[top, top, whole_spec(packed)],
        name="middle_backward",
        far_out=True,
    )


def early_body(t_ref, d_branch_ref, share_ref, normed_ref, slab_ref, kept_ref, sent_ref, block):
    t = t_ref[0]
    share = share_ref[...]
    block[...] = jnp.concatenate(
        [dot_tn(normed_ref[...], slab_ref[...]), dot_tn(d_branch_ref[...], unpack(share, share))], axis=1
    ).astype(bf16)
    for k in range(4):
        at = pl.multiple_of((t ^ k) * 128, 128)
        (kept_ref, sent_ref)[k & 1][k // 2] = block[:, pl.ds(at, 128)]


def early_grads(t, d_branch, share, normed, slab):
    arrays = [d_branch, share, normed, slab]
    pair = jax.ShapeDtypeStruct((2, D, 128), bf16)
    return kernel_call(
        early_body,
        [t],
        arrays,
        out_shape=[pair, pair],
        grid=(1,),
        in_specs=[whole_spec(x.shape) for x in arrays],
        out_specs=[whole_spec(pair.shape)] * 2,
        scratch_shapes=[pltpu.VMEM((D, WIDE), bf16)],
        name="early_grads",
        far_out=True,
    )


def attn_grad_body(me_ref, t_ref, normed_ref, slab_ref, near_ref, far_ref, *refs):
    branches, owns, kept_ref, sent_ref = refs[:4], refs[4:12], refs[12], refs[13]
    early = near_ref[...] + far_ref[...].astype(f32)
    grad = dot_tn(normed_ref[...], slab_ref[...])
    out = dot_tn(branches[0][...], unpack(owns[0][...], owns[1][...]))
    for k in (1, 2, 3):
        out = out + dot_tn(branches[k][...], unpack(owns[2 * k][...], owns[2 * k + 1][...]))
    whole = jnp.concatenate([early, grad, out], axis=1)
    rows = kept_ref.shape[1]
    split_chunks(me_ref, [whole[rows * j : rows * (j + 1)] for j in range(D // rows)], kept_ref, sent_ref)


def owner_specs(k):
    return [
        pl.BlockSpec((PIECE, 2 * HEADW), lambda i, me_ref, t_ref: (t_ref[0] ^ k, 0)),
        pl.BlockSpec((PIECE, 2 * HEADW), lambda i, me_ref, t_ref: (3 - (t_ref[0] ^ k), 0)),
    ]


def attn_grads(me, t, normed, slab, near, far, branches, attended):
    half = jax.ShapeDtypeStruct((4, D // 8, WIDE + 128), bf16)
    arrays = [normed, slab, near, far, *branches]
    return kernel_call(
        attn_grad_body,
        [me, t],
        arrays + [attended] * 8,
        out_shape=[half, half],
        grid=(1,),
        in_specs=[whole_spec(x.shape) for x in arrays] + [spec for k in range(4) for spec in owner_specs(k)],
        out_specs=[whole_spec(half.shape)] * 2,
        name="attn_grads",
    )


def input_body(t_ref, x_a, x_b, d_middle_ref, gain_ref, own_ref, shared_ref, *refs):
    came_refs, slabs, shared_slab, out_ref = refs[:3], refs[3:7], refs[7], refs[8]
    upstream = dot_nt(own_ref[...], slabs[0][0, :, :SLAB])
    for piece, slab in zip(came_refs, slabs[1:4]):
        upstream = upstream + dot_nt(piece[:, :SLAB], slab[0, :, :SLAB])
    shared = shared_ref[...]
    key_value = jnp.concatenate([shared[:, 96:128], shared[:, 224:256], shared[:, 256:]], axis=1).astype(f32)
    for piece in came_refs:
        key_value = key_value + piece[:, SLAB : SLAB + 2 * HD].astype(f32)
    key_value = key_value.astype(bf16)
    shared = jnp.concatenate(
        [shared[:, :96], key_value[:, :32], shared[:, 128:224], key_value[:, 32:64], key_value[:, 64:]], axis=1
    )
    upstream = upstream + dot_nt(shared, shared_slab[:, :SLAB])
    x = jnp.concatenate([x_a[...], x_b[...]], axis=0).astype(f32)
    out_ref[...] = (d_middle_ref[...] + norm_back(x, gain_ref[...], upstream)).astype(bf16)


def input_backward(t, x, d_middle, gain, own, shared, came, slabs, shared_block):
    rows = 2 * PIECE
    of_owner = [
        pl.BlockSpec((1, D, 384), functools.partial(lambda k, i, t_ref: (t_ref[0] ^ k, 0, 0), k)) for k in range(4)
    ]
    return kernel_call(
        input_body,
        [t],
        [x, x, d_middle, gain, own, shared, *came, *[slabs] * 4, shared_block],
        out_shape=jax.ShapeDtypeStruct((rows, D), bf16),
        grid=(1,),
        in_specs=pair_specs(D)
        + [whole_spec((rows, D)), whole_spec((1, D))]
        + [whole_spec((rows, SLAB))] * 2
        + [whole_spec((rows, WIDE))] * 3
        + of_owner
        + [pl.BlockSpec((D, 384), lambda i, *scalars: (0, 0))],
        out_specs=whole_spec((rows, D)),
        name="input_backward",
        far=True,
    )


MATRIX_RATE = 0.5 * D ** (-0.5)
OUTPUT_RATE = 0.5 * OUT_FAN ** (-0.5)
FEED_RATE = 0.5 * FF ** (-0.5)


def adam_step(weight, first, second, average, gradient, step_rate, decay_rate):
    first_new = beta_first * first + (1.0 - beta_first) * gradient
    second_new = beta_second * second + (1.0 - beta_second) * gradient * gradient
    corrected_first = first_new / (1.0 - beta_first**STEP)
    corrected_second = second_new / (1.0 - beta_second**STEP)
    weight_new = weight - step_rate * (
        corrected_first / (jnp.sqrt(corrected_second) + adam_eps) + decay_rate * weight
    )
    average_new = average_keep * average + (1.0 - average_keep) * weight_new
    return (first_new, second_new, weight_new, average_new)


def adam_steps(count):
    return count // 24 if count % 24 == 0 else 1


def feed_adam_body(grad_ref, *refs):
    in_state, ffn_state, in_outs, ffn_outs, term_ref = refs[:4], refs[4:8], refs[8:13], refs[13:18], refs[18]
    width = ffn_state[0].shape[1]

    def total(part):
        return grad_ref[:, part * width : (part + 1) * width].astype(f32)

    term = 0.0
    for half in range(2):
        gradient = total(half)
        state = [ref[:, half, :] for ref in in_state]
        term = term + jnp.sum(state[0].astype(bf16).astype(f32) * gradient, axis=1, keepdims=True)
        for ref, value in zip(in_outs, (gradient,) + adam_step(*state, gradient, MATRIX_RATE, 0.1)):
            ref[:, half, :] = value
    gradient = total(2)
    state = [ref[...] for ref in ffn_state]
    for ref, value in zip(ffn_outs, (gradient,) + adam_step(*state, gradient, FEED_RATE, 0.1)):
        ref[...] = value
    high = term.astype(bf16).astype(f32)
    lane = lax.broadcasted_iota(jnp.int32, term_ref.shape, 1)
    term_ref[...] = jnp.where(lane == 0, high, jnp.where(lane == 1, term - high, 0.0)).astype(bf16)


def feed_adam(gradient, in_state, ffn_state):
    rows, width = ffn_state[0].shape
    steps = adam_steps(rows)
    each = rows // steps
    flat = lambda columns: pl.BlockSpec((each, columns), lambda i: (i, 0))
    pair = pl.BlockSpec((each, 2, width), lambda i: (i, 0, 0))
    outs = kernel_call(
        feed_adam_body,
        [],
        [gradient, *in_state, *ffn_state],
        out_shape=[jax.ShapeDtypeStruct((rows, 2, width), f32)] * 5
        + [jax.ShapeDtypeStruct((rows, width), f32)] * 5
        + [jax.ShapeDtypeStruct((rows, 128), bf16)],
        grid=(steps,),
        in_specs=[flat(3 * width)] + [pair] * 4 + [flat(width)] * 4,
        out_specs=[pair] * 5 + [flat(width)] * 5 + [flat(128)],
        name="feed_adam",
        far=True,
    )
    return outs[:10], outs[10]


def attn_adam_body(t_ref, group_ref, *refs):
    pieces, query_state, keyval_state, output_state, gain_state = (
        refs[:4], refs[4:8], refs[8:12], refs[12:16], refs[16:20],
    )
    query_outs, keyval_outs, output_outs, gain_outs = refs[20:25], refs[25:30], refs[30:35], refs[35:40]
    query_grad, keyval_grad, output_grad, column = refs[40:]
    step, t = pl.program_id(0), t_ref[0]
    count = pieces[0].shape[0]

    @pl.when(step == 0)
    def _():
        column[...] = jnp.zeros_like(column)
        total_query, total_keyval = 0.0, 0.0
        quarters = []
        for quarter in range(4):
            here = pieces[0][:, :128]
            for k in (1, 2, 3):
                here = jnp.where((t ^ k) == quarter, pieces[k][:, :128], here)
            quarters.append(here)
        shared = jnp.concatenate(quarters, axis=1)
        for k in range(5):
            group = KV - 1 if k == 4 else t ^ k
            block = shared if k == 4 else pieces[k][:, 128 : 128 + WIDE]
            query_at, key_at = slab_target(group, group_ref)
            slab = block[:, :SLAB]
            total_query = total_query + dot_nt(slab, pick(NQ * HD, query_at))
            total_keyval = total_keyval + dot_nt(slab, pick(2 * KV * HD, key_at))
            turned = dot_nt(unit(HEADW), block[:, SLAB:])
            for which in range(GROUP):
                at = pl.multiple_of(head_of(group, which, group_ref) * HD, HD)
                output_grad[pl.ds(at, HD), :] = turned[which * HD : (which + 1) * HD, :]
        query_grad[...] = total_query
        keyval_grad[...] = total_keyval

    each = query_state[0].shape[0]
    here = pl.ds(pl.multiple_of(step * each, 8), each) if each < count else slice(0, count)
    out_each = output_state[0].shape[0]
    out_here = pl.ds(pl.multiple_of(step * out_each, 8), out_each)
    term = 0.0
    for state_refs, outs, gradient, rate in (
        (query_state, query_outs, query_grad[here, :], MATRIX_RATE),
        (keyval_state, keyval_outs, keyval_grad[here, :], MATRIX_RATE),
        (output_state, output_outs, output_grad[out_here, :], OUTPUT_RATE),
    ):
        state = [ref[...] for ref in state_refs]
        if rate == MATRIX_RATE:
            term = term + jnp.sum(state[0].astype(bf16).astype(f32) * gradient, axis=1, keepdims=True)
        for ref, value in zip(outs, (gradient,) + adam_step(*state, gradient, rate, 0.1)):
            ref[...] = value
    lane = lax.broadcasted_iota(jnp.int32, (each, 128), 1)
    column[here, :] = jnp.where(lane == 0, term, 0.0)

    @pl.when(step == pl.num_programs(0) - 1)
    def _():
        second = 0.0
        for piece in pieces:
            second = second + piece[:, 128 + WIDE :].astype(f32)
        second = jnp.sum(second, axis=1, keepdims=True)
        lane = lax.broadcasted_iota(jnp.int32, (count, 128), 1)
        column[:count, :] = jnp.where(lane == 1, second, column[:count, :])
        terms = jnp.transpose(column[...])[:2, :count]
        state = [ref[...] for ref in gain_state]
        gradient = terms / state[0]
        for ref, value in zip(gain_outs, (gradient,) + adam_step(*state, gradient, 0.3, 0.0)):
            ref[...] = value


def attn_adam(t, query_group, pieces, query_state, keyval_state, output_state, gain_state):
    rows = query_state[0].shape[0]
    steps = adam_steps(rows)
    states = (query_state, keyval_state, output_state)
    specs = [
        pl.BlockSpec((x[0].shape[0] // steps, x[0].shape[1]), lambda i, *scalars: (i, 0)) for x in states
    ] + [whole_spec(gain_state[0].shape)]
    states = states + (gain_state,)
    outs = kernel_call(
        attn_adam_body,
        [t, query_group],
        [*pieces, *[x for state in states for x in state]],
        out_shape=[jax.ShapeDtypeStruct(state[0].shape, f32) for state in states for _ in range(5)],
        grid=(steps,),
        in_specs=[whole_spec(pieces[0].shape)] * 4 + [spec for spec in specs for _ in range(4)],
        out_specs=[spec for spec in specs for _ in range(5)],
        scratch_shapes=[
            pltpu.VMEM((rows, NQ * HD), f32), pltpu.VMEM((rows, 2 * KV * HD), f32), pltpu.VMEM((NQ * HD, rows), f32),
            pltpu.VMEM((128, 128), f32),
        ],
        name="attn_adam",
        far=True,
    )
    return outs[:5], outs[5:10], outs[10:15], outs[15:20]


def local(
    tokens, cotangent, lengths, valid, query_group,
    w_query, w_keyval, w_output, w_ffn_in, w_ffn_out, norm_gains,
    first_query, first_keyval, first_output, first_ffn_in, first_ffn_out, first_gains,
    second_query, second_keyval, second_output, second_ffn_in, second_ffn_out, second_gains,
    average_query, average_keyval, average_output, average_ffn_in, average_ffn_out, average_gains,
):
    t = lax.axis_index("tensor").astype(jnp.int32)
    t_array = t.reshape(1)
    row_count = tokens.shape[0]
    owned_rows = w_query.shape[0]
    hidden_count = w_ffn_out.shape[0]

    me = lax.axis_index("dp").astype(jnp.int32).reshape(1)
    small = lax.axis_size("dp") == 8
    rest_rows = 8 if owned_rows % 8 == 0 else 17
    own_part = prepare(t_array, query_group, w_query, w_keyval, w_output, norm_gains, owned_rows + rest_rows)
    own_one = gather_one(own_part)
    length_row = lengths[0]
    seq_ends = jnp.cumsum(length_row)
    valid, seq_ends = after((valid, seq_ends), own_part)
    row_index = jnp.arange(row_count, dtype=jnp.int32)
    row_start = jnp.where(
        row_index >= seq_ends[1], seq_ends[1], jnp.where(row_index >= seq_ends[0], seq_ends[0], 0)
    )
    position = (row_index - row_start).astype(f32)
    frequency = rope_base ** (-jnp.arange(0, HD, 2, dtype=f32) / HD)
    angles = position[:, None] * jnp.tile(frequency, 4)[None, :]
    cosine, sine = jnp.cos(angles), jnp.sin(angles)
    valid_wide = jnp.broadcast_to(valid[:, None], (row_count, 128))
    tables = (cosine, sine, valid_wide)

    own_two = gather_two(after(own_one, tables))
    w_in_now, w_out_now = after((w_ffn_in, w_ffn_out), (own_one, tables))
    feed_part = jnp.concatenate(
        [w_in_now[:, 0].astype(bf16), w_in_now[:, 1].astype(bf16), jnp.transpose(w_out_now).astype(bf16)], axis=1
    )
    feed_all = lax.all_gather(feed_part, "dp", axis=0, tiled=True)

    own_cotangent = own_order(after(cotangent, feed_part), t_array)
    slab_own, out_own, quarter, rest = gather_end(after(own_two, own_cotangent), owned_rows)
    quarters = gather_first(quarter)
    parts = jnp.swapaxes(rest[:, :6, :owned_rows].astype(f32), 0, 1).reshape(6, D)
    gains = parts[0:2] + parts[2:4] + parts[4:6]
    gain_one, gain_two = gains[0:1], gains[1:2]

    normed_one, q_own, k_own, v_own = project(length_row, tokens, after(gain_one, quarters[1]), slab_own, cosine, sine, valid_wide)
    out_owns = gather_first(after(out_own, normed_one))
    blocks = jnp.arange(row_count // KEYS, dtype=jnp.int32)
    part_blocks = jnp.stack([t, 7 - t])
    q_own = after(q_own, out_owns[1])
    att_own, log_own = attend_forward(length_row, blocks, KEYS, q_own, k_own, v_own)
    att_owns = gather_first(att_own)
    quarters, out_owns = after((quarters, out_owns), att_own)
    quarters, out_owns = gather_second(quarters), gather_second(out_owns)
    shared_block = assemble(t_array, after(quarters, att_owns[1]))
    q_part, k_part, v_part = project(length_row, normed_one, None, shared_block, cosine, sine, valid_wide)
    att_part, log_part = attend_forward(length_row, part_blocks, PIECE, q_part, k_part, v_part)
    att_shares = [att_part] + exchange_tensor([att_part] * 3)
    att_owns = gather_second(after(att_owns, att_shares[1]))
    weights = out_owns + [shared_block]
    slabs = lax.all_gather(after(slab_own, (att_owns[2], out_owns[2])), "tensor", axis=0)
    middle_mine, normed_two = out_project(t_array, tokens, gain_two, att_owns, att_shares, weights)
    hidden, d_gate_up, two_kept, two_sent, terms_kept, terms_sent = feed_forward(
        normed_two, own_cotangent, after(feed_all, normed_two)
    )

    two_came = swap(two_sent, "tensor", 1)
    terms_came = swap(terms_sent, "tensor", 1)
    two_near, two_far = near_far(two_kept, two_came)
    two_far = swap(two_far, "tensor", 2)

    feed_grad = feed_grads(after(normed_two, two_near), own_cotangent, d_gate_up, hidden)

    own_rows = 2 * PIECE
    d_middle, d_branch, d_att_part = middle_backward(
        two_near, after(two_far, (feed_grad, slabs)), middle_mine, own_cotangent, gain_two, shared_block
    )
    feed_sum = lax.psum_scatter(after(feed_grad, two_far), "dp", scatter_dimension=0, tiled=True)
    branches = gather_first(d_branch)
    d_shared, shared_mine = attend_backward_shared(
        t_array, length_row, part_blocks, q_part, k_part, v_part, log_part, att_part,
        after(d_att_part, branches[1]), cosine, sine,
    )
    terms_near, terms_far = near_far(terms_kept, after(terms_came, d_shared))
    early_kept, early_sent = early_grads(t_array, d_branch, att_part, normed_one, after(d_shared, terms_near))
    early_near, early_far = near_far(early_kept, swap(early_sent, "tensor", 1))
    early_far = swap(early_far, "tensor", 2)
    branches = gather_second(after(branches, early_near))
    terms_far = swap(after(terms_far, branches[2]), "tensor", 2)
    d_own, *own_sent, own_mine = attend_backward_own(
        t_array, length_row, q_own, k_own, v_own, log_own, att_own, branches, out_own, cosine, sine, d_shared
    )
    own_came = exchange_tensor(own_sent)
    layer_mine = layer_rows(middle_mine, terms_near, after(terms_far, (d_own, early_far)))
    d_own = after(d_own, layer_mine)
    if small:
        attn_half = scatter_one(
            *attn_grads(
                me, t_array, normed_one, d_own, early_near, early_far, branches, att_own
            )
        )
    else:
        early = early_near + early_far.astype(f32)
        out_grad = 0.0
        for k in range(4):
            rows_of = [jnp.where(t >= 0, t ^ k, 0), 3 - (t ^ k)]
            low, high = (lax.dynamic_slice_in_dim(att_own, PIECE * at, PIECE, 0) for at in rows_of)
            out_grad = out_grad + dot_tn(branches[k], unpack(low, high))
        attn_half = (jnp.concatenate([early, dot_tn(normed_one, d_own), out_grad], axis=1),)
    layer_pieces = gather_tensor(layer_mine)
    attn_quarter = scatter_two(after(attn_half, layer_pieces))
    grad_mine = input_backward(
        t_array, tokens, d_middle, gain_one, own_mine, shared_mine, after(own_came, attn_quarter[0]), slabs, shared_block
    )
    grad_pieces = gather_first(grad_mine)
    layer_out = natural_order(after(layer_pieces, grad_mine), t_array)

    feed_results, gain_term = feed_adam(
        after(feed_sum, layer_out),
        (w_ffn_in, first_ffn_in, second_ffn_in, average_ffn_in),
        [jnp.transpose(x) for x in (w_ffn_out, first_ffn_out, second_ffn_out, average_ffn_out)],
    )
    in_results, out_results = feed_results[:5], [jnp.transpose(x) for x in feed_results[5:]]
    owned_attn = jnp.concatenate([scatter_end(after(attn_quarter, gain_term)).astype(bf16), gain_term], axis=1)
    attn_first = gather_first(owned_attn)
    input_grad = natural_order(gather_second(after(grad_pieces, attn_first[1])), t_array)
    attn_pieces = gather_second(after(attn_first, input_grad))
    query_results, keyval_results, output_results, gain_results = attn_adam(
        t_array, query_group, attn_pieces,
        (w_query, first_query, second_query, average_query),
        (w_keyval, first_keyval, second_keyval, average_keyval),
        (w_output, first_output, second_output, average_output),
        (norm_gains, first_gains, second_gains, average_gains),
    )
    results = (query_results, keyval_results, output_results, in_results, out_results, gain_results)
    return (layer_out, input_grad) + tuple(result[part] for part in range(5) for result in results)


def solution(mesh):
    token, rows, columns = P("dp", None), P("dp", None), P(None, "dp")
    weight_specs = (rows, rows, columns, P("dp", None, "tensor"), P("tensor", "dp"), columns)
    in_specs = (token, token, P("dp", None), P("dp"), P()) + weight_specs * 4
    out_specs = (token, token) + weight_specs * 5
    return jax.shard_map(local, mesh=mesh, in_specs=in_specs, out_specs=out_specs, check_vma=False)
```

```python
import functools

import jax
import jax.numpy as jnp
import numpy as np
from jax import lax
from jax.experimental import pallas as pl
from jax.experimental.layout import Layout, with_layout_constraint
from jax.experimental.pallas import tpu as pltpu
from jax.sharding import PartitionSpec as P

D = 960
FF = 2560
NQ = 15
KV = 5
HD = 64
STEP = 10
GROUP = 3
OUT_FAN = 3
SLAB = 320
HEADW = GROUP * HD
WIDE = SLAB + HEADW
PIECE = 160
KEYS = 256

norm_eps = 1e-05
rope_base = 10000.0
beta_first = 0.5
beta_second = 0.5
adam_eps = 1e-08
average_keep = 0.5
bf16 = jnp.bfloat16
f32 = jnp.float32
VMEM_LIMIT = 48 * 1024 * 1024


def params(*semantics):
    return pltpu.CompilerParams(dimension_semantics=semantics, vmem_limit_bytes=VMEM_LIMIT)


def by_rows(x):
    return with_layout_constraint(x, Layout(major_to_minor=tuple(range(x.ndim))))


def swap(x, axis, offset):
    count = lax.axis_size(axis)
    return by_rows(lax.ppermute(by_rows(x), axis, [(i, i ^ offset) for i in range(count)]))


def dot_nn(a, b):
    return lax.dot_general(a, b, (((1,), (0,)), ((), ())), preferred_element_type=f32)


def dot_nt(a, b):
    return lax.dot_general(a, b, (((1,), (1,)), ((), ())), preferred_element_type=f32)


def dot_tn(a, b):
    return lax.dot_general(a, b, (((0,), (0,)), ((), ())), preferred_element_type=f32)


TIMES = {
    "prepare": 2.5, "place": 3.5, "assemble": 1.0, "own_order": 1.0, "natural_order": 2.5, "project": 4.5,
    "attend_forward": 8.0, "out_project": 10.0, "feed_forward": 20.0, "feed_grads": 0.0, "far_part": 1.0, "half_sums": 2.0,
    "middle_backward": 4.5, "attend_backward_shared": 5.5, "early_grads": 6.5, "attend_backward_own": 18.0,
    "attn_grads": 5.0, "layer_rows": 1.5, "feed_adam": 5.0, "attn_adam": 6.0, "input_backward": 0.0,
}


def kernel_call(body, scalars, arrays, *, out_shape, grid, in_specs, out_specs, scratch_shapes=(), name, far=False, far_out=False):
    single = not isinstance(out_shape, (list, tuple))
    shapes = [out_shape] if single else out_shape
    call = pl.pallas_call(
        body,
        out_shape=[pltpu.HBM(shape.shape, shape.dtype) for shape in shapes] if far_out else shapes,
        grid_spec=pltpu.PrefetchScalarGridSpec(
            num_scalar_prefetch=len(scalars),
        grid=grid,
        in_specs=in_specs,
        out_specs=[out_specs] if single else out_specs,
        scratch_shapes=scratch_shapes,
        ),
        compiler_params=params("arbitrary"),
        cost_estimate=pl.CostEstimate(flops=0, bytes_accessed=int(TIMES[name] * 3.2e6), transcendentals=0),
        name=name,
    )
    if far:
        arrays = [pltpu.with_memory_space_constraint(x, pltpu.HBM) for x in arrays]
    outs = call(*scalars, *arrays)
    return outs[0] if single else outs


def after(values, *earlier):
    return lax.optimization_barrier((values, earlier))[0]


def turn(k):
    return (k & 1) * 2 + k // 2


def place_of(block, t):
    owner = jnp.minimum(block, 7 - block)
    return 2 * turn(owner ^ t) + (block > 3).astype(jnp.int32)


def place_body(index_ref, *refs):
    pieces, (slab_ref, out_ref, quarter_ref, gains_ref, rest) = refs[:-5], refs[-5:]
    rows = slab_ref.shape[1]
    half = len(pieces) // 2
    for slot, piece in enumerate(pieces):
        at = index_ref[slot]
        slab_ref[at] = piece[:rows, : slab_ref.shape[2]]
        quarter_ref[at] = piece[:rows, WIDE:]
        parts = piece[rows:, :128].astype(f32)
        rest[at] = parts[0:2] + parts[2:4] + parts[4:6]
        out = piece[:rows, SLAB:WIDE]

        @pl.when(at < half)
        def _():
            out_ref[at, :, :HEADW] = out

        @pl.when(at >= half)
        def _():
            out_ref[at - half, :, HEADW:] = out

    gains_ref[...] = jnp.concatenate([rest[j][:, :rows] for j in range(len(pieces))], axis=1)


def place(pieces, index, rows):
    count = len(pieces)
    shapes = [(count, rows, 384), (count // 2, rows, 2 * HEADW), (count, rows, 128)]
    return kernel_call(
        place_body,
        [index],
        pieces,
        out_shape=[jax.ShapeDtypeStruct(shape, pieces[0].dtype) for shape in shapes]
        + [jax.ShapeDtypeStruct((2, count * rows), f32)],
        grid=(1,),
        in_specs=[whole_spec(pieces[0].shape)] * count,
        out_specs=[whole_spec(shape) for shape in shapes] + [whole_spec((2, count * rows))],
        scratch_shapes=[pltpu.VMEM((count, 2, 128), f32)],
        name="place",
        far=True,
        far_out=True,
    )


def assemble_body(t_ref, *refs):
    for k in range(4):
        at = pl.multiple_of((t_ref[0] ^ k) * 128, 128)
        refs[4][:, pl.ds(at, 128)] = refs[k][...]


def assemble(t, pieces):
    rows = pieces[0].shape[0]
    return kernel_call(
        assemble_body,
        [t],
        pieces,
        out_shape=jax.ShapeDtypeStruct((rows, WIDE), bf16),
        grid=(1,),
        in_specs=[whole_spec((rows, 128))] * 4,
        out_specs=whole_spec((rows, WIDE)),
        name="assemble",
    )


def reorder_body(t_ref, x_ref, out_ref):
    out_ref[...] = x_ref[...]


def own_order(x, t):
    width = x.shape[1]
    owner = lambda p, t_ref: t_ref[0] ^ turn(p // 2)
    return kernel_call(
        reorder_body,
        [t],
        [x],
        out_shape=jax.ShapeDtypeStruct(x.shape, x.dtype),
        grid=(8,),
        in_specs=[
                pl.BlockSpec(
                    (PIECE, width),
                    lambda p, t_ref: (jnp.where(p % 2 == 0, owner(p, t_ref), 7 - owner(p, t_ref)), 0),
                )
            ],
        out_specs=pl.BlockSpec((PIECE, width), lambda p, t_ref: (p, 0)),
        name="own_order",
    )


def natural_body(t_ref, *refs):
    half, t = pl.program_id(0), t_ref[0]
    pieces, out_ref = refs[:4], refs[4]
    parts = []
    for block in range(4):
        owner = jnp.where(half == 0, block, 3 - block)
        part = pieces[0][...]
        for k in (1, 2, 3):
            part = jnp.where((owner ^ t) == k, pieces[k][...], part)
        parts.append(part)
    out_ref[...] = jnp.transpose(jnp.concatenate(parts, axis=0))


def natural_order(pieces, t):
    width = pieces[0].shape[1]
    turned = kernel_call(
        natural_body,
        [t],
        pieces,
        out_shape=jax.ShapeDtypeStruct((width, 8 * PIECE), pieces[0].dtype),
        grid=(2,),
        in_specs=[pl.BlockSpec((PIECE, width), lambda b, t_ref: (b, 0))] * 4,
        out_specs=pl.BlockSpec((width, 4 * PIECE), lambda b, t_ref: (0, b)),
        name="natural_order",
        far=True,
    )
    return jnp.transpose(turned)


def gather_one(x):
    if lax.axis_size("dp") != 8:
        return [x]
    return [x] + [swap(x, "dp", k) for k in (2, 4, 6)]


def gather_two(pieces):
    if len(pieces) == 1:
        return pieces
    return pieces + [swap(piece, "dp", 1) for piece in pieces]


def gather_end(pieces, rows):
    if len(pieces) == 1:
        both = lax.all_gather(pieces[0], "dp", axis=0)
        whole = both[:, :rows].reshape(D, WIDE + 128)
        out = whole[:, SLAB:WIDE]
        parts = jnp.swapaxes(both[:, rows : rows + 6, :rows].astype(f32), 0, 1).reshape(6, D)
        gains = parts[0:2] + parts[2:4] + parts[4:6]
        return whole[:, :384], jnp.concatenate([out[: D // 2], out[D // 2 :]], axis=1), whole[:, WIDE:], gains
    me = lax.axis_index("dp")
    index = jnp.stack([me ^ k for k in (0, 2, 4, 6, 1, 3, 5, 7)]).astype(jnp.int32)
    slab, out, quarter, gains = place(pieces, index, rows)
    return slab.reshape(D, 384), out.reshape(D // 2, 2 * HEADW), quarter.reshape(D, 128), gains


def scatter_one(kept, sent):
    if sent is None:
        return (kept,)
    return kept, swap(sent, "dp", 1)


def scatter_two(halves):
    if len(halves) == 1:
        return halves
    mine, *sent = half_sums(lax.axis_index("dp").astype(jnp.int32).reshape(1), *halves)
    return [mine] + [swap(piece, "dp", 2 * (k + 1)) for k, piece in enumerate(sent)]


def scatter_end(quarters):
    if len(quarters) == 1:
        return lax.psum_scatter(quarters[0].astype(f32), "dp", scatter_dimension=0, tiled=True)
    return sum(quarter.astype(f32) for quarter in quarters)


def half_body(me_ref, kept_ref, came_ref, mine_ref, *sent_refs):
    at_z = me_ref[0] >> 1
    mine_ref[...] = kept_ref[at_z].astype(f32) + came_ref[at_z].astype(f32)
    for k, sent_ref in enumerate(sent_refs):
        at = at_z ^ (k + 1)
        sent_ref[...] = (kept_ref[at].astype(f32) + came_ref[at].astype(f32)).astype(bf16)


def half_sums(me, kept, came):
    count, rows, columns = kept.shape
    return kernel_call(
        half_body,
        [me],
        [kept, came],
        out_shape=[jax.ShapeDtypeStruct((rows, columns), f32)]
        + [jax.ShapeDtypeStruct((rows, columns), bf16)] * (count - 1),
        grid=(1,),
        in_specs=[whole_spec(kept.shape)] * 2,
        out_specs=[whole_spec((rows, columns))] * count,
        name="half_sums",
    )


def split_chunks(me_ref, chunks, kept_ref, sent_ref):
    at_y = (me_ref[0] & 1) == 0
    for z in range(len(chunks) // 2):
        even, odd = chunks[2 * z].astype(bf16), chunks[2 * z + 1].astype(bf16)
        kept_ref[z] = jnp.where(at_y, even, odd)
        sent_ref[z] = jnp.where(at_y, odd, even)


def gather_first(x):
    across = swap(x, "tensor", 2)
    return [x, swap(x, "tensor", 1), across]


def gather_second(pieces):
    return pieces + [swap(pieces[2], "tensor", 1)]


def gather_tensor(x):
    return gather_second(gather_first(x))


def exchange_tensor(pieces):
    return [swap(piece, "tensor", k + 1) for k, piece in enumerate(pieces)]


def slab_target(group, group_ref):
    lane = lax.broadcasted_iota(jnp.int32, (1, SLAB), 1)
    second = lane >= 128
    value = lane >= 256
    within = jnp.where(second, lane - 128, lane)
    inside = (within & 31) + jnp.where(second, 32, 0)
    member = within >> 5
    query_at = jnp.full_like(lane, -1)
    for which in range(GROUP):
        query_at = jnp.where(member == which, head_of(group, which, group_ref) * HD + inside, query_at)
    query_at = jnp.where(value, -1, query_at)
    key_at = jnp.where(member == GROUP, group * HD + inside, -1)
    key_at = jnp.where(value, KV * HD + group * HD + lane - 256, key_at)
    return query_at, key_at


def head_of(group, which, group_ref):
    slot = group * GROUP + which
    head = jnp.int32(0)
    for h in range(NQ):
        head = jnp.where(group_ref[h] == slot, h, head)
    return head


def pick(width, index):
    rows = lax.broadcasted_iota(jnp.int32, (width, index.shape[1]), 0)
    return jnp.where(rows == index, 1.0, 0.0).astype(bf16)


def unit(count):
    rows = lax.broadcasted_iota(jnp.int32, (count, count), 0)
    return jnp.where(rows == lax.broadcasted_iota(jnp.int32, (count, count), 1), 1.0, 0.0).astype(bf16)


def prep_body(t_ref, index_ref, query_ref, keyval_ref, output_ref, gains_ref, out_ref):
    count = query_ref.shape[0]
    query, keyval = query_ref[...].astype(bf16), keyval_ref[...].astype(bf16)

    def block(group):
        query_at, key_at = slab_target(group, index_ref)
        picked = dot_nn(query, pick(NQ * HD, query_at)) + dot_nn(keyval, pick(2 * KV * HD, key_at))
        heads = [
            output_ref[pl.ds(pl.multiple_of(head_of(group, which, index_ref) * HD, HD), HD), :] for which in range(GROUP)
        ]
        turned = dot_nt(unit(count), jnp.concatenate(heads, axis=0).astype(bf16))
        return jnp.concatenate([picked, turned], axis=1)

    t = t_ref[0]
    shared = block(KV - 1)
    quarter = shared[:, :128]
    for k in (1, 2, 3):
        quarter = jnp.where(t == k, shared[:, 128 * k : 128 * (k + 1)], quarter)
    out_ref[:count, :] = jnp.concatenate([block(t), quarter], axis=1).astype(bf16)
    missing = out_ref.shape[0] - count
    gains = gains_ref[...]
    high = gains.astype(bf16).astype(f32)
    middle = (gains - high).astype(bf16).astype(f32)
    low = gains - high - middle
    rest = jnp.concatenate([high, middle, low, jnp.zeros((missing - 6, count), f32)], axis=0)
    rest = jnp.concatenate([rest, jnp.zeros((missing, WIDE + 128 - count), f32)], axis=1)
    out_ref[count:, :] = rest.astype(bf16)


def prepare(t, query_group, w_query, w_keyval, w_output, norm_gains, rows):
    return kernel_call(
        prep_body,
        [t, query_group],
        [w_query, w_keyval, w_output, norm_gains],
        out_shape=jax.ShapeDtypeStruct((rows, WIDE + 128), bf16),
        grid=(1,),
        in_specs=[whole_spec(x.shape) for x in (w_query, w_keyval, w_output, norm_gains)],
        out_specs=whole_spec((rows, WIDE + 128)),
        name="prepare",
        far=True,
    )


def pair_specs(width):
    owner = lambda p, t_ref: t_ref[0] ^ turn(p)
    return [
        pl.BlockSpec((PIECE, width), lambda p, t_ref: (owner(p, t_ref), 0)),
        pl.BlockSpec((PIECE, width), lambda p, t_ref: (7 - owner(p, t_ref), 0)),
    ]


def packed_specs():
    owner = lambda p, t_ref: t_ref[0] ^ turn(p)
    return [
        pl.BlockSpec((PIECE, 2 * HEADW), lambda p, t_ref: (owner(p, t_ref), 0)),
        pl.BlockSpec((PIECE, 2 * HEADW), lambda p, t_ref: (3 - owner(p, t_ref), 0)),
    ]


def unpack(low, high):
    return jnp.concatenate([low[:, :HEADW], high[:, HEADW:]], axis=0)


def pack(pair):
    rows = pair.shape[0] // 2
    return jnp.concatenate([pair[:rows], pair[rows:]], axis=1)


def split_heads(normed, w_ref, cosine, sine, guard, q_ref, k_ref, v_ref):
    y = dot_nn(normed, w_ref[:, :SLAB])
    first, second = y[:, :128], y[:, 128:256]
    turned_first = first * cosine - second * sine
    turned_second = second * cosine + first * sine
    for head in range(GROUP + 1):
        columns = slice(32 * head, 32 * head + 32)
        both = jnp.concatenate([turned_first[:, columns], turned_second[:, columns]], axis=1)
        if head < GROUP:
            both = both.astype(bf16).astype(f32) * HD ** (-0.5)
            q_ref[head] = jnp.concatenate([both, guard[:, :HD]], axis=1).astype(bf16)
        else:
            k_ref[...] = jnp.concatenate([both, guard[:, HD:]], axis=1).astype(bf16)
    v_ref[...] = y[:, 256:].astype(bf16)


def guards(length_ref, valid_ref, rows):
    row = pl.program_id(0) * rows + lax.broadcasted_iota(jnp.int32, (rows, 128), 0)
    lane = lax.broadcasted_iota(jnp.int32, (rows, 128), 1)
    end_one = length_ref[0]
    end_two = end_one + length_ref[1]
    sequence = (row >= end_one).astype(jnp.int32) + (row >= end_two).astype(jnp.int32)
    query = jnp.where((lane == sequence) | (lane == 3), 1.0, 0.0)
    shut = ((lane >= HD) & (lane < HD + 3) & (lane - HD != sequence)) | ((lane == HD + 3) & (valid_ref[...] != 1))
    return jnp.where(lane < HD, query, jnp.where(shut, -(2.0**100), 0.0))


def proj_own_body(length_ref, x_ref, gain_ref, w_ref, cos_ref, sin_ref, valid_ref, normed_ref, q_ref, k_ref, v_ref):
    x = x_ref[...].astype(f32)
    factor = lax.rsqrt(jnp.mean(x * x, axis=-1, keepdims=True) + norm_eps)
    normed = (x * factor * gain_ref[0:1, :]).astype(bf16)
    normed_ref[...] = normed
    guard = guards(length_ref, valid_ref, x.shape[0])
    split_heads(normed, w_ref, cos_ref[...], sin_ref[...], guard, q_ref, k_ref, v_ref)


def proj_shared_body(length_ref, normed_ref, w_ref, cos_ref, sin_ref, valid_ref, q_ref, k_ref, v_ref):
    guard = guards(length_ref, valid_ref, normed_ref.shape[0])
    split_heads(normed_ref[...], w_ref, cos_ref[...], sin_ref[...], guard, q_ref, k_ref, v_ref)


def project(lengths, x, gain, weight, cosine, sine, valid):
    rows = x.shape[0]
    step = 2 * PIECE
    by_step = lambda width: pl.BlockSpec((step, width), lambda i, *scalars: (i, 0))
    outs = [
        (jax.ShapeDtypeStruct((GROUP, rows, 128), bf16), pl.BlockSpec((GROUP, step, 128), lambda i, *scalars: (0, i, 0))),
        (jax.ShapeDtypeStruct((rows, 128), bf16), by_step(128)),
        (jax.ShapeDtypeStruct((rows, HD), bf16), by_step(HD)),
    ]
    if gain is not None:
        outs = [(jax.ShapeDtypeStruct(x.shape, bf16), by_step(D))] + outs
    gains = [] if gain is None else [gain]
    return kernel_call(
        proj_shared_body if gain is None else proj_own_body,
        [lengths],
        [x, *gains, weight, cosine, sine, valid],
        out_shape=[shape for shape, _ in outs],
        grid=(rows // step,),
        in_specs=[by_step(D)]
        + [whole_spec((2, D))] * len(gains)
        + [whole_spec(weight.shape), by_step(128), by_step(128), by_step(128)],
        out_specs=[spec for _, spec in outs],
        name="project",
        far=True,
        far_out=True,
    )


def lanes_of(rows):
    return -(-GROUP * rows // 128) * 128


def start_of(row, length_ref):
    end_one = length_ref[0]
    end_two = end_one + length_ref[1]
    return jnp.where(row >= end_two, end_two, jnp.where(row >= end_one, end_one, 0))


def lane_rows(block, rows, length_ref):
    lane = lax.broadcasted_iota(jnp.int32, (1, lanes_of(rows)), 1)
    head = sum((lane >= h * rows).astype(jnp.int32) for h in range(1, GROUP + 1))
    row = jnp.where(head < GROUP, block * rows + lane - head * rows, 1 << 20)
    return row, jnp.where(head < GROUP, start_of(row, length_ref), 1 << 20)


def key_range(block, rows, length_ref):
    first = start_of(block * rows, length_ref) // KEYS
    return first, (block * rows + rows + KEYS - 1) // KEYS


def key_mask(shut, at, row, start):
    index = at + lax.broadcasted_iota(jnp.int32, (KEYS, row.shape[1]), 0)
    return ((index >= start) & (index <= row) & (shut == 0.0)) | (index == row)


def fill(stacked, lanes):
    parts = [stacked[head] for head in range(GROUP)]
    missing = lanes - GROUP * stacked[0].shape[0]
    if missing:
        parts.append(jnp.zeros((missing, parts[0].shape[1]), bf16))
    return jnp.concatenate(parts, axis=0)


def forward_body(length_ref, block_ref, q_ref, k_ref, v_ref, out_ref, log_ref, acc):
    rows = q_ref.shape[1]
    lanes = acc.shape[1]
    block = block_ref[pl.program_id(0)]
    q = fill(q_ref[...], lanes)
    row, start = lane_rows(block, rows, length_ref)
    acc[...] = jnp.zeros_like(acc)

    def step(carry, here, scores):
        peak, total = carry
        new_peak = jnp.maximum(peak, jnp.max(scores, axis=0, keepdims=True))
        exponent = jnp.exp(scores - new_peak)
        shrink = jnp.exp(peak - new_peak)
        total = total * shrink + jnp.sum(exponent, axis=0, keepdims=True)
        acc[...] = acc[...] * shrink + dot_tn(v_ref[here, :], exponent.astype(bf16))
        return new_peak, total

    def before(j, carry):
        here = pl.ds(pl.multiple_of(j * KEYS, KEYS), KEYS)
        return step(carry, here, dot_nt(k_ref[here, :], q))

    def across(j, carry):
        at = pl.multiple_of(j * KEYS, KEYS)
        here = pl.ds(at, KEYS)
        scores = dot_nt(k_ref[here, :HD], q[:, :HD])
        return step(carry, here, jnp.where(key_mask(k_ref[here, HD + 3 : HD + 4].astype(f32), at, row, start), scores, -1e30))

    low, high = key_range(block, rows, length_ref)
    middle = jnp.maximum(low, block * rows // KEYS)
    carry = (jnp.full((1, lanes), -1e30, f32), jnp.zeros((1, lanes), f32))
    peak, total = lax.fori_loop(middle, high, across, lax.fori_loop(low, middle, before, carry))
    log_ref[0] = peak + jnp.log(total)
    attended = jnp.transpose(acc[...] / total)
    attended = jnp.concatenate(
        [attended[head * rows : (head + 1) * rows] for head in range(GROUP)], axis=1
    ).astype(bf16)
    half = out_ref.shape[0]
    chunk = min(rows, 128) if half > rows else rows
    for part in range(rows // chunk):
        at = pl.program_id(0) * rows + part * chunk
        piece = attended[part * chunk : (part + 1) * chunk]

        @pl.when(at < half)
        def _():
            out_ref[pl.ds(pl.multiple_of(at, chunk), chunk), :HEADW] = piece

        @pl.when(at >= half)
        def _():
            out_ref[pl.ds(pl.multiple_of(at - half, chunk), chunk), HEADW:] = piece


def attend_forward(lengths, blocks, size, q, k, v):
    count, rows = blocks.shape[0], k.shape[0]
    lanes = lanes_of(size)
    return kernel_call(
        forward_body,
        [lengths, blocks],
        [q, k, v],
        out_shape=[
            jax.ShapeDtypeStruct((count * size // 2, 2 * HEADW), bf16),
            jax.ShapeDtypeStruct((count, 1, lanes), f32),
        ],
        grid=(count,),
        in_specs=[
                pl.BlockSpec((GROUP, size, 128), lambda i, lengths, blocks: (0, blocks[i], 0)),
                whole_spec((rows, 128)), whole_spec((rows, HD)),
            ],
        out_specs=[
                whole_spec((count * size // 2, 2 * HEADW)),
                pl.BlockSpec((1, 1, lanes), lambda i, *scalars: (i, 0, 0)),
            ],
        scratch_shapes=[pltpu.VMEM((HD, lanes), f32)],
        name="attend_forward",
        far=True,
        far_out=True,
    )


def backward_block(block, rows, length_ref, q, k_ref, v_ref, logs, attended, upstream, cosine, sine, dk, dv, acc):
    lanes = q.shape[0]
    row, start = lane_rows(block, rows, length_ref)
    heads = lambda wide: fill([wide[:, h * HD : (h + 1) * HD] for h in range(GROUP)], lanes)
    up = heads(upstream)
    both = up.astype(f32) * heads(attended).astype(f32)
    both_high = both.astype(bf16)
    both_low = (both - both_high.astype(f32)).astype(bf16)
    ones = jnp.ones((8, HD), bf16)
    inner = (dot_nt(ones, both_high) + dot_nt(ones, both_low))[:1]
    acc[...] = jnp.zeros_like(acc)

    heads_only = q[:, :HD]

    def step(here, scores):
        probs = jnp.exp(scores - logs)
        d_probs = dot_nt(v_ref[here, :], up)
        d_scores = (probs * (d_probs - inner)).astype(bf16)
        dv[here, :] += dot_nn(probs.astype(bf16), up)
        dk[here, :] += dot_nn(d_scores, heads_only)
        acc[...] += dot_tn(k_ref[here, :HD], d_scores)

    def before(j, carry):
        here = pl.ds(pl.multiple_of(j * KEYS, KEYS), KEYS)
        step(here, dot_nt(k_ref[here, :], q))
        return carry

    def across(j, carry):
        at = pl.multiple_of(j * KEYS, KEYS)
        here = pl.ds(at, KEYS)
        scores = dot_nt(k_ref[here, :HD], heads_only)
        step(here, jnp.where(key_mask(k_ref[here, HD + 3 : HD + 4].astype(f32), at, row, start), scores, -1e30))
        return carry

    low, high = key_range(block, rows, length_ref)
    middle = jnp.maximum(low, block * rows // KEYS)
    lax.fori_loop(low, middle, before, 0)
    lax.fori_loop(middle, high, across, 0)
    turned = jnp.transpose(acc[...] * HD ** (-0.5))
    first = jnp.concatenate([turned[h * rows : (h + 1) * rows, :32] for h in range(GROUP)], axis=1)
    second = jnp.concatenate([turned[h * rows : (h + 1) * rows, 32:] for h in range(GROUP)], axis=1)
    cosine, sine = cosine[:, :96], sine[:, :96]
    return first * cosine + second * sine, second * cosine - first * sine


def turn_back(dk, cosine, sine):
    first, second = dk[:, :32], dk[:, 32:]
    cosine, sine = cosine[:, :32], sine[:, :32]
    return first * cosine + second * sine, second * cosine - first * sine


def rows_at(block):
    return pl.ds(pl.multiple_of(block * PIECE, PIECE), PIECE)


def attended_rows(out_ref, at, rows):
    half = out_ref.shape[0]
    parts = []
    for part in range(rows // 128):
        here = at + part * 128
        low = pl.multiple_of(jnp.where(here < half, here, here - half), 128)
        both = out_ref[pl.ds(low, 128), :]
        parts.append(jnp.where(here < half, both[:, :HEADW], both[:, HEADW:]))
    return jnp.concatenate(parts, axis=0)


def backward_own_body(
    t_ref, length_ref, q_ref, k_ref, v_ref, log_ref, out_ref, up_0, up_1, up_2, up_3, weight_ref, cos_ref, sin_ref, shared_ref,
    slab_ref, *rest
):
    send_refs, mine_ref, (dk, dv, acc, upstream) = rest[:3], rest[3], rest[4:]
    rows = q_ref.shape[1]
    step = pl.program_id(0)
    t = t_ref[0]
    block = pl.num_programs(0) - 1 - step

    @pl.when(step == 0)
    def _():
        dk[...] = jnp.zeros_like(dk)
        dv[...] = jnp.zeros_like(dv)
        weight = out_weight(weight_ref)
        for k, piece in enumerate((up_0, up_1, up_2, up_3)):
            d_attended = dot_nn(piece[...], weight).astype(bf16)
            upstream[rows_at(t ^ k), :] = d_attended[:PIECE]
            upstream[rows_at(7 - (t ^ k)), :] = d_attended[PIECE:]

    cosine, sine = cos_ref[...], sin_ref[...]
    here = pl.ds(pl.multiple_of(block * rows, rows), rows)
    q = fill(q_ref[...], acc.shape[1])
    first, second = backward_block(
        block, rows, length_ref, q, k_ref, v_ref, log_ref[0], attended_rows(out_ref, block * rows, rows),
        upstream[here, :], cosine, sine, dk, dv, acc,
    )
    key_first, key_second = turn_back(dk[here, :], cosine, sine)
    slab_ref[here, :] = jnp.concatenate([first, key_first, second, key_second, dv[here, :]], axis=1).astype(bf16)

    @pl.when(step == pl.num_programs(0) - 1)
    def _():
        for half, owner in enumerate((t, 7 - t)):
            mine_ref[half * PIECE : (half + 1) * PIECE, :] = slab_ref[rows_at(owner), :]
        for k, target in enumerate(send_refs):
            for half, owner in enumerate((t ^ (k + 1), 7 - (t ^ (k + 1)))):
                own, shared = slab_ref[rows_at(owner), :], shared_ref[rows_at(owner), :]
                target[half * PIECE : (half + 1) * PIECE, :] = jnp.concatenate(
                    [own, shared[:, 96:128], shared[:, 224:256], shared[:, 256:], jnp.zeros((PIECE, 64), bf16)], axis=1
                )


def attend_backward_own(t, lengths, q, k, v, logs, attended, pieces, weight, cosine, sine, shared):
    rows = k.shape[0]
    size = KEYS
    count, lanes = rows // size, lanes_of(size)
    at = lambda i: count - 1 - i
    by_step = lambda width: pl.BlockSpec((size, width), lambda i, *scalars: (at(i), 0))
    return kernel_call(
        backward_own_body,
        [t, lengths],
        [q, k, v, logs, attended, *pieces, weight, cosine, sine, shared],
        out_shape=[jax.ShapeDtypeStruct((rows, SLAB), bf16)]
        + [jax.ShapeDtypeStruct((2 * PIECE, WIDE), bf16)] * 3
        + [jax.ShapeDtypeStruct((2 * PIECE, SLAB), bf16)],
        grid=(count,),
        in_specs=[
                pl.BlockSpec((GROUP, size, 128), lambda i, *scalars: (0, at(i), 0)),
                whole_spec((rows, 128)), whole_spec((rows, HD)),
                pl.BlockSpec((1, 1, lanes), lambda i, *scalars: (at(i), 0, 0)), whole_spec((rows // 2, 2 * HEADW)),
            ]
            + [whole_spec((2 * PIECE, D))] * 4
            + [whole_spec(weight.shape)]
            + [by_step(128)] * 2
            + [whole_spec((rows, SLAB))],
        out_specs=[whole_spec((rows, SLAB))] + [whole_spec((2 * PIECE, WIDE))] * 3 + [whole_spec((2 * PIECE, SLAB))],
        scratch_shapes=[
                pltpu.VMEM((rows, HD), f32), pltpu.VMEM((rows, HD), f32), pltpu.VMEM((HD, lanes), f32),
                pltpu.VMEM((rows, HEADW), bf16),
            ],
        name="attend_backward_own",
        far_out=True,
    )


def backward_shared_body(
    t_ref, length_ref, block_ref, q_ref, k_ref, v_ref, log_ref, out_ref, up_ref, cos_ref, sin_ref, cos_all, sin_all,
    slab_ref, mine_ref, dk, dv, acc
):
    step = pl.program_id(0)
    t = t_ref[0]
    block = block_ref[step]

    @pl.when(step == 0)
    def _():
        dk[...] = jnp.zeros_like(dk)
        dv[...] = jnp.zeros_like(dv)
        slab_ref[...] = jnp.zeros_like(slab_ref)

    half = lambda ref: jnp.where(step == 0, ref[:, :HEADW], ref[:, HEADW:])
    first, second = backward_block(
        block, PIECE, length_ref, fill(q_ref[...], acc.shape[1]), k_ref, v_ref, log_ref[0], half(out_ref), half(up_ref),
        cos_ref[...], sin_ref[...], dk, dv, acc,
    )
    slab_ref[rows_at(block), :96] = first.astype(bf16)
    slab_ref[rows_at(block), 128:224] = second.astype(bf16)

    @pl.when(step == pl.num_programs(0) - 1)
    def _():
        key_first, key_second = turn_back(dk[...], cos_all[...], sin_all[...])
        slab_ref[:, 96:128] = key_first.astype(bf16)
        slab_ref[:, 224:256] = key_second.astype(bf16)
        slab_ref[:, 256:] = dv[...].astype(bf16)
        mine_ref[:PIECE, :] = slab_ref[rows_at(t), :]
        mine_ref[PIECE:, :] = slab_ref[rows_at(7 - t), :]


def attend_backward_shared(t, lengths, blocks, q, k, v, logs, attended, upstream, cosine, sine):
    rows = k.shape[0]
    lanes = lanes_of(PIECE)
    mine = whole_spec((PIECE, 2 * HEADW))
    natural = pl.BlockSpec((PIECE, 128), lambda i, t_ref, length_ref, block_ref: (block_ref[i], 0))
    return kernel_call(
        backward_shared_body,
        [t, lengths, blocks],
        [q, k, v, logs, attended, upstream, cosine, sine, cosine, sine],
        out_shape=[jax.ShapeDtypeStruct((rows, SLAB), bf16), jax.ShapeDtypeStruct((2 * PIECE, SLAB), bf16)],
        grid=(2,),
        in_specs=[
                pl.BlockSpec((GROUP, PIECE, 128), lambda i, t_ref, length_ref, block_ref: (0, block_ref[i], 0)),
                whole_spec((rows, 128)), whole_spec((rows, HD)),
                pl.BlockSpec((1, 1, lanes), lambda i, *scalars: (i, 0, 0)), mine, mine,
            ]
            + [natural] * 2
            + [whole_spec((rows, 128))] * 2,
        out_specs=[whole_spec((rows, SLAB)), whole_spec((2 * PIECE, SLAB))],
        scratch_shapes=[pltpu.VMEM((rows, HD), f32), pltpu.VMEM((rows, HD), f32), pltpu.VMEM((HD, lanes), f32)],
        name="attend_backward_shared",
        far=True,
    )


def whole_spec(shape):
    return pl.BlockSpec(shape, lambda i, *scalars: (0,) * len(shape))


def out_weight(weight):
    if weight.shape[0] == D:
        return weight[:, SLAB:]
    return jnp.concatenate([weight[:, :HEADW], weight[:, HEADW:]], axis=0)


def out_body(t_ref, x_a, x_b, gain_ref, *refs):
    owns, shares, weights = refs[:8], refs[8:12], refs[12:17]
    mine_ref, normed_ref, w_out = refs[17:]
    step = pl.program_id(0)

    @pl.when(step == 0)
    def _():
        w_out[...] = jnp.concatenate([out_weight(weight) for weight in weights], axis=1)

    middle = jnp.concatenate([x_a[...], x_b[...]], axis=0).astype(f32)
    heads = [unpack(owns[2 * k][...], owns[2 * k + 1][...]) for k in range(4)]
    share = jnp.where(
        step == 0, shares[0][...],
        jnp.where(step == 1, shares[2][...], jnp.where(step == 2, shares[1][...], shares[3][...])),
    )
    middle = middle + dot_nt(jnp.concatenate(heads + [unpack(share, share)], axis=1), w_out[...])
    factor = lax.rsqrt(jnp.mean(middle * middle, axis=-1, keepdims=True) + norm_eps)
    normed_ref[...] = (middle * factor * gain_ref[1:2, :]).astype(bf16)

    @pl.when(step == 0)
    def _():
        mine_ref[...] = middle


def out_project(t, x, gain, owns, shares, weights):
    rows = x.shape[0]
    return kernel_call(
        out_body,
        [t],
        [x, x, gain, *[piece for piece in owns for _ in range(2)], *shares, *weights],
        out_shape=[jax.ShapeDtypeStruct((2 * PIECE, D), f32), jax.ShapeDtypeStruct(x.shape, bf16)],
        grid=(4,),
        in_specs=pair_specs(D)
        + [whole_spec((2, D))]
        + packed_specs() * 4
        + [whole_spec((PIECE, 2 * HEADW))] * 4
        + [whole_spec(weight.shape) for weight in weights],
        out_specs=[whole_spec((2 * PIECE, D)), pl.BlockSpec((2 * PIECE, D), lambda p, t_ref: (p, 0))],
        scratch_shapes=[pltpu.VMEM((D, D), bf16)],
        name="out_project",
        far=True,
        far_out=True,
    )


def feed_body(
    normed_ref, cot_ref, w_ref, hidden_ref, d_ref, kept_ref, sent_ref, terms_kept_ref, terms_sent_ref
):
    step = pl.program_id(0)
    width = hidden_ref.shape[1]
    w_gate, w_up, w_out = (w_ref[:, width * part : width * (part + 1)] for part in range(3))
    normed = normed_ref[...]
    gate = dot_nn(normed, w_gate)
    up = dot_nn(normed, w_up)
    d_hidden = dot_nn(cot_ref[...], w_out)
    sigmoid = 1.0 / (1.0 + jnp.exp(-gate))
    silu = gate * sigmoid
    hidden = (silu * up).astype(bf16)
    d_gate = (d_hidden * up * sigmoid * (1.0 + gate * (1.0 - sigmoid))).astype(bf16)
    d_up = (d_hidden * silu).astype(bf16)
    hidden_ref[...] = hidden
    d_ref[:, :width] = d_gate
    d_ref[:, width:] = d_up
    back = (dot_nt(d_gate, w_gate) + dot_nt(d_up, w_up)).astype(bf16)
    terms = dot_nt(hidden, w_out).astype(bf16)

    @pl.when(step < 2)
    def _():
        sent_ref[0] = back
        terms_sent_ref[0] = terms

    @pl.when(step >= 2)
    def _():
        kept_ref[0] = back
        terms_kept_ref[0] = terms


def feed_forward(normed, cotangent, weights):
    rows, width = normed.shape[0], weights.shape[1] // 3
    at = lambda i: (i + 2) % 4
    by_step = lambda columns: pl.BlockSpec((2 * PIECE, columns), lambda i: (at(i), 0))
    pair = jax.ShapeDtypeStruct((2, 2 * PIECE, D), bf16)
    kept = pl.BlockSpec((1, 2 * PIECE, D), lambda i: (jnp.maximum(i - 2, 0), 0, 0))
    sent = pl.BlockSpec((1, 2 * PIECE, D), lambda i: (jnp.minimum(i, 1), 0, 0))
    return kernel_call(
        feed_body,
        [],
        [normed, cotangent, weights],
        out_shape=[jax.ShapeDtypeStruct((rows, width), bf16), jax.ShapeDtypeStruct((rows, 2 * width), bf16)] + [pair] * 4,
        grid=(4,),
        in_specs=[by_step(D), by_step(D), whole_spec(weights.shape)],
        out_specs=[by_step(width), by_step(2 * width), kept, sent, kept, sent],
        name="feed_forward",
        far=True,
        far_out=True,
    )


def feed_grad_body(normed_ref, cot_ref, d_ref, hidden_ref, grad_ref):
    step = pl.program_id(0)

    @pl.when(step < 2)
    def _():
        grad_ref[...] = dot_tn(normed_ref[...], d_ref[...]).astype(bf16)

    @pl.when(step == 2)
    def _():
        grad_ref[...] = dot_tn(cot_ref[...], hidden_ref[...]).astype(bf16)


def feed_grads(normed, cotangent, d_gate_up, hidden):
    rows, width = hidden.shape
    return kernel_call(
        feed_grad_body,
        [],
        [normed, cotangent, d_gate_up, hidden],
        out_shape=jax.ShapeDtypeStruct((D, 3 * width), bf16),
        grid=(3,),
        in_specs=[
            whole_spec((rows, D)), whole_spec((rows, D)),
            pl.BlockSpec((rows, width), lambda i: (0, jnp.minimum(i, 1))), whole_spec((rows, width)),
        ],
        out_specs=pl.BlockSpec((D, width), lambda i: (0, i)),
        name="feed_grads",
        far_out=True,
    )


def far_body(kept_ref, came_ref, far_ref):
    far_ref[...] = (kept_ref[0].astype(f32) + came_ref[0].astype(f32)).astype(bf16)


def far_part(kept, came):
    shape = kept.shape[1:]
    second = pl.BlockSpec((1,) + shape, lambda i: (1, 0, 0))
    return kernel_call(
        far_body,
        [],
        [kept, came],
        out_shape=jax.ShapeDtypeStruct(shape, bf16),
        grid=(1,),
        in_specs=[second] * 2,
        out_specs=whole_spec(shape),
        name="far_part",
        far=True,
        far_out=True,
    )


def first_spec(x):
    return pl.BlockSpec((1,) + x.shape[1:], lambda i, *scalars: (0,) * x.ndim)


def norm_back(values, gain, upstream):
    factor = lax.rsqrt(jnp.mean(values * values, axis=-1, keepdims=True) + norm_eps)
    weighted = upstream * gain
    inner = jnp.mean(weighted * values, axis=-1, keepdims=True)
    return factor * weighted - values * factor**3 * inner


def total_of(kept_ref, came_ref, far_ref):
    return kept_ref[0].astype(f32) + came_ref[0].astype(f32) + far_ref[...].astype(f32)


def layer_body(middle_ref, kept_ref, came_ref, far_ref, out_ref):
    out_ref[...] = (middle_ref[...] + total_of(kept_ref, came_ref, far_ref)).astype(bf16)


def layer_rows(middle, kept, came, far):
    top = whole_spec(middle.shape)
    return kernel_call(
        layer_body,
        [],
        [middle, kept, came, far],
        out_shape=jax.ShapeDtypeStruct(middle.shape, bf16),
        grid=(1,),
        in_specs=[top, first_spec(kept), first_spec(came), top],
        out_specs=top,
        name="layer_rows",
    )


def middle_body(kept_ref, came_ref, far_ref, middle_ref, up_ref, gain_ref, weight_ref, d_middle_ref, d_branch_ref, d_ref):
    upstream = total_of(kept_ref, came_ref, far_ref)
    d_middle = up_ref[...].astype(f32) + norm_back(middle_ref[...], gain_ref[1:2, :], upstream)
    d_middle_ref[...] = d_middle
    d_branch = d_middle.astype(bf16)
    d_branch_ref[...] = d_branch
    d_ref[...] = pack(dot_nn(d_branch, weight_ref[:, SLAB:]).astype(bf16))


def middle_backward(kept, came, far, middle, upstream, gain, shared_block):
    rows = far.shape[0]
    top = whole_spec((rows, D))
    packed = (rows // 2, 2 * HEADW)
    return kernel_call(
        middle_body,
        [],
        [kept, came, far, middle, upstream, gain, shared_block],
        out_shape=[
            jax.ShapeDtypeStruct((rows, D), f32), jax.ShapeDtypeStruct((rows, D), bf16), jax.ShapeDtypeStruct(packed, bf16),
        ],
        grid=(1,),
        in_specs=[first_spec(kept), first_spec(came)] + [top] * 3 + [whole_spec((2, D)), whole_spec(shared_block.shape)],
        out_specs=[top, top, whole_spec(packed)],
        name="middle_backward",
        far=True,
        far_out=True,
    )


def early_body(t_ref, d_branch_ref, share_ref, normed_ref, slab_ref, kept_ref, sent_ref, block):
    t = t_ref[0]
    share = share_ref[...]
    block[...] = jnp.concatenate(
        [dot_tn(normed_ref[...], slab_ref[...]), dot_tn(d_branch_ref[...], unpack(share, share))], axis=1
    ).astype(bf16)
    for k in range(4):
        at = pl.multiple_of((t ^ k) * 128, 128)
        (kept_ref, sent_ref)[k & 1][k // 2] = block[:, pl.ds(at, 128)]


def early_grads(t, d_branch, share, normed, slab):
    arrays = [d_branch, share, normed, slab]
    pair = jax.ShapeDtypeStruct((2, D, 128), bf16)
    return kernel_call(
        early_body,
        [t],
        arrays,
        out_shape=[pair, pair],
        grid=(1,),
        in_specs=[whole_spec(x.shape) for x in arrays],
        out_specs=[whole_spec(pair.shape)] * 2,
        scratch_shapes=[pltpu.VMEM((D, WIDE), bf16)],
        name="early_grads",
        far_out=True,
    )


def attn_grad_body(me_ref, t_ref, normed_ref, slab_ref, early_kept_ref, came_ref, far_ref, *refs):
    branches, owns, kept_ref, sent_ref = refs[:4], refs[4:12], refs[12], refs[13]
    early = total_of(early_kept_ref, came_ref, far_ref)
    grad = dot_tn(normed_ref[...], slab_ref[...])
    out = dot_tn(branches[0][...], unpack(owns[0][...], owns[1][...]))
    for k in (1, 2, 3):
        out = out + dot_tn(branches[k][...], unpack(owns[2 * k][...], owns[2 * k + 1][...]))
    whole = jnp.concatenate([early, grad, out], axis=1)
    rows = kept_ref.shape[1]
    split_chunks(me_ref, [whole[rows * j : rows * (j + 1)] for j in range(D // rows)], kept_ref, sent_ref)


def owner_specs(k):
    return [
        pl.BlockSpec((PIECE, 2 * HEADW), lambda i, me_ref, t_ref: (t_ref[0] ^ k, 0)),
        pl.BlockSpec((PIECE, 2 * HEADW), lambda i, me_ref, t_ref: (3 - (t_ref[0] ^ k), 0)),
    ]


def attn_grads(me, t, normed, slab, kept, came, far, branches, attended):
    half = jax.ShapeDtypeStruct((4, D // 8, WIDE + 128), bf16)
    arrays = [normed, slab, kept, came, far, *branches]
    return kernel_call(
        attn_grad_body,
        [me, t],
        arrays + [attended] * 8,
        out_shape=[half, half],
        grid=(1,),
        in_specs=[first_spec(x) if x.ndim == 3 else whole_spec(x.shape) for x in arrays]
        + [spec for k in range(4) for spec in owner_specs(k)],
        out_specs=[whole_spec(half.shape)] * 2,
        name="attn_grads",
    )


def input_body(t_ref, x_a, x_b, d_middle_ref, gain_ref, own_ref, shared_ref, *refs):
    came_refs, slabs, shared_slab, out_ref = refs[:3], refs[3:7], refs[7], refs[8]
    upstream = dot_nt(own_ref[...], slabs[0][0, :, :SLAB])
    for piece, slab in zip(came_refs, slabs[1:4]):
        upstream = upstream + dot_nt(piece[:, :SLAB], slab[0, :, :SLAB])
    shared = shared_ref[...]
    key_value = jnp.concatenate([shared[:, 96:128], shared[:, 224:256], shared[:, 256:]], axis=1).astype(f32)
    for piece in came_refs:
        key_value = key_value + piece[:, SLAB : SLAB + 2 * HD].astype(f32)
    key_value = key_value.astype(bf16)
    shared = jnp.concatenate(
        [shared[:, :96], key_value[:, :32], shared[:, 128:224], key_value[:, 32:64], key_value[:, 64:]], axis=1
    )
    upstream = upstream + dot_nt(shared, shared_slab[:, :SLAB])
    x = jnp.concatenate([x_a[...], x_b[...]], axis=0).astype(f32)
    out_ref[...] = (d_middle_ref[...] + norm_back(x, gain_ref[0:1, :], upstream)).astype(bf16)


def input_backward(t, x, d_middle, gain, own, shared, came, slabs, shared_block):
    rows = 2 * PIECE
    of_owner = [
        pl.BlockSpec((1, D, 384), functools.partial(lambda k, i, t_ref: (t_ref[0] ^ k, 0, 0), k)) for k in range(4)
    ]
    return kernel_call(
        input_body,
        [t],
        [x, x, d_middle, gain, own, shared, *came, *[slabs] * 4, shared_block],
        out_shape=jax.ShapeDtypeStruct((rows, D), bf16),
        grid=(1,),
        in_specs=pair_specs(D)
        + [whole_spec((rows, D)), whole_spec((2, D))]
        + [whole_spec((rows, SLAB))] * 2
        + [whole_spec((rows, WIDE))] * 3
        + of_owner
        + [pl.BlockSpec((D, 384), lambda i, *scalars: (0, 0))],
        out_specs=whole_spec((rows, D)),
        name="input_backward",
        far=True,
    )


MATRIX_RATE = 0.5 * D ** (-0.5)
OUTPUT_RATE = 0.5 * OUT_FAN ** (-0.5)
FEED_RATE = 0.5 * FF ** (-0.5)


def adam_step(weight, first, second, average, gradient, step_rate, decay_rate):
    first_new = beta_first * first + (1.0 - beta_first) * gradient
    second_new = beta_second * second + (1.0 - beta_second) * gradient * gradient
    corrected_first = first_new / (1.0 - beta_first**STEP)
    corrected_second = second_new / (1.0 - beta_second**STEP)
    weight_new = weight - step_rate * (
        corrected_first / (jnp.sqrt(corrected_second) + adam_eps) + decay_rate * weight
    )
    average_new = average_keep * average + (1.0 - average_keep) * weight_new
    return (first_new, second_new, weight_new, average_new)


def adam_steps(count):
    return count // 24 if count % 24 == 0 else 1


def feed_adam_body(grad_ref, *refs):
    in_state, ffn_state, in_outs, ffn_outs, term_ref = refs[:4], refs[4:8], refs[8:13], refs[13:18], refs[18]
    width = ffn_state[0].shape[1]

    def total(part):
        return grad_ref[:, part * width : (part + 1) * width].astype(f32)

    term = 0.0
    for half in range(2):
        gradient = total(half)
        state = [ref[:, half, :] for ref in in_state]
        term = term + jnp.sum(state[0].astype(bf16).astype(f32) * gradient, axis=1, keepdims=True)
        for ref, value in zip(in_outs, (gradient,) + adam_step(*state, gradient, MATRIX_RATE, 0.1)):
            ref[:, half, :] = value
    gradient = total(2)
    state = [ref[...] for ref in ffn_state]
    for ref, value in zip(ffn_outs, (gradient,) + adam_step(*state, gradient, FEED_RATE, 0.1)):
        ref[...] = value
    high = term.astype(bf16).astype(f32)
    lane = lax.broadcasted_iota(jnp.int32, term_ref.shape, 1)
    term_ref[...] = jnp.where(lane == 0, high, jnp.where(lane == 1, term - high, 0.0)).astype(bf16)


def feed_adam(gradient, in_state, ffn_state):
    rows, width = ffn_state[0].shape
    steps = adam_steps(rows)
    each = rows // steps
    flat = lambda columns: pl.BlockSpec((each, columns), lambda i: (i, 0))
    pair = pl.BlockSpec((each, 2, width), lambda i: (i, 0, 0))
    outs = kernel_call(
        feed_adam_body,
        [],
        [gradient, *in_state, *ffn_state],
        out_shape=[jax.ShapeDtypeStruct((rows, 2, width), f32)] * 5
        + [jax.ShapeDtypeStruct((rows, width), f32)] * 5
        + [jax.ShapeDtypeStruct((rows, 128), bf16)],
        grid=(steps,),
        in_specs=[flat(3 * width)] + [pair] * 4 + [flat(width)] * 4,
        out_specs=[pair] * 5 + [flat(width)] * 5 + [flat(128)],
        name="feed_adam",
        far=True,
    )
    return outs[:10], outs[10]


def attn_adam_body(t_ref, group_ref, *refs):
    pieces, query_state, keyval_state, output_state, gain_state = (
        refs[:4], refs[4:8], refs[8:12], refs[12:16], refs[16:20],
    )
    query_outs, keyval_outs, output_outs, gain_outs = refs[20:25], refs[25:30], refs[30:35], refs[35:40]
    query_grad, keyval_grad, output_grad, column, head_parts, group_parts = refs[40:]
    step, t = pl.program_id(0), t_ref[0]
    count = pieces[0].shape[0]

    @pl.when(step == 0)
    def _():
        column[...] = jnp.zeros_like(column)
        quarters = []
        for quarter in range(4):
            here = pieces[0][:, :128]
            for k in (1, 2, 3):
                here = jnp.where((t ^ k) == quarter, pieces[k][:, :128], here)
            quarters.append(here)
        shared = jnp.concatenate(quarters, axis=1)
        for k in range(5):
            group = KV - 1 if k == 4 else t ^ k
            block = (shared if k == 4 else pieces[k][:, 128 : 128 + WIDE]).astype(f32)
            for member in range(GROUP + 1):
                at = 32 * member
                whole = jnp.concatenate([block[:, at : at + 32], block[:, 128 + at : 160 + at]], axis=1)
                if member < GROUP:
                    head_parts[group * GROUP + member] = whole
                else:
                    group_parts[group] = jnp.concatenate([whole, block[:, 256:SLAB]], axis=1)
            turned = dot_nt(unit(HEADW), block[:, SLAB:].astype(bf16))
            for which in range(GROUP):
                at = pl.multiple_of(head_of(group, which, group_ref) * HD, HD)
                output_grad[pl.ds(at, HD), :] = turned[which * HD : (which + 1) * HD, :]
        query_grad[...] = jnp.concatenate([head_parts[group_ref[h]] for h in range(NQ)], axis=1)
        both = [group_parts[g] for g in range(KV)]
        keyval_grad[...] = jnp.concatenate([x[:, :HD] for x in both] + [x[:, HD:] for x in both], axis=1)

    each = query_state[0].shape[0]
    here = pl.ds(pl.multiple_of(step * each, 8), each) if each < count else slice(0, count)
    out_each = output_state[0].shape[0]
    out_here = pl.ds(pl.multiple_of(step * out_each, 8), out_each)
    term = 0.0
    for state_refs, outs, gradient, rate in (
        (query_state, query_outs, query_grad[here, :], MATRIX_RATE),
        (keyval_state, keyval_outs, keyval_grad[here, :], MATRIX_RATE),
        (output_state, output_outs, output_grad[out_here, :], OUTPUT_RATE),
    ):
        state = [ref[...] for ref in state_refs]
        if rate == MATRIX_RATE:
            term = term + jnp.sum(state[0].astype(bf16).astype(f32) * gradient, axis=1, keepdims=True)
        for ref, value in zip(outs, (gradient,) + adam_step(*state, gradient, rate, 0.1)):
            ref[...] = value
    lane = lax.broadcasted_iota(jnp.int32, (each, 128), 1)
    column[here, :] = jnp.where(lane == 0, term, 0.0)

    @pl.when(step == pl.num_programs(0) - 1)
    def _():
        second = 0.0
        for piece in pieces:
            second = second + piece[:, 128 + WIDE :].astype(f32)
        second = jnp.sum(second, axis=1, keepdims=True)
        lane = lax.broadcasted_iota(jnp.int32, (count, 128), 1)
        column[:count, :] = jnp.where(lane == 1, second, column[:count, :])
        terms = jnp.transpose(column[...])[:2, :count]
        state = [ref[...] for ref in gain_state]
        gradient = terms / state[0]
        for ref, value in zip(gain_outs, (gradient,) + adam_step(*state, gradient, 0.3, 0.0)):
            ref[...] = value


def attn_adam(t, query_group, pieces, query_state, keyval_state, output_state, gain_state):
    rows = query_state[0].shape[0]
    steps = adam_steps(rows)
    states = (query_state, keyval_state, output_state)
    specs = [
        pl.BlockSpec((x[0].shape[0] // steps, x[0].shape[1]), lambda i, *scalars: (i, 0)) for x in states
    ] + [whole_spec(gain_state[0].shape)]
    states = states + (gain_state,)
    outs = kernel_call(
        attn_adam_body,
        [t, query_group],
        [*pieces, *[x for state in states for x in state]],
        out_shape=[jax.ShapeDtypeStruct(state[0].shape, f32) for state in states for _ in range(5)],
        grid=(steps,),
        in_specs=[whole_spec(pieces[0].shape)] * 4 + [spec for spec in specs for _ in range(4)],
        out_specs=[spec for spec in specs for _ in range(5)],
        scratch_shapes=[
            pltpu.VMEM((rows, NQ * HD), f32), pltpu.VMEM((rows, 2 * KV * HD), f32), pltpu.VMEM((NQ * HD, rows), f32),
            pltpu.VMEM((128, 128), f32), pltpu.VMEM((NQ, rows, HD), f32), pltpu.VMEM((KV, rows, 2 * HD), f32),
        ],
        name="attn_adam",
        far=True,
    )
    return outs[:5], outs[5:10], outs[10:15], outs[15:20]


def local(
    tokens, cotangent, lengths, valid, query_group,
    w_query, w_keyval, w_output, w_ffn_in, w_ffn_out, norm_gains,
    first_query, first_keyval, first_output, first_ffn_in, first_ffn_out, first_gains,
    second_query, second_keyval, second_output, second_ffn_in, second_ffn_out, second_gains,
    average_query, average_keyval, average_output, average_ffn_in, average_ffn_out, average_gains,
):
    t = lax.axis_index("tensor").astype(jnp.int32)
    t_array = t.reshape(1)
    row_count = tokens.shape[0]
    owned_rows = w_query.shape[0]
    hidden_count = w_ffn_out.shape[0]

    me = lax.axis_index("dp").astype(jnp.int32).reshape(1)
    small = lax.axis_size("dp") == 8
    rest_rows = 8 if owned_rows % 8 == 0 else 17
    own_part = prepare(t_array, query_group, w_query, w_keyval, w_output, norm_gains, owned_rows + rest_rows)
    own_one = gather_one(own_part)
    length_row = lengths[0]
    seq_ends = jnp.cumsum(length_row)
    valid, seq_ends = after((valid, seq_ends), own_part)
    row_index = jnp.arange(row_count, dtype=jnp.int32)
    row_start = jnp.where(
        row_index >= seq_ends[1], seq_ends[1], jnp.where(row_index >= seq_ends[0], seq_ends[0], 0)
    )
    position = (row_index - row_start).astype(f32)
    frequency = rope_base ** (-jnp.arange(0, HD, 2, dtype=f32) / HD)
    angles = position[:, None] * jnp.tile(frequency, 4)[None, :]
    cosine, sine = jnp.cos(angles), jnp.sin(angles)
    valid_wide = jnp.broadcast_to(valid[:, None], (row_count, 128))
    tables = (cosine, sine, valid_wide)

    w_in_now, w_out_now = after((w_ffn_in, w_ffn_out), own_part)
    feed_part = jnp.concatenate(
        [w_in_now[:, 0].astype(bf16), w_in_now[:, 1].astype(bf16), jnp.transpose(w_out_now).astype(bf16)], axis=1
    )
    own_two = gather_two(after(own_one, (tables, feed_part)))
    feed_all = lax.all_gather(after(feed_part, (own_one, tables)), "dp", axis=0, tiled=True)

    own_cotangent = own_order(after(cotangent, feed_part), t_array)
    tokens = by_rows(after(tokens, feed_part))
    slab_own, out_own, quarter, gains = gather_end(after(own_two, (own_cotangent, tokens)), owned_rows)
    quarters = gather_first(quarter)

    normed_one, q_own, k_own, v_own = project(length_row, tokens, after(gains, quarters[1]), slab_own, cosine, sine, valid_wide)
    out_owns = gather_first(after(out_own, normed_one))
    blocks = jnp.arange(row_count // KEYS, dtype=jnp.int32)
    part_blocks = jnp.stack([t, 7 - t])
    q_own = after(q_own, out_owns[1])
    att_own, log_own = attend_forward(length_row, blocks, KEYS, q_own, k_own, v_own)
    att_owns = gather_first(att_own)
    quarters, out_owns = after((quarters, out_owns), att_own)
    quarters, out_owns = gather_second(quarters), gather_second(out_owns)
    shared_block = assemble(t_array, after(quarters, att_owns[1]))
    q_part, k_part, v_part = project(length_row, normed_one, None, shared_block, cosine, sine, valid_wide)
    att_part, log_part = attend_forward(length_row, part_blocks, PIECE, q_part, k_part, v_part)
    att_shares = [att_part] + exchange_tensor([att_part] * 3)
    att_owns = gather_second(after(att_owns, att_part))
    weights = out_owns + [shared_block]
    slabs = lax.all_gather(after(slab_own, (att_owns[2], out_owns[2])), "tensor", axis=0)
    middle_mine, normed_two = out_project(t_array, tokens, gains, att_owns, att_shares, weights)
    hidden, d_gate_up, two_kept, two_sent, terms_kept, terms_sent = feed_forward(
        normed_two, own_cotangent, after(feed_all, normed_two)
    )

    two_came = swap(two_sent, "tensor", 1)
    terms_came = swap(terms_sent, "tensor", 1)
    two_part = far_part(two_kept, two_came)
    two_far = swap(two_part, "tensor", 2)

    feed_grad = feed_grads(after(normed_two, two_part), own_cotangent, d_gate_up, hidden)

    own_rows = 2 * PIECE
    d_middle, d_branch, d_att_part = middle_backward(
        two_kept, two_came, after(two_far, (feed_grad, slabs)), middle_mine, own_cotangent, gains, shared_block
    )
    feed_sum = lax.psum_scatter(after(feed_grad, two_far), "dp", scatter_dimension=0, tiled=True)
    branches = gather_first(d_branch)
    d_shared, shared_mine = attend_backward_shared(
        t_array, length_row, part_blocks, q_part, k_part, v_part, log_part, att_part,
        after(d_att_part, branches[1]), cosine, sine,
    )
    terms_part = far_part(terms_kept, after(terms_came, d_shared))
    early_kept, early_sent = early_grads(t_array, d_branch, att_part, normed_one, after(d_shared, terms_part))
    early_came = swap(early_sent, "tensor", 1)
    early_part = far_part(early_kept, early_came)
    early_far = swap(early_part, "tensor", 2)
    branches = gather_second(after(branches, early_part))
    terms_far = swap(after(terms_part, branches[2]), "tensor", 2)
    d_own, *own_sent, own_mine = attend_backward_own(
        t_array, length_row, q_own, k_own, v_own, log_own, att_own, branches, out_own, cosine, sine, d_shared
    )
    own_came = exchange_tensor(own_sent)
    layer_mine = layer_rows(middle_mine, terms_kept, terms_came, after(terms_far, (d_own, early_far)))
    d_own = after(d_own, layer_mine)
    if small:
        attn_half = scatter_one(
            *attn_grads(
                me, t_array, normed_one, d_own, early_kept, early_came, early_far, branches, att_own
            )
        )
    else:
        early = early_kept[0].astype(f32) + early_came[0].astype(f32) + early_far.astype(f32)
        out_grad = 0.0
        for k in range(4):
            rows_of = [jnp.where(t >= 0, t ^ k, 0), 3 - (t ^ k)]
            low, high = (lax.dynamic_slice_in_dim(att_own, PIECE * at, PIECE, 0) for at in rows_of)
            out_grad = out_grad + dot_tn(branches[k], unpack(low, high))
        attn_half = (jnp.concatenate([early, dot_tn(normed_one, d_own), out_grad], axis=1),)
    layer_pieces = gather_tensor(layer_mine)
    attn_quarter = scatter_two(after(attn_half, layer_pieces))
    grad_mine = input_backward(
        t_array, tokens, d_middle, gains, own_mine, shared_mine, after(own_came, attn_quarter[0]), slabs, shared_block
    )
    grad_pieces = gather_first(grad_mine)
    layer_out = natural_order(after(layer_pieces, grad_mine), t_array)

    feed_results, gain_term = feed_adam(
        after(feed_sum, layer_out),
        (w_ffn_in, first_ffn_in, second_ffn_in, average_ffn_in),
        [jnp.transpose(x) for x in (w_ffn_out, first_ffn_out, second_ffn_out, average_ffn_out)],
    )
    in_results, out_results = feed_results[:5], [jnp.transpose(x) for x in feed_results[5:]]
    owned_attn = jnp.concatenate([scatter_end(after(attn_quarter, gain_term)).astype(bf16), gain_term], axis=1)
    attn_first = gather_first(owned_attn)
    input_grad = natural_order(gather_second(after(grad_pieces, attn_first[1])), t_array)
    attn_pieces = gather_second(after(attn_first, input_grad))
    query_results, keyval_results, output_results, gain_results = attn_adam(
        t_array, query_group, attn_pieces,
        (w_query, first_query, second_query, average_query),
        (w_keyval, first_keyval, second_keyval, average_keyval),
        (w_output, first_output, second_output, average_output),
        (norm_gains, first_gains, second_gains, average_gains),
    )
    results = (query_results, keyval_results, output_results, in_results, out_results, gain_results)
    return (layer_out, input_grad) + tuple(result[part] for part in range(5) for result in results)


def solution(mesh):
    token, rows, columns = P("dp", None), P("dp", None), P(None, "dp")
    weight_specs = (rows, rows, columns, P("dp", None, "tensor"), P("tensor", "dp"), columns)
    in_specs = (token, token, P("dp", None), P("dp"), P()) + weight_specs * 4
    out_specs = (token, token) + weight_specs * 5
    return jax.shard_map(local, mesh=mesh, in_specs=in_specs, out_specs=out_specs, check_vma=False)
```

```python
import functools

import jax
import jax.numpy as jnp
import numpy as np
from jax import lax
from jax.experimental import pallas as pl
from jax.experimental.layout import Layout, with_layout_constraint
from jax.experimental.pallas import tpu as pltpu
from jax.sharding import PartitionSpec as P

D = 960
FF = 2560
NQ = 15
KV = 5
HD = 64
STEP = 10
GROUP = 3
OUT_FAN = 3
SLAB = 320
HEADW = GROUP * HD
WIDE = SLAB + HEADW
PIECE = 160
KEYS = 256

norm_eps = 1e-05
rope_base = 10000.0
beta_first = 0.5
beta_second = 0.5
adam_eps = 1e-08
average_keep = 0.5
bf16 = jnp.bfloat16
f32 = jnp.float32
VMEM_LIMIT = 48 * 1024 * 1024


def params(*semantics):
    return pltpu.CompilerParams(dimension_semantics=semantics, vmem_limit_bytes=VMEM_LIMIT)


def by_rows(x):
    return with_layout_constraint(x, Layout(major_to_minor=tuple(range(x.ndim))))


def swap(x, axis, offset):
    count = lax.axis_size(axis)
    return by_rows(lax.ppermute(by_rows(x), axis, [(i, i ^ offset) for i in range(count)]))


def dot_nn(a, b):
    return lax.dot_general(a, b, (((1,), (0,)), ((), ())), preferred_element_type=f32)


def dot_nt(a, b):
    return lax.dot_general(a, b, (((1,), (1,)), ((), ())), preferred_element_type=f32)


def dot_tn(a, b):
    return lax.dot_general(a, b, (((0,), (0,)), ((), ())), preferred_element_type=f32)


TIMES = {
    "prepare": 2.5, "place": 3.5, "assemble": 1.0, "own_order": 1.0, "natural_order": 2.5, "project": 4.5,
    "attend_forward": 8.0, "out_project": 10.0, "feed_forward": 20.0, "feed_grads": 0.0, "far_part": 1.0, "half_sums": 2.0,
    "middle_backward": 4.5, "attend_backward_shared": 5.5, "early_grads": 6.5, "attend_backward_own": 18.0,
    "attn_grads": 5.0, "layer_rows": 1.5, "feed_adam": 5.0, "attn_adam": 6.0, "input_backward": 0.0,
}


def kernel_call(body, scalars, arrays, *, out_shape, grid, in_specs, out_specs, scratch_shapes=(), name, far=False, far_out=False):
    single = not isinstance(out_shape, (list, tuple))
    shapes = [out_shape] if single else out_shape
    call = pl.pallas_call(
        body,
        out_shape=[pltpu.HBM(shape.shape, shape.dtype) for shape in shapes] if far_out else shapes,
        grid_spec=pltpu.PrefetchScalarGridSpec(
            num_scalar_prefetch=len(scalars),
        grid=grid,
        in_specs=in_specs,
        out_specs=[out_specs] if single else out_specs,
        scratch_shapes=scratch_shapes,
        ),
        compiler_params=params("arbitrary"),
        cost_estimate=pl.CostEstimate(flops=0, bytes_accessed=int(TIMES[name] * 3.2e6), transcendentals=0),
        name=name,
    )
    if far:
        arrays = [pltpu.with_memory_space_constraint(x, pltpu.HBM) for x in arrays]
    outs = call(*scalars, *arrays)
    return outs[0] if single else outs


def after(values, *earlier):
    return lax.optimization_barrier((values, earlier))[0]


def turn(k):
    return (k & 1) * 2 + k // 2


def place_of(block, t):
    owner = jnp.minimum(block, 7 - block)
    return 2 * turn(owner ^ t) + (block > 3).astype(jnp.int32)


def place_body(index_ref, *refs):
    pieces, (slab_ref, out_ref, quarter_ref, gains_ref, rest) = refs[:-5], refs[-5:]
    rows = slab_ref.shape[1]
    half = len(pieces) // 2
    for slot, piece in enumerate(pieces):
        at = index_ref[slot]
        slab_ref[at] = piece[:rows, : slab_ref.shape[2]]
        quarter_ref[at] = piece[:rows, WIDE:]
        parts = piece[rows:, :128].astype(f32)
        rest[at] = parts[0:2] + parts[2:4] + parts[4:6]
        out = piece[:rows, SLAB:WIDE]

        @pl.when(at < half)
        def _():
            out_ref[at, :, :HEADW] = out

        @pl.when(at >= half)
        def _():
            out_ref[at - half, :, HEADW:] = out

    gains_ref[...] = jnp.concatenate([rest[j][:, :rows] for j in range(len(pieces))], axis=1)


def place(pieces, index, rows):
    count = len(pieces)
    shapes = [(count, rows, 384), (count // 2, rows, 2 * HEADW), (count, rows, 128)]
    return kernel_call(
        place_body,
        [index],
        pieces,
        out_shape=[jax.ShapeDtypeStruct(shape, pieces[0].dtype) for shape in shapes]
        + [jax.ShapeDtypeStruct((2, count * rows), f32)],
        grid=(1,),
        in_specs=[whole_spec(pieces[0].shape)] * count,
        out_specs=[whole_spec(shape) for shape in shapes] + [whole_spec((2, count * rows))],
        scratch_shapes=[pltpu.VMEM((count, 2, 128), f32)],
        name="place",
        far=True,
        far_out=True,
    )


def assemble_body(t_ref, *refs):
    for k in range(4):
        at = pl.multiple_of((t_ref[0] ^ k) * 128, 128)
        refs[4][:, pl.ds(at, 128)] = refs[k][...]


def assemble(t, pieces):
    rows = pieces[0].shape[0]
    return kernel_call(
        assemble_body,
        [t],
        pieces,
        out_shape=jax.ShapeDtypeStruct((rows, WIDE), bf16),
        grid=(1,),
        in_specs=[whole_spec((rows, 128))] * 4,
        out_specs=whole_spec((rows, WIDE)),
        name="assemble",
    )


def reorder_body(t_ref, x_ref, out_ref):
    out_ref[...] = x_ref[...]


def own_order(x, t):
    width = x.shape[1]
    owner = lambda p, t_ref: t_ref[0] ^ turn(p // 2)
    return kernel_call(
        reorder_body,
        [t],
        [x],
        out_shape=jax.ShapeDtypeStruct(x.shape, x.dtype),
        grid=(8,),
        in_specs=[
                pl.BlockSpec(
                    (PIECE, width),
                    lambda p, t_ref: (jnp.where(p % 2 == 0, owner(p, t_ref), 7 - owner(p, t_ref)), 0),
                )
            ],
        out_specs=pl.BlockSpec((PIECE, width), lambda p, t_ref: (p, 0)),
        name="own_order",
    )


def natural_body(t_ref, *refs):
    half, t = pl.program_id(0), t_ref[0]
    pieces, out_ref = refs[:4], refs[4]
    parts = []
    for block in range(4):
        owner = jnp.where(half == 0, block, 3 - block)
        part = pieces[0][...]
        for k in (1, 2, 3):
            part = jnp.where((owner ^ t) == k, pieces[k][...], part)
        parts.append(part)
    out_ref[...] = jnp.transpose(jnp.concatenate(parts, axis=0))


def natural_order(pieces, t):
    width = pieces[0].shape[1]
    turned = kernel_call(
        natural_body,
        [t],
        pieces,
        out_shape=jax.ShapeDtypeStruct((width, 8 * PIECE), pieces[0].dtype),
        grid=(2,),
        in_specs=[pl.BlockSpec((PIECE, width), lambda b, t_ref: (b, 0))] * 4,
        out_specs=pl.BlockSpec((width, 4 * PIECE), lambda b, t_ref: (0, b)),
        name="natural_order",
        far=True,
    )
    return jnp.transpose(turned)


def gather_one(x):
    if lax.axis_size("dp") != 8:
        return [x]
    return [x] + [swap(x, "dp", k) for k in (2, 4, 6)]


def gather_two(pieces):
    if len(pieces) == 1:
        return pieces
    return pieces + [swap(piece, "dp", 1) for piece in pieces]


def gather_end(pieces, rows):
    if len(pieces) == 1:
        both = lax.all_gather(pieces[0], "dp", axis=0)
        whole = both[:, :rows].reshape(D, WIDE + 128)
        out = whole[:, SLAB:WIDE]
        parts = jnp.swapaxes(both[:, rows : rows + 6, :rows].astype(f32), 0, 1).reshape(6, D)
        gains = parts[0:2] + parts[2:4] + parts[4:6]
        return whole[:, :384], jnp.concatenate([out[: D // 2], out[D // 2 :]], axis=1), whole[:, WIDE:], gains
    me = lax.axis_index("dp")
    index = jnp.stack([me ^ k for k in (0, 2, 4, 6, 1, 3, 5, 7)]).astype(jnp.int32)
    slab, out, quarter, gains = place(pieces, index, rows)
    return slab.reshape(D, 384), out.reshape(D // 2, 2 * HEADW), quarter.reshape(D, 128), gains


def scatter_one(kept, sent):
    if sent is None:
        return (kept,)
    return kept, swap(sent, "dp", 1)


def scatter_two(halves):
    if len(halves) == 1:
        return halves
    mine, *sent = half_sums(lax.axis_index("dp").astype(jnp.int32).reshape(1), *halves)
    return [mine] + [swap(piece, "dp", 2 * (k + 1)) for k, piece in enumerate(sent)]


def scatter_end(quarters):
    if len(quarters) == 1:
        return lax.psum_scatter(quarters[0].astype(f32), "dp", scatter_dimension=0, tiled=True)
    return sum(quarter.astype(f32) for quarter in quarters)


def half_body(me_ref, kept_ref, came_ref, mine_ref, *sent_refs):
    at_z = me_ref[0] >> 1
    mine_ref[...] = kept_ref[at_z].astype(f32) + came_ref[at_z].astype(f32)
    for k, sent_ref in enumerate(sent_refs):
        at = at_z ^ (k + 1)
        sent_ref[...] = (kept_ref[at].astype(f32) + came_ref[at].astype(f32)).astype(bf16)


def half_sums(me, kept, came):
    count, rows, columns = kept.shape
    return kernel_call(
        half_body,
        [me],
        [kept, came],
        out_shape=[jax.ShapeDtypeStruct((rows, columns), f32)]
        + [jax.ShapeDtypeStruct((rows, columns), bf16)] * (count - 1),
        grid=(1,),
        in_specs=[whole_spec(kept.shape)] * 2,
        out_specs=[whole_spec((rows, columns))] * count,
        name="half_sums",
    )


def split_chunks(me_ref, chunks, kept_ref, sent_ref):
    at_y = (me_ref[0] & 1) == 0
    for z in range(len(chunks) // 2):
        even, odd = chunks[2 * z].astype(bf16), chunks[2 * z + 1].astype(bf16)
        kept_ref[z] = jnp.where(at_y, even, odd)
        sent_ref[z] = jnp.where(at_y, odd, even)


def gather_first(x):
    across = swap(x, "tensor", 2)
    return [x, swap(x, "tensor", 1), across]


def gather_second(pieces):
    return pieces + [swap(pieces[2], "tensor", 1)]


def gather_tensor(x):
    return gather_second(gather_first(x))


def exchange_tensor(pieces):
    return [swap(piece, "tensor", k + 1) for k, piece in enumerate(pieces)]


def slab_target(group, group_ref):
    lane = lax.broadcasted_iota(jnp.int32, (1, SLAB), 1)
    second = lane >= 128
    value = lane >= 256
    within = jnp.where(second, lane - 128, lane)
    inside = (within & 31) + jnp.where(second, 32, 0)
    member = within >> 5
    query_at = jnp.full_like(lane, -1)
    for which in range(GROUP):
        query_at = jnp.where(member == which, head_of(group, which, group_ref) * HD + inside, query_at)
    query_at = jnp.where(value, -1, query_at)
    key_at = jnp.where(member == GROUP, group * HD + inside, -1)
    key_at = jnp.where(value, KV * HD + group * HD + lane - 256, key_at)
    return query_at, key_at


def head_of(group, which, group_ref):
    slot = group * GROUP + which
    head = jnp.int32(0)
    for h in range(NQ):
        head = jnp.where(group_ref[h] == slot, h, head)
    return head


def pick(width, index):
    rows = lax.broadcasted_iota(jnp.int32, (width, index.shape[1]), 0)
    return jnp.where(rows == index, 1.0, 0.0).astype(bf16)


def unit(count):
    rows = lax.broadcasted_iota(jnp.int32, (count, count), 0)
    return jnp.where(rows == lax.broadcasted_iota(jnp.int32, (count, count), 1), 1.0, 0.0).astype(bf16)


def prep_body(t_ref, index_ref, query_ref, keyval_ref, output_ref, gains_ref, out_ref):
    count = query_ref.shape[0]
    query, keyval = query_ref[...].astype(bf16), keyval_ref[...].astype(bf16)

    def block(group):
        query_at, key_at = slab_target(group, index_ref)
        picked = dot_nn(query, pick(NQ * HD, query_at)) + dot_nn(keyval, pick(2 * KV * HD, key_at))
        heads = [
            output_ref[pl.ds(pl.multiple_of(head_of(group, which, index_ref) * HD, HD), HD), :] for which in range(GROUP)
        ]
        turned = dot_nt(unit(count), jnp.concatenate(heads, axis=0).astype(bf16))
        return jnp.concatenate([picked, turned], axis=1)

    t = t_ref[0]
    shared = block(KV - 1)
    quarter = shared[:, :128]
    for k in (1, 2, 3):
        quarter = jnp.where(t == k, shared[:, 128 * k : 128 * (k + 1)], quarter)
    out_ref[:count, :] = jnp.concatenate([block(t), quarter], axis=1).astype(bf16)
    missing = out_ref.shape[0] - count
    gains = gains_ref[...]
    high = gains.astype(bf16).astype(f32)
    middle = (gains - high).astype(bf16).astype(f32)
    low = gains - high - middle
    rest = jnp.concatenate([high, middle, low, jnp.zeros((missing - 6, count), f32)], axis=0)
    rest = jnp.concatenate([rest, jnp.zeros((missing, WIDE + 128 - count), f32)], axis=1)
    out_ref[count:, :] = rest.astype(bf16)


def prepare(t, query_group, w_query, w_keyval, w_output, norm_gains, rows):
    return kernel_call(
        prep_body,
        [t, query_group],
        [w_query, w_keyval, w_output, norm_gains],
        out_shape=jax.ShapeDtypeStruct((rows, WIDE + 128), bf16),
        grid=(1,),
        in_specs=[whole_spec(x.shape) for x in (w_query, w_keyval, w_output, norm_gains)],
        out_specs=whole_spec((rows, WIDE + 128)),
        name="prepare",
        far=True,
    )


def pair_specs(width):
    owner = lambda p, t_ref: t_ref[0] ^ turn(p)
    return [
        pl.BlockSpec((PIECE, width), lambda p, t_ref: (owner(p, t_ref), 0)),
        pl.BlockSpec((PIECE, width), lambda p, t_ref: (7 - owner(p, t_ref), 0)),
    ]


def packed_specs():
    owner = lambda p, t_ref: t_ref[0] ^ turn(p)
    return [
        pl.BlockSpec((PIECE, 2 * HEADW), lambda p, t_ref: (owner(p, t_ref), 0)),
        pl.BlockSpec((PIECE, 2 * HEADW), lambda p, t_ref: (3 - owner(p, t_ref), 0)),
    ]


def unpack(low, high):
    return jnp.concatenate([low[:, :HEADW], high[:, HEADW:]], axis=0)


def pack(pair):
    rows = pair.shape[0] // 2
    return jnp.concatenate([pair[:rows], pair[rows:]], axis=1)


def split_heads(normed, w_ref, cosine, sine, guard, q_ref, k_ref, v_ref):
    y = dot_nn(normed, w_ref[:, :SLAB])
    first, second = y[:, :128], y[:, 128:256]
    turned_first = first * cosine - second * sine
    turned_second = second * cosine + first * sine
    for head in range(GROUP + 1):
        columns = slice(32 * head, 32 * head + 32)
        both = jnp.concatenate([turned_first[:, columns], turned_second[:, columns]], axis=1)
        if head < GROUP:
            both = both.astype(bf16).astype(f32) * HD ** (-0.5)
            q_ref[head] = jnp.concatenate([both, guard[:, :HD]], axis=1).astype(bf16)
        else:
            k_ref[...] = jnp.concatenate([both, guard[:, HD:]], axis=1).astype(bf16)
    v_ref[...] = y[:, 256:].astype(bf16)


def guards(length_ref, valid_ref, rows):
    row = pl.program_id(0) * rows + lax.broadcasted_iota(jnp.int32, (rows, 128), 0)
    lane = lax.broadcasted_iota(jnp.int32, (rows, 128), 1)
    end_one = length_ref[0]
    end_two = end_one + length_ref[1]
    sequence = (row >= end_one).astype(jnp.int32) + (row >= end_two).astype(jnp.int32)
    query = jnp.where((lane == sequence) | (lane == 3), 1.0, 0.0)
    shut = ((lane >= HD) & (lane < HD + 3) & (lane - HD != sequence)) | ((lane == HD + 3) & (valid_ref[...] != 1))
    return jnp.where(lane < HD, query, jnp.where(shut, -(2.0**100), 0.0))


def proj_own_body(length_ref, x_ref, gain_ref, w_ref, cos_ref, sin_ref, valid_ref, normed_ref, q_ref, k_ref, v_ref):
    x = x_ref[...].astype(f32)
    factor = lax.rsqrt(jnp.mean(x * x, axis=-1, keepdims=True) + norm_eps)
    normed = (x * factor * gain_ref[0:1, :]).astype(bf16)
    normed_ref[...] = normed
    guard = guards(length_ref, valid_ref, x.shape[0])
    split_heads(normed, w_ref, cos_ref[...], sin_ref[...], guard, q_ref, k_ref, v_ref)


def proj_shared_body(length_ref, normed_ref, w_ref, cos_ref, sin_ref, valid_ref, q_ref, k_ref, v_ref):
    guard = guards(length_ref, valid_ref, normed_ref.shape[0])
    split_heads(normed_ref[...], w_ref, cos_ref[...], sin_ref[...], guard, q_ref, k_ref, v_ref)


def project(lengths, x, gain, weight, cosine, sine, valid):
    rows = x.shape[0]
    step = 2 * PIECE
    by_step = lambda width: pl.BlockSpec((step, width), lambda i, *scalars: (i, 0))
    outs = [
        (jax.ShapeDtypeStruct((GROUP, rows, 128), bf16), pl.BlockSpec((GROUP, step, 128), lambda i, *scalars: (0, i, 0))),
        (jax.ShapeDtypeStruct((rows, 128), bf16), by_step(128)),
        (jax.ShapeDtypeStruct((rows, HD), bf16), by_step(HD)),
    ]
    if gain is not None:
        outs = [(jax.ShapeDtypeStruct(x.shape, bf16), by_step(D))] + outs
    gains = [] if gain is None else [gain]
    return kernel_call(
        proj_shared_body if gain is None else proj_own_body,
        [lengths],
        [x, *gains, weight, cosine, sine, valid],
        out_shape=[shape for shape, _ in outs],
        grid=(rows // step,),
        in_specs=[by_step(D)]
        + [whole_spec((2, D))] * len(gains)
        + [whole_spec(weight.shape), by_step(128), by_step(128), by_step(128)],
        out_specs=[spec for _, spec in outs],
        name="project",
        far=True,
        far_out=True,
    )


def lanes_of(rows):
    return -(-GROUP * rows // 128) * 128


def start_of(row, length_ref):
    end_one = length_ref[0]
    end_two = end_one + length_ref[1]
    return jnp.where(row >= end_two, end_two, jnp.where(row >= end_one, end_one, 0))


def lane_rows(block, rows, length_ref):
    lane = lax.broadcasted_iota(jnp.int32, (1, lanes_of(rows)), 1)
    head = sum((lane >= h * rows).astype(jnp.int32) for h in range(1, GROUP + 1))
    row = jnp.where(head < GROUP, block * rows + lane - head * rows, 1 << 20)
    return row, jnp.where(head < GROUP, start_of(row, length_ref), 1 << 20)


def key_range(block, rows, length_ref):
    first = start_of(block * rows, length_ref) // KEYS
    return first, (block * rows + rows + KEYS - 1) // KEYS


def key_mask(shut, at, row, start):
    index = at + lax.broadcasted_iota(jnp.int32, (KEYS, row.shape[1]), 0)
    return ((index >= start) & (index <= row) & (shut == 0.0)) | (index == row)


def fill(stacked, lanes):
    parts = [stacked[head] for head in range(GROUP)]
    missing = lanes - GROUP * stacked[0].shape[0]
    if missing:
        parts.append(jnp.zeros((missing, parts[0].shape[1]), bf16))
    return jnp.concatenate(parts, axis=0)


def forward_body(length_ref, block_ref, q_ref, k_ref, v_ref, out_ref, log_ref, acc):
    rows = q_ref.shape[1]
    lanes = acc.shape[1]
    block = block_ref[pl.program_id(0)]
    q = fill(q_ref[...], lanes)
    row, start = lane_rows(block, rows, length_ref)
    acc[...] = jnp.zeros_like(acc)

    def step(carry, here, scores):
        peak, total = carry
        new_peak = jnp.maximum(peak, jnp.max(scores, axis=0, keepdims=True))
        exponent = jnp.exp(scores - new_peak)
        shrink = jnp.exp(peak - new_peak)
        total = total * shrink + jnp.sum(exponent, axis=0, keepdims=True)
        acc[...] = acc[...] * shrink + dot_tn(v_ref[here, :], exponent.astype(bf16))
        return new_peak, total

    def before(j, carry):
        here = pl.ds(pl.multiple_of(j * KEYS, KEYS), KEYS)
        return step(carry, here, dot_nt(k_ref[here, :], q))

    def across(j, carry):
        at = pl.multiple_of(j * KEYS, KEYS)
        here = pl.ds(at, KEYS)
        scores = dot_nt(k_ref[here, :HD], q[:, :HD])
        return step(carry, here, jnp.where(key_mask(k_ref[here, HD + 3 : HD + 4].astype(f32), at, row, start), scores, -1e30))

    low, high = key_range(block, rows, length_ref)
    middle = jnp.maximum(low, block * rows // KEYS)
    carry = (jnp.full((1, lanes), -1e30, f32), jnp.zeros((1, lanes), f32))
    peak, total = lax.fori_loop(middle, high, across, lax.fori_loop(low, middle, before, carry))
    log_ref[0] = peak + jnp.log(total)
    attended = jnp.transpose(acc[...] / total)
    attended = jnp.concatenate(
        [attended[head * rows : (head + 1) * rows] for head in range(GROUP)], axis=1
    ).astype(bf16)
    half = out_ref.shape[0]
    chunk = min(rows, 128) if half > rows else rows
    for part in range(rows // chunk):
        at = pl.program_id(0) * rows + part * chunk
        piece = attended[part * chunk : (part + 1) * chunk]

        @pl.when(at < half)
        def _():
            out_ref[pl.ds(pl.multiple_of(at, chunk), chunk), :HEADW] = piece

        @pl.when(at >= half)
        def _():
            out_ref[pl.ds(pl.multiple_of(at - half, chunk), chunk), HEADW:] = piece


def attend_forward(lengths, blocks, size, q, k, v):
    count, rows = blocks.shape[0], k.shape[0]
    lanes = lanes_of(size)
    return kernel_call(
        forward_body,
        [lengths, blocks],
        [q, k, v],
        out_shape=[
            jax.ShapeDtypeStruct((count * size // 2, 2 * HEADW), bf16),
            jax.ShapeDtypeStruct((count, 1, lanes), f32),
        ],
        grid=(count,),
        in_specs=[
                pl.BlockSpec((GROUP, size, 128), lambda i, lengths, blocks: (0, blocks[i], 0)),
                whole_spec((rows, 128)), whole_spec((rows, HD)),
            ],
        out_specs=[
                whole_spec((count * size // 2, 2 * HEADW)),
                pl.BlockSpec((1, 1, lanes), lambda i, *scalars: (i, 0, 0)),
            ],
        scratch_shapes=[pltpu.VMEM((HD, lanes), f32)],
        name="attend_forward",
        far=True,
        far_out=True,
    )


def backward_block(block, rows, length_ref, q, k_ref, v_ref, logs, attended, upstream, cosine, sine, dk, dv, acc):
    lanes = q.shape[0]
    row, start = lane_rows(block, rows, length_ref)
    heads = lambda wide: fill([wide[:, h * HD : (h + 1) * HD] for h in range(GROUP)], lanes)
    up = heads(upstream)
    both = up.astype(f32) * heads(attended).astype(f32)
    both_high = both.astype(bf16)
    both_low = (both - both_high.astype(f32)).astype(bf16)
    ones = jnp.ones((8, HD), bf16)
    inner = (dot_nt(ones, both_high) + dot_nt(ones, both_low))[:1]
    acc[...] = jnp.zeros_like(acc)

    heads_only = q[:, :HD]

    def step(here, scores):
        probs = jnp.exp(scores - logs)
        d_probs = dot_nt(v_ref[here, :], up)
        d_scores = (probs * (d_probs - inner)).astype(bf16)
        dv[here, :] += dot_nn(probs.astype(bf16), up)
        dk[here, :] += dot_nn(d_scores, heads_only)
        acc[...] += dot_tn(k_ref[here, :HD], d_scores)

    def before(j, carry):
        here = pl.ds(pl.multiple_of(j * KEYS, KEYS), KEYS)
        step(here, dot_nt(k_ref[here, :], q))
        return carry

    def across(j, carry):
        at = pl.multiple_of(j * KEYS, KEYS)
        here = pl.ds(at, KEYS)
        scores = dot_nt(k_ref[here, :HD], heads_only)
        step(here, jnp.where(key_mask(k_ref[here, HD + 3 : HD + 4].astype(f32), at, row, start), scores, -1e30))
        return carry

    low, high = key_range(block, rows, length_ref)
    middle = jnp.maximum(low, block * rows // KEYS)
    lax.fori_loop(low, middle, before, 0)
    lax.fori_loop(middle, high, across, 0)
    turned = jnp.transpose(acc[...] * HD ** (-0.5))
    first = jnp.concatenate([turned[h * rows : (h + 1) * rows, :32] for h in range(GROUP)], axis=1)
    second = jnp.concatenate([turned[h * rows : (h + 1) * rows, 32:] for h in range(GROUP)], axis=1)
    cosine, sine = cosine[:, :96], sine[:, :96]
    return first * cosine + second * sine, second * cosine - first * sine


def turn_back(dk, cosine, sine):
    first, second = dk[:, :32], dk[:, 32:]
    cosine, sine = cosine[:, :32], sine[:, :32]
    return first * cosine + second * sine, second * cosine - first * sine


def rows_at(block):
    return pl.ds(pl.multiple_of(block * PIECE, PIECE), PIECE)


def attended_rows(out_ref, at, rows):
    half = out_ref.shape[0]
    parts = []
    for part in range(rows // 128):
        here = at + part * 128
        low = pl.multiple_of(jnp.where(here < half, here, here - half), 128)
        both = out_ref[pl.ds(low, 128), :]
        parts.append(jnp.where(here < half, both[:, :HEADW], both[:, HEADW:]))
    return jnp.concatenate(parts, axis=0)


def backward_own_body(
    t_ref, length_ref, q_ref, k_ref, v_ref, log_ref, out_ref, up_0, up_1, up_2, up_3, weight_ref, cos_ref, sin_ref, shared_ref,
    slab_ref, *rest
):
    send_refs, mine_ref, (dk, dv, acc, upstream) = rest[:3], rest[3], rest[4:]
    rows = q_ref.shape[1]
    step = pl.program_id(0)
    t = t_ref[0]
    block = pl.num_programs(0) - 1 - step

    @pl.when(step == 0)
    def _():
        dk[...] = jnp.zeros_like(dk)
        dv[...] = jnp.zeros_like(dv)
        weight = out_weight(weight_ref)
        for k, piece in enumerate((up_0, up_1, up_2, up_3)):
            d_attended = dot_nn(piece[...], weight).astype(bf16)
            upstream[rows_at(t ^ k), :] = d_attended[:PIECE]
            upstream[rows_at(7 - (t ^ k)), :] = d_attended[PIECE:]

    cosine, sine = cos_ref[...], sin_ref[...]
    here = pl.ds(pl.multiple_of(block * rows, rows), rows)
    q = fill(q_ref[...], acc.shape[1])
    first, second = backward_block(
        block, rows, length_ref, q, k_ref, v_ref, log_ref[0], attended_rows(out_ref, block * rows, rows),
        upstream[here, :], cosine, sine, dk, dv, acc,
    )
    key_first, key_second = turn_back(dk[here, :], cosine, sine)
    slab_ref[here, :] = jnp.concatenate([first, key_first, second, key_second, dv[here, :]], axis=1).astype(bf16)

    @pl.when(step == pl.num_programs(0) - 1)
    def _():
        for half, owner in enumerate((t, 7 - t)):
            mine_ref[half * PIECE : (half + 1) * PIECE, :] = slab_ref[rows_at(owner), :]
        for k, target in enumerate(send_refs):
            for half, owner in enumerate((t ^ (k + 1), 7 - (t ^ (k + 1)))):
                own, shared = slab_ref[rows_at(owner), :], shared_ref[rows_at(owner), :]
                target[half * PIECE : (half + 1) * PIECE, :] = jnp.concatenate(
                    [own, shared[:, 96:128], shared[:, 224:256], shared[:, 256:], jnp.zeros((PIECE, 64), bf16)], axis=1
                )


def attend_backward_own(t, lengths, q, k, v, logs, attended, pieces, weight, cosine, sine, shared):
    rows = k.shape[0]
    size = KEYS
    count, lanes = rows // size, lanes_of(size)
    at = lambda i: count - 1 - i
    by_step = lambda width: pl.BlockSpec((size, width), lambda i, *scalars: (at(i), 0))
    return kernel_call(
        backward_own_body,
        [t, lengths],
        [q, k, v, logs, attended, *pieces, weight, cosine, sine, shared],
        out_shape=[jax.ShapeDtypeStruct((rows, SLAB), bf16)]
        + [jax.ShapeDtypeStruct((2 * PIECE, WIDE), bf16)] * 3
        + [jax.ShapeDtypeStruct((2 * PIECE, SLAB), bf16)],
        grid=(count,),
        in_specs=[
                pl.BlockSpec((GROUP, size, 128), lambda i, *scalars: (0, at(i), 0)),
                whole_spec((rows, 128)), whole_spec((rows, HD)),
                pl.BlockSpec((1, 1, lanes), lambda i, *scalars: (at(i), 0, 0)), whole_spec((rows // 2, 2 * HEADW)),
            ]
            + [whole_spec((2 * PIECE, D))] * 4
            + [whole_spec(weight.shape)]
            + [by_step(128)] * 2
            + [whole_spec((rows, SLAB))],
        out_specs=[whole_spec((rows, SLAB))] + [whole_spec((2 * PIECE, WIDE))] * 3 + [whole_spec((2 * PIECE, SLAB))],
        scratch_shapes=[
                pltpu.VMEM((rows, HD), f32), pltpu.VMEM((rows, HD), f32), pltpu.VMEM((HD, lanes), f32),
                pltpu.VMEM((rows, HEADW), bf16),
            ],
        name="attend_backward_own",
        far_out=True,
    )


def backward_shared_body(
    t_ref, length_ref, block_ref, q_ref, k_ref, v_ref, log_ref, out_ref, up_ref, cos_ref, sin_ref, cos_all, sin_all,
    slab_ref, mine_ref, dk, dv, acc
):
    step = pl.program_id(0)
    t = t_ref[0]
    block = block_ref[step]

    @pl.when(step == 0)
    def _():
        dk[...] = jnp.zeros_like(dk)
        dv[...] = jnp.zeros_like(dv)
        slab_ref[...] = jnp.zeros_like(slab_ref)

    half = lambda ref: jnp.where(step == 0, ref[:, :HEADW], ref[:, HEADW:])
    first, second = backward_block(
        block, PIECE, length_ref, fill(q_ref[...], acc.shape[1]), k_ref, v_ref, log_ref[0], half(out_ref), half(up_ref),
        cos_ref[...], sin_ref[...], dk, dv, acc,
    )
    slab_ref[rows_at(block), :96] = first.astype(bf16)
    slab_ref[rows_at(block), 128:224] = second.astype(bf16)

    @pl.when(step == pl.num_programs(0) - 1)
    def _():
        key_first, key_second = turn_back(dk[...], cos_all[...], sin_all[...])
        slab_ref[:, 96:128] = key_first.astype(bf16)
        slab_ref[:, 224:256] = key_second.astype(bf16)
        slab_ref[:, 256:] = dv[...].astype(bf16)
        mine_ref[:PIECE, :] = slab_ref[rows_at(t), :]
        mine_ref[PIECE:, :] = slab_ref[rows_at(7 - t), :]


def attend_backward_shared(t, lengths, blocks, q, k, v, logs, attended, upstream, cosine, sine):
    rows = k.shape[0]
    lanes = lanes_of(PIECE)
    mine = whole_spec((PIECE, 2 * HEADW))
    natural = pl.BlockSpec((PIECE, 128), lambda i, t_ref, length_ref, block_ref: (block_ref[i], 0))
    return kernel_call(
        backward_shared_body,
        [t, lengths, blocks],
        [q, k, v, logs, attended, upstream, cosine, sine, cosine, sine],
        out_shape=[jax.ShapeDtypeStruct((rows, SLAB), bf16), jax.ShapeDtypeStruct((2 * PIECE, SLAB), bf16)],
        grid=(2,),
        in_specs=[
                pl.BlockSpec((GROUP, PIECE, 128), lambda i, t_ref, length_ref, block_ref: (0, block_ref[i], 0)),
                whole_spec((rows, 128)), whole_spec((rows, HD)),
                pl.BlockSpec((1, 1, lanes), lambda i, *scalars: (i, 0, 0)), mine, mine,
            ]
            + [natural] * 2
            + [whole_spec((rows, 128))] * 2,
        out_specs=[whole_spec((rows, SLAB)), whole_spec((2 * PIECE, SLAB))],
        scratch_shapes=[pltpu.VMEM((rows, HD), f32), pltpu.VMEM((rows, HD), f32), pltpu.VMEM((HD, lanes), f32)],
        name="attend_backward_shared",
        far=True,
    )


def whole_spec(shape):
    return pl.BlockSpec(shape, lambda i, *scalars: (0,) * len(shape))


def out_weight(weight):
    if weight.shape[0] == D:
        return weight[:, SLAB:]
    return jnp.concatenate([weight[:, :HEADW], weight[:, HEADW:]], axis=0)


def out_body(t_ref, x_a, x_b, gain_ref, *refs):
    owns, shares, weights = refs[:8], refs[8:12], refs[12:17]
    mine_ref, normed_ref, w_out = refs[17:]
    step = pl.program_id(0)

    @pl.when(step == 0)
    def _():
        w_out[...] = jnp.concatenate([out_weight(weight) for weight in weights], axis=1)

    middle = jnp.concatenate([x_a[...], x_b[...]], axis=0).astype(f32)
    heads = [unpack(owns[2 * k][...], owns[2 * k + 1][...]) for k in range(4)]
    share = jnp.where(
        step == 0, shares[0][...],
        jnp.where(step == 1, shares[2][...], jnp.where(step == 2, shares[1][...], shares[3][...])),
    )
    middle = middle + dot_nt(jnp.concatenate(heads + [unpack(share, share)], axis=1), w_out[...])
    factor = lax.rsqrt(jnp.mean(middle * middle, axis=-1, keepdims=True) + norm_eps)
    normed_ref[...] = (middle * factor * gain_ref[1:2, :]).astype(bf16)

    @pl.when(step == 0)
    def _():
        mine_ref[...] = middle


def out_project(t, x, gain, owns, shares, weights):
    rows = x.shape[0]
    return kernel_call(
        out_body,
        [t],
        [x, x, gain, *[piece for piece in owns for _ in range(2)], *shares, *weights],
        out_shape=[jax.ShapeDtypeStruct((2 * PIECE, D), f32), jax.ShapeDtypeStruct(x.shape, bf16)],
        grid=(4,),
        in_specs=pair_specs(D)
        + [whole_spec((2, D))]
        + packed_specs() * 4
        + [whole_spec((PIECE, 2 * HEADW))] * 4
        + [whole_spec(weight.shape) for weight in weights],
        out_specs=[whole_spec((2 * PIECE, D)), pl.BlockSpec((2 * PIECE, D), lambda p, t_ref: (p, 0))],
        scratch_shapes=[pltpu.VMEM((D, D), bf16)],
        name="out_project",
    )


def feed_body(
    normed_ref, cot_ref, w_ref, hidden_ref, d_ref, kept_ref, sent_ref, terms_kept_ref, terms_sent_ref
):
    step = pl.program_id(0)
    width = hidden_ref.shape[1]
    w_gate, w_up, w_out = (w_ref[:, width * part : width * (part + 1)] for part in range(3))
    normed = normed_ref[...]
    gate = dot_nn(normed, w_gate)
    up = dot_nn(normed, w_up)
    d_hidden = dot_nn(cot_ref[...], w_out)
    sigmoid = 1.0 / (1.0 + jnp.exp(-gate))
    silu = gate * sigmoid
    hidden = (silu * up).astype(bf16)
    d_gate = (d_hidden * up * sigmoid * (1.0 + gate * (1.0 - sigmoid))).astype(bf16)
    d_up = (d_hidden * silu).astype(bf16)
    hidden_ref[...] = hidden
    d_ref[:, :width] = d_gate
    d_ref[:, width:] = d_up
    back = (dot_nt(d_gate, w_gate) + dot_nt(d_up, w_up)).astype(bf16)
    terms = dot_nt(hidden, w_out).astype(bf16)

    @pl.when(step < 2)
    def _():
        sent_ref[0] = back
        terms_sent_ref[0] = terms

    @pl.when(step >= 2)
    def _():
        kept_ref[0] = back
        terms_kept_ref[0] = terms


def feed_forward(normed, cotangent, weights):
    rows, width = normed.shape[0], weights.shape[1] // 3
    at = lambda i: (i + 2) % 4
    by_step = lambda columns: pl.BlockSpec((2 * PIECE, columns), lambda i: (at(i), 0))
    pair = jax.ShapeDtypeStruct((2, 2 * PIECE, D), bf16)
    kept = pl.BlockSpec((1, 2 * PIECE, D), lambda i: (jnp.maximum(i - 2, 0), 0, 0))
    sent = pl.BlockSpec((1, 2 * PIECE, D), lambda i: (jnp.minimum(i, 1), 0, 0))
    return kernel_call(
        feed_body,
        [],
        [normed, cotangent, weights],
        out_shape=[jax.ShapeDtypeStruct((rows, width), bf16), jax.ShapeDtypeStruct((rows, 2 * width), bf16)] + [pair] * 4,
        grid=(4,),
        in_specs=[by_step(D), by_step(D), whole_spec(weights.shape)],
        out_specs=[by_step(width), by_step(2 * width), kept, sent, kept, sent],
        name="feed_forward",
    )


def feed_grad_body(normed_ref, cot_ref, d_ref, hidden_ref, grad_ref):
    step = pl.program_id(0)

    @pl.when(step < 2)
    def _():
        grad_ref[...] = dot_tn(normed_ref[...], d_ref[...]).astype(bf16)

    @pl.when(step == 2)
    def _():
        grad_ref[...] = dot_tn(cot_ref[...], hidden_ref[...]).astype(bf16)


def feed_grads(normed, cotangent, d_gate_up, hidden):
    rows, width = hidden.shape
    return kernel_call(
        feed_grad_body,
        [],
        [normed, cotangent, d_gate_up, hidden],
        out_shape=jax.ShapeDtypeStruct((D, 3 * width), bf16),
        grid=(3,),
        in_specs=[
            whole_spec((rows, D)), whole_spec((rows, D)),
            pl.BlockSpec((rows, width), lambda i: (0, jnp.minimum(i, 1))), whole_spec((rows, width)),
        ],
        out_specs=pl.BlockSpec((D, width), lambda i: (0, i)),
        name="feed_grads",
        far_out=True,
    )


def far_body(kept_ref, came_ref, far_ref):
    far_ref[...] = (kept_ref[0].astype(f32) + came_ref[0].astype(f32)).astype(bf16)


def far_part(kept, came):
    shape = kept.shape[1:]
    second = pl.BlockSpec((1,) + shape, lambda i: (1, 0, 0))
    return kernel_call(
        far_body,
        [],
        [kept, came],
        out_shape=jax.ShapeDtypeStruct(shape, bf16),
        grid=(1,),
        in_specs=[second] * 2,
        out_specs=whole_spec(shape),
        name="far_part",
        far=True,
        far_out=True,
    )


def first_spec(x):
    return pl.BlockSpec((1,) + x.shape[1:], lambda i, *scalars: (0,) * x.ndim)


def norm_back(values, gain, upstream):
    factor = lax.rsqrt(jnp.mean(values * values, axis=-1, keepdims=True) + norm_eps)
    weighted = upstream * gain
    inner = jnp.mean(weighted * values, axis=-1, keepdims=True)
    return factor * weighted - values * factor**3 * inner


def total_of(kept_ref, came_ref, far_ref):
    return kept_ref[0].astype(f32) + came_ref[0].astype(f32) + far_ref[...].astype(f32)


def layer_body(middle_ref, kept_ref, came_ref, far_ref, out_ref):
    out_ref[...] = (middle_ref[...] + total_of(kept_ref, came_ref, far_ref)).astype(bf16)


def layer_rows(middle, kept, came, far):
    top = whole_spec(middle.shape)
    return kernel_call(
        layer_body,
        [],
        [middle, kept, came, far],
        out_shape=jax.ShapeDtypeStruct(middle.shape, bf16),
        grid=(1,),
        in_specs=[top, first_spec(kept), first_spec(came), top],
        out_specs=top,
        name="layer_rows",
    )


def middle_body(kept_ref, came_ref, far_ref, middle_ref, up_ref, gain_ref, weight_ref, d_middle_ref, d_branch_ref, d_ref):
    upstream = total_of(kept_ref, came_ref, far_ref)
    d_middle = up_ref[...].astype(f32) + norm_back(middle_ref[...], gain_ref[1:2, :], upstream)
    d_middle_ref[...] = d_middle
    d_branch = d_middle.astype(bf16)
    d_branch_ref[...] = d_branch
    d_ref[...] = pack(dot_nn(d_branch, weight_ref[:, SLAB:]).astype(bf16))


def middle_backward(kept, came, far, middle, upstream, gain, shared_block):
    rows = far.shape[0]
    top = whole_spec((rows, D))
    packed = (rows // 2, 2 * HEADW)
    return kernel_call(
        middle_body,
        [],
        [kept, came, far, middle, upstream, gain, shared_block],
        out_shape=[
            jax.ShapeDtypeStruct((rows, D), f32), jax.ShapeDtypeStruct((rows, D), bf16), jax.ShapeDtypeStruct(packed, bf16),
        ],
        grid=(1,),
        in_specs=[first_spec(kept), first_spec(came)] + [top] * 3 + [whole_spec((2, D)), whole_spec(shared_block.shape)],
        out_specs=[top, top, whole_spec(packed)],
        name="middle_backward",
        far=True,
        far_out=True,
    )


def early_body(t_ref, d_branch_ref, share_ref, normed_ref, slab_ref, kept_ref, sent_ref, block):
    t = t_ref[0]
    share = share_ref[...]
    block[...] = jnp.concatenate(
        [dot_tn(normed_ref[...], slab_ref[...]), dot_tn(d_branch_ref[...], unpack(share, share))], axis=1
    ).astype(bf16)
    for k in range(4):
        at = pl.multiple_of((t ^ k) * 128, 128)
        (kept_ref, sent_ref)[k & 1][k // 2] = block[:, pl.ds(at, 128)]


def early_grads(t, d_branch, share, normed, slab):
    arrays = [d_branch, share, normed, slab]
    pair = jax.ShapeDtypeStruct((2, D, 128), bf16)
    return kernel_call(
        early_body,
        [t],
        arrays,
        out_shape=[pair, pair],
        grid=(1,),
        in_specs=[whole_spec(x.shape) for x in arrays],
        out_specs=[whole_spec(pair.shape)] * 2,
        scratch_shapes=[pltpu.VMEM((D, WIDE), bf16)],
        name="early_grads",
        far_out=True,
    )


def attn_grad_body(me_ref, t_ref, normed_ref, slab_ref, early_kept_ref, came_ref, far_ref, *refs):
    branches, owns, kept_ref, sent_ref = refs[:4], refs[4:12], refs[12], refs[13]
    early = total_of(early_kept_ref, came_ref, far_ref)
    grad = dot_tn(normed_ref[...], slab_ref[...])
    out = dot_tn(branches[0][...], unpack(owns[0][...], owns[1][...]))
    for k in (1, 2, 3):
        out = out + dot_tn(branches[k][...], unpack(owns[2 * k][...], owns[2 * k + 1][...]))
    whole = jnp.concatenate([early, grad, out], axis=1)
    rows = kept_ref.shape[1]
    split_chunks(me_ref, [whole[rows * j : rows * (j + 1)] for j in range(D // rows)], kept_ref, sent_ref)


def owner_specs(k):
    return [
        pl.BlockSpec((PIECE, 2 * HEADW), lambda i, me_ref, t_ref: (t_ref[0] ^ k, 0)),
        pl.BlockSpec((PIECE, 2 * HEADW), lambda i, me_ref, t_ref: (3 - (t_ref[0] ^ k), 0)),
    ]


def attn_grads(me, t, normed, slab, kept, came, far, branches, attended):
    half = jax.ShapeDtypeStruct((4, D // 8, WIDE + 128), bf16)
    arrays = [normed, slab, kept, came, far, *branches]
    return kernel_call(
        attn_grad_body,
        [me, t],
        arrays + [attended] * 8,
        out_shape=[half, half],
        grid=(1,),
        in_specs=[first_spec(x) if x.ndim == 3 else whole_spec(x.shape) for x in arrays]
        + [spec for k in range(4) for spec in owner_specs(k)],
        out_specs=[whole_spec(half.shape)] * 2,
        name="attn_grads",
    )


def input_body(t_ref, x_a, x_b, d_middle_ref, gain_ref, own_ref, shared_ref, *refs):
    came_refs, slabs, shared_slab, out_ref = refs[:3], refs[3:7], refs[7], refs[8]
    upstream = dot_nt(own_ref[...], slabs[0][0, :, :SLAB])
    for piece, slab in zip(came_refs, slabs[1:4]):
        upstream = upstream + dot_nt(piece[:, :SLAB], slab[0, :, :SLAB])
    shared = shared_ref[...]
    key_value = jnp.concatenate([shared[:, 96:128], shared[:, 224:256], shared[:, 256:]], axis=1).astype(f32)
    for piece in came_refs:
        key_value = key_value + piece[:, SLAB : SLAB + 2 * HD].astype(f32)
    key_value = key_value.astype(bf16)
    shared = jnp.concatenate(
        [shared[:, :96], key_value[:, :32], shared[:, 128:224], key_value[:, 32:64], key_value[:, 64:]], axis=1
    )
    upstream = upstream + dot_nt(shared, shared_slab[:, :SLAB])
    x = jnp.concatenate([x_a[...], x_b[...]], axis=0).astype(f32)
    out_ref[...] = (d_middle_ref[...] + norm_back(x, gain_ref[0:1, :], upstream)).astype(bf16)


def input_backward(t, x, d_middle, gain, own, shared, came, slabs, shared_block):
    rows = 2 * PIECE
    of_owner = [
        pl.BlockSpec((1, D, 384), functools.partial(lambda k, i, t_ref: (t_ref[0] ^ k, 0, 0), k)) for k in range(4)
    ]
    return kernel_call(
        input_body,
        [t],
        [x, x, d_middle, gain, own, shared, *came, *[slabs] * 4, shared_block],
        out_shape=jax.ShapeDtypeStruct((rows, D), bf16),
        grid=(1,),
        in_specs=pair_specs(D)
        + [whole_spec((rows, D)), whole_spec((2, D))]
        + [whole_spec((rows, SLAB))] * 2
        + [whole_spec((rows, WIDE))] * 3
        + of_owner
        + [pl.BlockSpec((D, 384), lambda i, *scalars: (0, 0))],
        out_specs=whole_spec((rows, D)),
        name="input_backward",
        far=True,
    )


MATRIX_RATE = 0.5 * D ** (-0.5)
OUTPUT_RATE = 0.5 * OUT_FAN ** (-0.5)
FEED_RATE = 0.5 * FF ** (-0.5)


def adam_step(weight, first, second, average, gradient, step_rate, decay_rate):
    first_new = beta_first * first + (1.0 - beta_first) * gradient
    second_new = beta_second * second + (1.0 - beta_second) * gradient * gradient
    corrected_first = first_new / (1.0 - beta_first**STEP)
    corrected_second = second_new / (1.0 - beta_second**STEP)
    weight_new = weight - step_rate * (
        corrected_first / (jnp.sqrt(corrected_second) + adam_eps) + decay_rate * weight
    )
    average_new = average_keep * average + (1.0 - average_keep) * weight_new
    return (first_new, second_new, weight_new, average_new)


def adam_steps(count):
    return count // 40 if count % 40 == 0 else 1


def feed_adam_body(grad_ref, *refs):
    in_state, ffn_state, in_outs, ffn_outs, term_ref = refs[:4], refs[4:8], refs[8:13], refs[13:18], refs[18]
    width = ffn_state[0].shape[1]

    def total(part):
        return grad_ref[:, part * width : (part + 1) * width].astype(f32)

    term = 0.0
    for half in range(2):
        gradient = total(half)
        state = [ref[:, half, :] for ref in in_state]
        term = term + jnp.sum(state[0].astype(bf16).astype(f32) * gradient, axis=1, keepdims=True)
        for ref, value in zip(in_outs, (gradient,) + adam_step(*state, gradient, MATRIX_RATE, 0.1)):
            ref[:, half, :] = value
    gradient = total(2)
    state = [ref[...] for ref in ffn_state]
    for ref, value in zip(ffn_outs, (gradient,) + adam_step(*state, gradient, FEED_RATE, 0.1)):
        ref[...] = value
    high = term.astype(bf16).astype(f32)
    lane = lax.broadcasted_iota(jnp.int32, term_ref.shape, 1)
    term_ref[...] = jnp.where(lane == 0, high, jnp.where(lane == 1, term - high, 0.0)).astype(bf16)


def feed_adam(gradient, in_state, ffn_state):
    rows, width = ffn_state[0].shape
    steps = adam_steps(rows)
    each = rows // steps
    flat = lambda columns: pl.BlockSpec((each, columns), lambda i: (i, 0))
    pair = pl.BlockSpec((each, 2, width), lambda i: (i, 0, 0))
    outs = kernel_call(
        feed_adam_body,
        [],
        [gradient, *in_state, *ffn_state],
        out_shape=[jax.ShapeDtypeStruct((rows, 2, width), f32)] * 5
        + [jax.ShapeDtypeStruct((rows, width), f32)] * 5
        + [jax.ShapeDtypeStruct((rows, 128), bf16)],
        grid=(steps,),
        in_specs=[flat(3 * width)] + [pair] * 4 + [flat(width)] * 4,
        out_specs=[pair] * 5 + [flat(width)] * 5 + [flat(128)],
        name="feed_adam",
        far=True,
    )
    return outs[:10], outs[10]


def attn_adam_body(t_ref, group_ref, *refs):
    pieces, query_state, keyval_state, output_state, gain_state = (
        refs[:4], refs[4:8], refs[8:12], refs[12:16], refs[16:20],
    )
    query_outs, keyval_outs, output_outs, gain_outs = refs[20:25], refs[25:30], refs[30:35], refs[35:40]
    query_grad, keyval_grad, output_grad, column, head_parts, group_parts = refs[40:]
    step, t = pl.program_id(0), t_ref[0]
    count = pieces[0].shape[0]

    @pl.when(step == 0)
    def _():
        column[...] = jnp.zeros_like(column)
        quarters = []
        for quarter in range(4):
            here = pieces[0][:, :128]
            for k in (1, 2, 3):
                here = jnp.where((t ^ k) == quarter, pieces[k][:, :128], here)
            quarters.append(here)
        shared = jnp.concatenate(quarters, axis=1)
        for k in range(5):
            group = KV - 1 if k == 4 else t ^ k
            block = (shared if k == 4 else pieces[k][:, 128 : 128 + WIDE]).astype(f32)
            for member in range(GROUP + 1):
                at = 32 * member
                whole = jnp.concatenate([block[:, at : at + 32], block[:, 128 + at : 160 + at]], axis=1)
                if member < GROUP:
                    head_parts[group * GROUP + member] = whole
                else:
                    group_parts[group] = jnp.concatenate([whole, block[:, 256:SLAB]], axis=1)
            turned = dot_nt(unit(HEADW), block[:, SLAB:].astype(bf16))
            for which in range(GROUP):
                at = pl.multiple_of(head_of(group, which, group_ref) * HD, HD)
                output_grad[pl.ds(at, HD), :] = turned[which * HD : (which + 1) * HD, :]
        query_grad[...] = jnp.concatenate([head_parts[group_ref[h]] for h in range(NQ)], axis=1)
        both = [group_parts[g] for g in range(KV)]
        keyval_grad[...] = jnp.concatenate([x[:, :HD] for x in both] + [x[:, HD:] for x in both], axis=1)

    each = query_state[0].shape[0]
    here = pl.ds(pl.multiple_of(step * each, 8), each) if each < count else slice(0, count)
    out_each = output_state[0].shape[0]
    out_here = pl.ds(pl.multiple_of(step * out_each, 8), out_each)
    term = 0.0
    for state_refs, outs, gradient, rate in (
        (query_state, query_outs, query_grad[here, :], MATRIX_RATE),
        (keyval_state, keyval_outs, keyval_grad[here, :], MATRIX_RATE),
        (output_state, output_outs, output_grad[out_here, :], OUTPUT_RATE),
    ):
        state = [ref[...] for ref in state_refs]
        if rate == MATRIX_RATE:
            term = term + jnp.sum(state[0].astype(bf16).astype(f32) * gradient, axis=1, keepdims=True)
        for ref, value in zip(outs, (gradient,) + adam_step(*state, gradient, rate, 0.1)):
            ref[...] = value
    lane = lax.broadcasted_iota(jnp.int32, (each, 128), 1)
    column[here, :] = jnp.where(lane == 0, term, 0.0)

    @pl.when(step == pl.num_programs(0) - 1)
    def _():
        second = 0.0
        for piece in pieces:
            second = second + piece[:, 128 + WIDE :].astype(f32)
        second = jnp.sum(second, axis=1, keepdims=True)
        lane = lax.broadcasted_iota(jnp.int32, (count, 128), 1)
        column[:count, :] = jnp.where(lane == 1, second, column[:count, :])
        terms = jnp.transpose(column[...])[:2, :count]
        state = [ref[...] for ref in gain_state]
        gradient = terms / state[0]
        for ref, value in zip(gain_outs, (gradient,) + adam_step(*state, gradient, 0.3, 0.0)):
            ref[...] = value


def attn_adam(t, query_group, pieces, query_state, keyval_state, output_state, gain_state):
    rows = query_state[0].shape[0]
    steps = adam_steps(rows)
    states = (query_state, keyval_state, output_state)
    specs = [
        pl.BlockSpec((x[0].shape[0] // steps, x[0].shape[1]), lambda i, *scalars: (i, 0)) for x in states
    ] + [whole_spec(gain_state[0].shape)]
    states = states + (gain_state,)
    outs = kernel_call(
        attn_adam_body,
        [t, query_group],
        [*pieces, *[x for state in states for x in state]],
        out_shape=[jax.ShapeDtypeStruct(state[0].shape, f32) for state in states for _ in range(5)],
        grid=(steps,),
        in_specs=[whole_spec(pieces[0].shape)] * 4 + [spec for spec in specs for _ in range(4)],
        out_specs=[spec for spec in specs for _ in range(5)],
        scratch_shapes=[
            pltpu.VMEM((rows, NQ * HD), f32), pltpu.VMEM((rows, 2 * KV * HD), f32), pltpu.VMEM((NQ * HD, rows), f32),
            pltpu.VMEM((128, 128), f32), pltpu.VMEM((NQ, rows, HD), f32), pltpu.VMEM((KV, rows, 2 * HD), f32),
        ],
        name="attn_adam",
        far=True,
    )
    return outs[:5], outs[5:10], outs[10:15], outs[15:20]


def local(
    tokens, cotangent, lengths, valid, query_group,
    w_query, w_keyval, w_output, w_ffn_in, w_ffn_out, norm_gains,
    first_query, first_keyval, first_output, first_ffn_in, first_ffn_out, first_gains,
    second_query, second_keyval, second_output, second_ffn_in, second_ffn_out, second_gains,
    average_query, average_keyval, average_output, average_ffn_in, average_ffn_out, average_gains,
):
    t = lax.axis_index("tensor").astype(jnp.int32)
    t_array = t.reshape(1)
    row_count = tokens.shape[0]
    owned_rows = w_query.shape[0]
    hidden_count = w_ffn_out.shape[0]

    me = lax.axis_index("dp").astype(jnp.int32).reshape(1)
    small = lax.axis_size("dp") == 8
    rest_rows = 8 if owned_rows % 8 == 0 else 17
    own_part = prepare(t_array, query_group, w_query, w_keyval, w_output, norm_gains, owned_rows + rest_rows)
    own_one = gather_one(own_part)
    length_row = lengths[0]
    seq_ends = jnp.cumsum(length_row)
    valid, seq_ends = after((valid, seq_ends), own_part)
    valid_wide = jnp.broadcast_to(valid[:, None], (row_count, 128))
    seq_ends = after(seq_ends, valid_wide)
    row_index = jnp.arange(row_count, dtype=jnp.int32)
    row_start = jnp.where(
        row_index >= seq_ends[1], seq_ends[1], jnp.where(row_index >= seq_ends[0], seq_ends[0], 0)
    )
    position = (row_index - row_start).astype(f32)
    frequency = rope_base ** (-jnp.arange(0, HD, 2, dtype=f32) / HD)
    angles = position[:, None] * jnp.tile(frequency, 4)[None, :]
    cosine, sine = jnp.cos(angles), jnp.sin(angles)
    tables = (cosine, sine, valid_wide)

    w_in_now, w_out_now = after((w_ffn_in, w_ffn_out), own_part)
    feed_part = jnp.concatenate(
        [w_in_now[:, 0].astype(bf16), w_in_now[:, 1].astype(bf16), jnp.transpose(w_out_now).astype(bf16)], axis=1
    )
    own_two = gather_two(after(own_one, (tables, feed_part)))
    feed_all = lax.all_gather(after(feed_part, (own_one, tables)), "dp", axis=0, tiled=True)

    own_cotangent = own_order(after(cotangent, feed_part), t_array)
    tokens = by_rows(after(tokens, feed_part))
    slab_own, out_own, quarter, gains = gather_end(after(own_two, (own_cotangent, tokens)), owned_rows)
    quarters = gather_first(quarter)

    normed_one, q_own, k_own, v_own = project(length_row, tokens, after(gains, quarters[1]), slab_own, cosine, sine, valid_wide)
    out_owns = gather_first(after(out_own, normed_one))
    blocks = jnp.arange(row_count // KEYS, dtype=jnp.int32)
    part_blocks = jnp.stack([t, 7 - t])
    q_own = after(q_own, out_owns[1])
    att_own, log_own = attend_forward(length_row, blocks, KEYS, q_own, k_own, v_own)
    att_owns = gather_first(att_own)
    quarters, out_owns = after((quarters, out_owns), att_own)
    quarters, out_owns = gather_second(quarters), gather_second(out_owns)
    shared_block = assemble(t_array, after(quarters, att_owns[1]))
    q_part, k_part, v_part = project(length_row, normed_one, None, shared_block, cosine, sine, valid_wide)
    att_part, log_part = attend_forward(length_row, part_blocks, PIECE, q_part, k_part, v_part)
    att_shares = [att_part] + exchange_tensor([att_part] * 3)
    att_owns = gather_second(after(att_owns, att_part))
    weights = out_owns + [shared_block]
    slabs = lax.all_gather(after(slab_own, (att_owns[2], out_owns[2])), "tensor", axis=0)
    middle_mine, normed_two = out_project(t_array, tokens, gains, att_owns, att_shares, weights)
    hidden, d_gate_up, two_kept, two_sent, terms_kept, terms_sent = feed_forward(
        normed_two, own_cotangent, after(feed_all, normed_two)
    )

    two_came = swap(two_sent, "tensor", 1)
    terms_came = swap(terms_sent, "tensor", 1)
    two_part = far_part(two_kept, two_came)
    two_far = swap(two_part, "tensor", 2)

    feed_grad = feed_grads(after(normed_two, two_part), own_cotangent, d_gate_up, hidden)

    own_rows = 2 * PIECE
    d_middle, d_branch, d_att_part = middle_backward(
        two_kept, two_came, after(two_far, (feed_grad, slabs)), middle_mine, own_cotangent, gains, shared_block
    )
    feed_sum = lax.psum_scatter(after(feed_grad, two_far), "dp", scatter_dimension=0, tiled=True)
    branches = gather_first(d_branch)
    d_shared, shared_mine = attend_backward_shared(
        t_array, length_row, part_blocks, q_part, k_part, v_part, log_part, att_part,
        after(d_att_part, branches[1]), cosine, sine,
    )
    terms_part = far_part(terms_kept, after(terms_came, d_shared))
    early_kept, early_sent = early_grads(t_array, d_branch, att_part, normed_one, after(d_shared, terms_part))
    early_came = swap(early_sent, "tensor", 1)
    early_part = far_part(early_kept, early_came)
    early_far = swap(early_part, "tensor", 2)
    branches = gather_second(after(branches, early_part))
    terms_far = swap(after(terms_part, branches[2]), "tensor", 2)
    d_own, *own_sent, own_mine = attend_backward_own(
        t_array, length_row, q_own, k_own, v_own, log_own, att_own, branches, out_own, cosine, sine, d_shared
    )
    own_came = exchange_tensor(own_sent)
    layer_mine = layer_rows(middle_mine, terms_kept, terms_came, after(terms_far, (d_own, early_far)))
    d_own = after(d_own, layer_mine)
    if small:
        attn_half = scatter_one(
            *attn_grads(
                me, t_array, normed_one, d_own, early_kept, early_came, early_far, branches, att_own
            )
        )
    else:
        early = early_kept[0].astype(f32) + early_came[0].astype(f32) + early_far.astype(f32)
        out_grad = 0.0
        for k in range(4):
            rows_of = [jnp.where(t >= 0, t ^ k, 0), 3 - (t ^ k)]
            low, high = (lax.dynamic_slice_in_dim(att_own, PIECE * at, PIECE, 0) for at in rows_of)
            out_grad = out_grad + dot_tn(branches[k], unpack(low, high))
        attn_half = (jnp.concatenate([early, dot_tn(normed_one, d_own), out_grad], axis=1),)
    layer_pieces = gather_tensor(layer_mine)
    attn_quarter = scatter_two(after(attn_half, layer_pieces))
    grad_mine = input_backward(
        t_array, tokens, d_middle, gains, own_mine, shared_mine, after(own_came, attn_quarter[0]), slabs, shared_block
    )
    grad_pieces = gather_first(grad_mine)
    layer_out = natural_order(after(layer_pieces, grad_mine), t_array)

    feed_results, gain_term = feed_adam(
        after(feed_sum, layer_out),
        (w_ffn_in, first_ffn_in, second_ffn_in, average_ffn_in),
        [jnp.transpose(x) for x in (w_ffn_out, first_ffn_out, second_ffn_out, average_ffn_out)],
    )
    in_results, out_results = feed_results[:5], [jnp.transpose(x) for x in feed_results[5:]]
    owned_attn = jnp.concatenate([scatter_end(after(attn_quarter, gain_term)).astype(bf16), gain_term], axis=1)
    attn_first = gather_first(owned_attn)
    input_grad = natural_order(gather_second(after(grad_pieces, attn_first[1])), t_array)
    attn_pieces = gather_second(after(attn_first, input_grad))
    query_results, keyval_results, output_results, gain_results = attn_adam(
        t_array, query_group, attn_pieces,
        (w_query, first_query, second_query, average_query),
        (w_keyval, first_keyval, second_keyval, average_keyval),
        (w_output, first_output, second_output, average_output),
        (norm_gains, first_gains, second_gains, average_gains),
    )
    results = (query_results, keyval_results, output_results, in_results, out_results, gain_results)
    return (layer_out, input_grad) + tuple(result[part] for part in range(5) for result in results)


def solution(mesh):
    token, rows, columns = P("dp", None), P("dp", None), P(None, "dp")
    weight_specs = (rows, rows, columns, P("dp", None, "tensor"), P("tensor", "dp"), columns)
    in_specs = (token, token, P("dp", None), P("dp"), P()) + weight_specs * 4
    out_specs = (token, token) + weight_specs * 5
    return jax.shard_map(local, mesh=mesh, in_specs=in_specs, out_specs=out_specs, check_vma=False)
```
